32 devices in a mesh: docs: 8 (over z, y), seq: 4 (over x, core).
Axes of the slice: x: 2, y: 2, z: 4, core: 2. Of those that a mesh axis runs over, the one named last changes fastest.
Arguments:
- seg_input: bfloat16 [24, 512, 512], P('docs', 'seq'), may hold values from -6 to 6
- memory: bfloat16 [24, 64, 512], P('docs'), may hold values from -6 to 6
- lengths: int32 [24], P('docs'), may hold values from 4096 to 8192, as said below
- seg_index: int32 [24], P('docs'), may hold values from 0 to 15, as said below
- self_qkv: bfloat16 [3, 512, 512], replicated, may hold values from -0.25 to 0.25
- self_out: bfloat16 [512, 512], replicated, may hold values from -1.5 to 1.5
- cross_qkv: bfloat16 [3, 512, 512], replicated, may hold values from -0.25 to 0.25
- cross_out: bfloat16 [512, 512], replicated, may hold values from -1.5 to 1.5
- ffn_in: bfloat16 [512, 2048], replicated, may hold values from -0.25 to 0.25
- ffn_out: bfloat16 [2048, 512], replicated, may hold values from -0.125 to 0.125
- writer_qkv: bfloat16 [3, 512, 512], replicated, may hold values from -0.25 to 0.25
- writer_out: bfloat16 [512, 512], replicated, may hold values from -1.5 to 1.5
- norm_gains: float32 [5, 512], replicated, may hold values from 0.1 to 1.9
- output_cotangent: bfloat16 [24, 512, 512], P('docs', 'seq'), may hold values from -6 to 6
- memory_cotangent: bfloat16 [24, 64, 512], P('docs'), may hold values from -6 to 6
Outputs:
- enc_out: bfloat16 [24, 512, 512], P('docs', 'seq')
- new_memory: bfloat16 [24, 64, 512], P('docs')
- input_grad: float32 [24, 512, 512], P('docs', 'seq')
- memory_grad: float32 [24, 64, 512], P('docs')
- self_qkv_grad: float32 [3, 512, 512], replicated
- self_out_grad: float32 [512, 512], replicated
- cross_qkv_grad: float32 [3, 512, 512], replicated
- cross_out_grad: float32 [512, 512], replicated
- ffn_in_grad: float32 [512, 2048], replicated
- ffn_out_grad: float32 [2048, 512], replicated
- writer_qkv_grad: float32 [3, 512, 512], replicated
- writer_out_grad: float32 [512, 512], replicated
- gains_grad: float32 [5, 512], replicated
The draws below stay inside these ranges and needn't reach their ends.
Inputs may be any that keep to these rules, and one draw needn't show every extreme that they name: `lengths`: some document has length exactly 8192 and some exactly 4096. seg_index * 512 < the document's length; some document is at segment 0 and some at segment 15; in each aligned block of 3 documents the one at an offset drawn from the seed has a segment without padding.
All inputs are finite; a program needn't handle non-finite values.
Results may differ from the reference program's by a relative error of at most 0.019.
Values may be sent and summed in bfloat16 or wider, within the bound.
A program may use at most 256 MiB of HBM per device.

```python
import math
import jax
import jax.numpy as jnp
from jax import lax

D = 512
H = 8
HD = 64
FF = 2048
SLOTS = 64
SEG = 512
DOCS_DEV = 3
DOCS = 24


def document_draw(key):
    length_key, index_key, pick_key = jax.random.split(key, 3)
    order = jnp.arange(DOCS)
    lengths = jax.random.randint(length_key, (DOCS,), 8 * SEG, 16 * SEG + 1)
    picks = jax.random.randint(pick_key, (2,), 0, 1 << 20)
    longest = order == picks[0] % DOCS
    shortest = order == (picks[0] + 1) % DOCS
    lengths = jnp.where(longest, 16 * SEG, lengths)
    lengths = jnp.where(shortest, 8 * SEG, lengths)
    whole_count = lengths // SEG
    started = (lengths + SEG - 1) // SEG
    limit = jnp.where(order % DOCS_DEV == picks[1] % DOCS_DEV, whole_count, started)
    raw_index = jax.random.randint(index_key, (DOCS,), 0, 1 << 20)
    index = raw_index % limit
    index = jnp.where(longest, 15, index)
    index = jnp.where(shortest, 0, index)
    return (lengths.astype(jnp.int32), index.astype(jnp.int32))


def draw_lengths(key, part):
    shared = document_draw(key)
    return shared[0]


def draw_seg_index(key, part):
    shared = document_draw(key)
    return shared[1]


def shard_levels(rng, shape, cuts, least, top_value):
    def one(position, parts):
        draws = jax.random.uniform(jax.random.fold_in(jax.random.fold_in(rng, 6), position), (parts,), jnp.float32, least / len(cuts), top_value / len(cuts))
        return jnp.repeat(jnp.exp(draws), shape[position] // parts).reshape((-1,) + (1,) * (len(shape) - position - 1))

    factor_of = one(*cuts[0])
    for cut in cuts[1:]:
        factor_of = factor_of * one(*cut)
    return factor_of


def centred(rng, dims, scale, bound, cuts=(), held_as=jnp.bfloat16):
    drawn = scale * jax.random.normal(rng, dims, jnp.float32)
    if cuts:
        drawn = drawn * shard_levels(rng, dims, cuts, -0.22, 0.18)
    return jnp.clip(drawn, -bound, bound).astype(held_as)


def setup_inputs(seed: int = 0) -> dict:
    splits = jax.random.split(jax.random.key(seed), 16)
    seg_input = centred(splits[0], (DOCS, SEG, D), 1.0, 6.0, ((0, 8), (1, 4)))
    memory = centred(splits[1], (DOCS, SLOTS, D), 1.0, 6.0, ((0, 8),))
    lengths = draw_lengths(jax.random.fold_in(splits[15], 71), 0)
    seg_index = draw_seg_index(jax.random.fold_in(splits[15], 71), 0)
    self_qkv = centred(splits[4], (3, D, D), D ** -0.5, 0.25)
    self_out = centred(splits[5], (D, D), (D // 32) ** -0.5, 1.5)
    cross_qkv = centred(splits[6], (3, D, D), D ** -0.5, 0.25)
    cross_out = centred(splits[7], (D, D), (D // 32) ** -0.5, 1.5)
    ffn_in = centred(splits[8], (D, FF), D ** -0.5, 0.25)
    ffn_out = centred(splits[9], (FF, D), FF ** -0.5, 0.125)
    writer_qkv = centred(splits[10], (3, D, D), D ** -0.5, 0.25)
    writer_out = centred(splits[11], (D, D), (D // 32) ** -0.5, 1.5)
    norm_gains = jnp.clip(1.0 + 0.18 * jax.random.normal(splits[12], (5, D), jnp.float32), 0.1, 1.9)
    output_cotangent = centred(splits[13], (DOCS, SEG, D), 1.0, 6.0, ((0, 8), (1, 4)))
    memory_cotangent = centred(splits[14], (DOCS, SLOTS, D), 1.0, 6.0, ((0, 8),))
    return dict(seg_input=seg_input, memory=memory, lengths=lengths, seg_index=seg_index, self_qkv=self_qkv, self_out=self_out, cross_qkv=cross_qkv, cross_out=cross_out, ffn_in=ffn_in, ffn_out=ffn_out, writer_qkv=writer_qkv, writer_out=writer_out, norm_gains=norm_gains, output_cotangent=output_cotangent, memory_cotangent=memory_cotangent)


@jax.custom_vjp
def low(v):
    return lax.optimization_barrier(v.astype(jnp.bfloat16)).astype(jnp.float32)

@jax.custom_vjp
def low_back(v):
    return v

def low_keep(v):
    return (low(v), None)

def low_pass(kept, grad):
    return (grad,)

def back_keep(v):
    return (v, None)

def back_low(kept, grad):
    return (low(grad),)
low.defvjp(low_keep, low_pass)
low_back.defvjp(back_keep, back_low)
highest = lax.Precision.HIGHEST

def norm_rows(values, gain_row):
    centered = values - lax.optimization_barrier(jnp.mean(values, axis=-1, keepdims=True))
    spread = lax.optimization_barrier(jnp.mean(centered * centered, axis=-1, keepdims=True))
    return centered * lax.rsqrt(spread + 1e-05) * gain_row

def rounded(values):
    return low_back(low(values))

def matmul(left_side, right_side):
    return jnp.matmul(left_side, right_side, precision=highest)

def heads_of(values):
    return values.reshape(values.shape[0], H, HD)

def attend(queries, key_rows, value_rows, key_open):
    scores = low_back(jnp.einsum('qhd,khd->hqk', heads_of(queries), heads_of(key_rows), precision=highest))
    scores = jnp.where(key_open[None], scores, -1e+30)
    row_max = lax.optimization_barrier(jnp.max(scores, axis=-1, keepdims=True))
    exponent = jnp.exp(scores - row_max)
    attention = low(exponent / lax.optimization_barrier(jnp.sum(exponent, axis=-1, keepdims=True)))
    blended = jnp.einsum('hqk,khd->qhd', attention, heads_of(value_rows), precision=highest)
    return low(low_back(blended.reshape(queries.shape[0], H * HD)))

def document(parameters, tokens, memory_rows, valid_count):
    self_qkv, self_out, cross_qkv, cross_out, ffn_in, ffn_out, writer_qkv, writer_out, gain_rows = parameters
    query_scale = HD ** (-0.5)
    positions = jnp.arange(SEG)
    token_ok = positions < valid_count
    normed = low(norm_rows(tokens, gain_rows[0]))
    queries = rounded(matmul(normed, self_qkv[0]) * query_scale)
    key_rows = rounded(matmul(normed, self_qkv[1]))
    value_rows = rounded(matmul(normed, self_qkv[2]))
    causal = (positions[:, None] >= positions[None, :]) & token_ok[None, :]
    after_self = tokens + low_back(matmul(attend(queries, key_rows, value_rows, causal), self_out))
    normed = low(norm_rows(after_self, gain_rows[1]))
    slot_rows = low(norm_rows(memory_rows, gain_rows[3]))
    queries = rounded(matmul(normed, cross_qkv[0]) * query_scale)
    key_rows = rounded(matmul(slot_rows, cross_qkv[1]))
    value_rows = rounded(matmul(slot_rows, cross_qkv[2]))
    all_open = jnp.ones((SEG, SLOTS), bool)
    after_cross = after_self + low_back(matmul(attend(queries, key_rows, value_rows, all_open), cross_out))
    normed = low(norm_rows(after_cross, gain_rows[2]))
    hidden = low(jax.nn.gelu(low_back(matmul(normed, ffn_in))))
    encoded = after_cross + low_back(matmul(hidden, ffn_out))
    written = low(norm_rows(encoded, gain_rows[4]))
    sources = jnp.concatenate([slot_rows, written], axis=0)
    queries = rounded(matmul(slot_rows, writer_qkv[0]) * query_scale)
    key_rows = rounded(matmul(sources, writer_qkv[1]))
    value_rows = rounded(matmul(sources, writer_qkv[2]))
    open_keys = jnp.concatenate([jnp.ones((SLOTS,), bool), token_ok])
    key_mask = jnp.broadcast_to(open_keys[None, :], (SLOTS, SLOTS + SEG))
    updated = memory_rows + low_back(matmul(attend(queries, key_rows, value_rows, key_mask), writer_out))
    return (encoded, updated)

def reference(seg_input, memory, lengths, seg_index, self_qkv, self_out, cross_qkv, cross_out, ffn_in, ffn_out, writer_qkv, writer_out, norm_gains, output_cotangent, memory_cotangent):
    parameters = tuple((weight.astype(jnp.float32) for weight in (self_qkv, self_out, cross_qkv, cross_out, ffn_in, ffn_out, writer_qkv, writer_out, norm_gains)))
    valid_count = jnp.minimum(lengths - seg_index * SEG, SEG).astype(jnp.int32)
    block_size = math.gcd(DOCS, 8)

    def regroup(array):
        return array.reshape((DOCS // block_size, block_size) + array.shape[1:])

    def one_block(totals, pieces):
        tokens, memory_rows, counts, tangent_out, tangent_memory = pieces

        def forward(weights, token_rows, slot_rows):
            return jax.vmap(document, in_axes=(None, 0, 0, 0))(weights, token_rows, slot_rows, counts)
        outputs, pullback = jax.vjp(forward, parameters, tokens, memory_rows)
        gradients = pullback((tangent_out, tangent_memory))
        totals = jax.tree.map(jnp.add, totals, gradients[0])
        return (totals, (outputs[0], outputs[1], gradients[1], gradients[2]))
    initial = jax.tree.map(jnp.zeros_like, parameters)
    inputs = (regroup(seg_input.astype(jnp.float32)), regroup(memory.astype(jnp.float32)), regroup(valid_count), regroup(output_cotangent.astype(jnp.float32)), regroup(memory_cotangent.astype(jnp.float32)))
    totals, stacked = lax.scan(one_block, initial, inputs)
    encoded = stacked[0].reshape(DOCS, SEG, D)
    updated = stacked[1].reshape(DOCS, SLOTS, D)
    input_grad = stacked[2].reshape(DOCS, SEG, D)
    memory_grad = stacked[3].reshape(DOCS, SLOTS, D)
    return (encoded.astype(jnp.bfloat16), updated.astype(jnp.bfloat16), input_grad, memory_grad, totals[0], totals[1], totals[2], totals[3], totals[4], totals[5], totals[6], totals[7], totals[8])
```

```python
import functools

import jax
import jax.numpy as jnp
from jax import lax
from jax.experimental import pallas as pl
from jax.experimental.pallas import tpu as pltpu
from jax.sharding import PartitionSpec as P

MESH = pl.DeviceIdType.MESH
D = 512
H = 8
HD = 64
SEG = 512


def merged(value, axis, combine):
    everything = jax.tree.map(lambda part: lax.all_gather(part, axis), value)
    initial = jax.tree.map(lambda part: part[0], everything)

    def turn(k, so_far):
        return combine(so_far, jax.tree.map(lambda part: part[k], everything))

    return lax.fori_loop(1, lax.axis_size(axis), turn, initial)


def to_low(values):
    return values.astype(jnp.bfloat16)


def norm_rows(values, gain_row):
    centered = values - jnp.mean(values, axis=-1, keepdims=True)
    inverse = lax.rsqrt(jnp.mean(centered * centered, axis=-1, keepdims=True) + 1e-05)
    unit_rows = centered * inverse
    return (unit_rows * gain_row, unit_rows, inverse)


def norm_back(grad_out, unit_rows, inverse, gain_row):
    scaled = grad_out * gain_row
    adjusted = (
        scaled
        - jnp.mean(scaled, axis=-1, keepdims=True)
        - unit_rows * jnp.mean(scaled * unit_rows, axis=-1, keepdims=True)
    )
    return adjusted * inverse


def project(left_side, right_side):
    return jnp.einsum("bti,ij->btj", left_side, right_side, preferred_element_type=jnp.float32)


def back_project(left_side, right_side):
    return jnp.einsum("btj,ij->bti", left_side, right_side, preferred_element_type=jnp.float32)


def outer_sum(left_side, right_side):
    return jnp.einsum("bti,btj->ij", left_side, right_side, preferred_element_type=jnp.float32)


def split_heads(values):
    return values.reshape(values.shape[:-1] + (H, HD))


def join_heads(values):
    return values.reshape(values.shape[:-2] + (H * HD,))


def scores_of(queries, key_rows, key_open):
    scores = jnp.einsum(
        "bqhd,bkhd->bhqk",
        split_heads(queries),
        split_heads(key_rows),
        preferred_element_type=jnp.float32,
    )
    return jnp.where(key_open[:, None], scores, -1e30)


def softmax_rows(scores):
    row_max = jnp.max(scores, axis=-1, keepdims=True)
    return row_max + jnp.log(jnp.sum(jnp.exp(scores - row_max), axis=-1, keepdims=True))


def mix_values(probs_low, value_rows):
    return join_heads(
        jnp.einsum(
            "bhqk,bkhd->bqhd",
            probs_low,
            split_heads(value_rows),
            preferred_element_type=jnp.float32,
        )
    )


def grad_probs_of(grad_mix, value_rows):
    return jnp.einsum(
        "bqhd,bkhd->bhqk",
        split_heads(grad_mix),
        split_heads(value_rows),
        preferred_element_type=jnp.float32,
    )


def to_queries(grad_scores, key_rows):
    return join_heads(
        jnp.einsum(
            "bhqk,bkhd->bqhd",
            grad_scores,
            split_heads(key_rows),
            preferred_element_type=jnp.float32,
        )
    )


def to_keys(grad_scores, query_rows):
    return join_heads(
        jnp.einsum(
            "bhqk,bqhd->bkhd",
            grad_scores,
            split_heads(query_rows),
            preferred_element_type=jnp.float32,
        )
    )


CORE, X, Y, Z0, Z1 = ("seq", 1), ("seq", 2), ("docs", 1), ("docs", 2), ("docs", 4)
ORDERS = (
    (CORE, X, Y, Z0, Z1),
    (CORE, Y, X, Z0, Z1),
    (CORE, Z0, Z1, X, Y),
)
GROUP = 8


def place_of(stage):
    axis, stride = stage
    index = lax.axis_index(axis)
    bit = lax.rem(lax.div(index, stride), 2)
    return bit, {axis: index + stride * (1 - 2 * bit)}


def greet(docs_count):
    barrier = pltpu.get_barrier_semaphore()
    partners = [place_of(stage)[1] for stage in ORDERS[0]] + outer_partners(docs_count)
    for partner in partners:
        pl.semaphore_signal(barrier, inc=1, device_id=partner, device_id_type=MESH)
    pl.semaphore_wait(barrier, len(partners))


def outer_partners(docs_count):
    index = lax.axis_index("docs")
    return [{"docs": lax.rem(index + GROUP * k, docs_count)} for k in range(1, docs_count // GROUP)]


def add_rows(total, start, rows, landed, first):
    tile = 16

    def turn(t, carry):
        here = pl.ds(pl.multiple_of(start + t * tile, tile), tile)
        there = pl.ds(pl.multiple_of(first + t * tile, tile), tile)
        total[here, :] = (
            total[here, :].astype(jnp.float32) + landed[there, :].astype(jnp.float32)
        ).astype(total.dtype)
        return carry

    lax.fori_loop(0, rows // tile, turn, 0)


def reduce_kernel(docs_count, chunks, flat_ref, out_ref, total, landed, outer, load_sem, ss, rs, gs, gr, os, orr, store_sem):
    loads = []
    for c, (base, rows, order) in enumerate(chunks):
        load = pltpu.make_async_copy(flat_ref.at[pl.ds(base, rows)], total.at[pl.ds(base, rows)], load_sem.at[c])
        load.start()
        loads.append(load)
    greet(docs_count)
    stages = len(ORDERS[0])
    state = []
    flying = [None] * len(chunks)

    def send(c, j, start, size):
        base, rows, order = chunks[c]
        bit, partner = place_of(ORDERS[order][j])
        half = size // 2
        keep = start + bit * half
        give = start + (1 - bit) * half
        first = base + rows - size
        copy = pltpu.make_async_remote_copy(
            src_ref=total.at[pl.ds(pl.multiple_of(give, 16), half)],
            dst_ref=landed.at[pl.ds(first, half)],
            send_sem=ss.at[c, j],
            recv_sem=rs.at[c, j],
            device_id=partner,
            device_id_type=MESH,
        )
        copy.start()
        flying[c] = (copy, keep, half, first)

    for c, (base, rows, order) in enumerate(chunks):
        loads[c].wait()
        send(c, 0, base, rows)
    for j in range(stages):
        for c in range(len(chunks)):
            copy, keep, half, first = flying[c]
            copy.wait()
            add_rows(total, keep, half, landed, first)
            if j + 1 < stages:
                send(c, j + 1, keep, half)
            else:
                flying[c] = (keep, half)
    others = outer_partners(docs_count)
    if others:
        copies = []
        mine = lax.div(lax.axis_index("docs"), GROUP)
        for c in range(len(chunks)):
            keep, half = flying[c]
            share = pl.ds(chunks[c][0] // 32, half)
            piece = total.at[pl.ds(pl.multiple_of(keep, 16), half)]
            outer[mine, share, :] = piece[...]
            for k, partner in enumerate(others):
                copy = pltpu.make_async_remote_copy(
                    src_ref=piece,
                    dst_ref=outer.at[mine, share],
                    send_sem=os.at[c, k],
                    recv_sem=orr.at[c, k],
                    device_id=partner,
                    device_id_type=MESH,
                )
                copy.start()
                copies.append(copy)
        for copy in copies:
            copy.wait()
        for c in range(len(chunks)):
            keep, half = flying[c]
            share = pl.ds(chunks[c][0] // 32, half)
            parts = [outer[k, share, :].astype(jnp.float32) for k in range(len(others) + 1)]
            total[pl.ds(pl.multiple_of(keep, 16), half), :] = sum(parts).astype(total.dtype)

    def spread(c, j, start, size):
        base, rows, order = chunks[c]
        bit, partner = place_of(ORDERS[order][j])
        here = pl.ds(pl.multiple_of(start, 16), size)
        copy = pltpu.make_async_remote_copy(
            src_ref=(total if j == stages - 1 else out_ref).at[here],
            dst_ref=out_ref.at[here],
            send_sem=gs.at[c, j],
            recv_sem=gr.at[c, j],
            device_id=partner,
            device_id_type=MESH,
        )
        copy.start()
        flying[c] = (copy, start - bit * size, 2 * size)

    stores = []
    for c in range(len(chunks)):
        start, size = flying[c]
        here = pl.ds(pl.multiple_of(start, 16), size)
        store = pltpu.make_async_copy(total.at[here], out_ref.at[here], store_sem.at[c])
        store.start()
        stores.append(store)
        spread(c, stages - 1, start, size)
    for j in reversed(range(stages)):
        for c in range(len(chunks)):
            copy, start, size = flying[c]
            copy.wait()
            if j == stages - 1:
                stores[c].wait()
            if j > 0:
                spread(c, j - 1, start, size)


def reduce_weights(flat, docs_count):
    chunks = [(1024 * c, 1024, (0, 1, 0, 1, 2)[c % 5]) for c in range(10)] + [(10240, 512, 0)]
    count, stages, outers = len(chunks), len(ORDERS[0]), max(1, docs_count // GROUP)
    return pl.pallas_call(
        functools.partial(reduce_kernel, docs_count, chunks),
        out_shape=jax.ShapeDtypeStruct(flat.shape, flat.dtype),
        in_specs=[pl.BlockSpec(memory_space=pl.ANY)],
        out_specs=pl.BlockSpec(memory_space=pl.ANY),
        scratch_shapes=[
            pltpu.VMEM(flat.shape, flat.dtype),
            pltpu.VMEM(flat.shape, flat.dtype),
            pltpu.VMEM((outers, flat.shape[0] // 32, flat.shape[1]), flat.dtype),
            pltpu.SemaphoreType.DMA((count,)),
            pltpu.SemaphoreType.DMA((count, stages)),
            pltpu.SemaphoreType.DMA((count, stages)),
            pltpu.SemaphoreType.DMA((count, stages)),
            pltpu.SemaphoreType.DMA((count, stages)),
            pltpu.SemaphoreType.DMA((count, outers)),
            pltpu.SemaphoreType.DMA((count, outers)),
            pltpu.SemaphoreType.DMA((count,)),
        ],
        compiler_params=pltpu.CompilerParams(
            collective_id=0, has_side_effects=True, vmem_limit_bytes=56 << 20
        ),
    )(flat)


def on_device(
    seg_input,
    memory,
    lengths,
    seg_index,
    self_qkv,
    self_out,
    cross_qkv,
    cross_out,
    ffn_in,
    ffn_out,
    writer_qkv,
    writer_out,
    norm_gains,
    output_cotangent,
    memory_cotangent,
):
    docs_here, local_len, model_width = seg_input.shape
    slot_count = memory.shape[1]
    seq_rank = lax.axis_index("seq")
    seq_count = lax.axis_size("seq")
    query_scale = HD ** (-0.5)
    tokens = seg_input.astype(jnp.float32)
    memory_rows = memory.astype(jnp.float32)
    valid_count = jnp.minimum(lengths - seg_index * SEG, SEG)
    query_pos = seq_rank * local_len + jnp.arange(local_len)
    key_pos = jnp.arange(SEG)
    self_open = (query_pos[:, None] >= key_pos[None, :])[None] & (
        key_pos[None, None, :] < valid_count[:, None, None]
    )
    self_normed, self_unit, self_inverse = norm_rows(tokens, norm_gains[0])
    self_input = to_low(self_normed)
    self_query = to_low(project(self_input, self_qkv[0]) * query_scale)
    key_local = to_low(project(self_input, self_qkv[1]))
    value_local = to_low(project(self_input, self_qkv[2]))
    key_all, value_all = (
        lax.all_gather(key_local, "seq", axis=1, tiled=True),
        lax.all_gather(value_local, "seq", axis=1, tiled=True),
    )
    self_scores = scores_of(self_query, key_all, self_open)
    self_lse = softmax_rows(self_scores)
    self_probs = jnp.exp(self_scores - self_lse)
    self_mix = to_low(mix_values(to_low(self_probs), value_all))
    after_self = tokens + project(self_mix, self_out)
    cross_normed, cross_unit, cross_inverse = norm_rows(after_self, norm_gains[1])
    cross_input = to_low(cross_normed)
    slot_normed, slot_unit, slot_inverse = norm_rows(memory_rows, norm_gains[3])
    slot_input = to_low(slot_normed)
    cross_query = to_low(project(cross_input, cross_qkv[0]) * query_scale)
    cross_key = to_low(project(slot_input, cross_qkv[1]))
    cross_value = to_low(project(slot_input, cross_qkv[2]))
    cross_scores = scores_of(
        cross_query, cross_key, jnp.ones((docs_here, local_len, slot_count), bool)
    )
    cross_probs = jnp.exp(cross_scores - softmax_rows(cross_scores))
    cross_low = to_low(cross_probs)
    cross_mix = to_low(mix_values(cross_low, cross_value))
    after_cross = after_self + project(cross_mix, cross_out)
    ffn_normed, ffn_unit, ffn_inverse = norm_rows(after_cross, norm_gains[2])
    ffn_input = to_low(ffn_normed)
    before_gelu = project(ffn_input, ffn_in)
    activated, gelu_back = jax.vjp(jax.nn.gelu, before_gelu)
    hidden = to_low(activated)
    encoded = after_cross + project(hidden, ffn_out)
    writer_normed, writer_unit, writer_inverse = norm_rows(encoded, norm_gains[4])
    writer_input = to_low(writer_normed)
    writer_query = to_low(project(slot_input, writer_qkv[0]) * query_scale)
    slot_key = to_low(project(slot_input, writer_qkv[1]))
    slot_value = to_low(project(slot_input, writer_qkv[2]))
    token_key = to_low(project(writer_input, writer_qkv[1]))
    token_value = to_low(project(writer_input, writer_qkv[2]))
    token_open = jnp.broadcast_to(
        (query_pos < valid_count[:, None])[:, None, :], (docs_here, slot_count, local_len)
    )
    token_scores = scores_of(writer_query, token_key, token_open)
    local_max = jnp.max(token_scores, axis=-1)
    local_total = jnp.sum(jnp.exp(token_scores - local_max[..., None]), axis=-1)

    def combine_parts(first_part, second_part):
        joint_max = jnp.maximum(first_part[0], second_part[0])
        return (
            joint_max,
            first_part[1] * jnp.exp(first_part[0] - joint_max)
            + second_part[1] * jnp.exp(second_part[0] - joint_max),
        )

    token_max, token_total = merged((local_max, local_total), "seq", combine_parts)
    slot_scores = scores_of(
        writer_query, slot_key, jnp.ones((docs_here, slot_count, slot_count), bool)
    )
    joint_max = jnp.maximum(token_max, jnp.max(slot_scores, axis=-1))
    slot_total = jnp.sum(jnp.exp(slot_scores - joint_max[..., None]), axis=-1)
    writer_lse = joint_max + jnp.log(token_total * jnp.exp(token_max - joint_max) + slot_total)
    token_probs = jnp.exp(token_scores - writer_lse[..., None])
    slot_probs = jnp.exp(slot_scores - writer_lse[..., None])
    token_low = to_low(token_probs)
    slot_low = to_low(slot_probs)
    token_part = mix_values(token_low, token_value)
    token_sum = lax.psum(token_part.astype(jnp.bfloat16), "seq").astype(jnp.float32)
    writer_mix = to_low(token_sum + mix_values(slot_low, slot_value))
    updated = memory_rows + project(writer_mix, writer_out)
    slot_share = slot_count // seq_count
    slot_start = seq_rank * slot_share

    def own_slots(values):
        return lax.dynamic_slice_in_dim(values, slot_start, slot_share, 1)

    grad_new = memory_cotangent.astype(jnp.float32)
    grad_new_low = to_low(grad_new)
    writer_out_grad = outer_sum(own_slots(writer_mix), own_slots(grad_new_low))
    grad_mix = to_low(back_project(grad_new_low, writer_out))
    grad_token_probs = grad_probs_of(grad_mix, token_value)
    grad_slot_probs = grad_probs_of(grad_mix, slot_value)
    local_delta = jnp.sum(token_probs * grad_token_probs, axis=-1)
    token_delta = lax.psum(local_delta, "seq")
    writer_delta = token_delta + jnp.sum(slot_probs * grad_slot_probs, axis=-1)
    grad_token_scores = to_low(token_probs * (grad_token_probs - writer_delta[..., None]))
    grad_slot_scores = to_low(slot_probs * (grad_slot_probs - writer_delta[..., None]))
    query_token_part = to_queries(grad_token_scores, token_key)
    query_slot_part = to_queries(grad_slot_scores, slot_key)
    grad_token_key = to_low(to_keys(grad_token_scores, writer_query))
    grad_slot_key = to_low(to_keys(grad_slot_scores, writer_query))
    grad_token_value = to_low(to_keys(token_low, grad_mix))
    grad_slot_value = to_low(to_keys(slot_low, grad_mix))
    grad_writer_input = back_project(grad_token_key, writer_qkv[1]) + back_project(
        grad_token_value, writer_qkv[2]
    )
    grad_encoded = output_cotangent.astype(jnp.float32) + norm_back(
        grad_writer_input, writer_unit, writer_inverse, norm_gains[4]
    )
    grad_encoded_low = to_low(grad_encoded)
    ffn_out_grad = outer_sum(hidden, grad_encoded_low)
    grad_hidden = back_project(grad_encoded_low, ffn_out)
    grad_before = to_low(gelu_back(grad_hidden)[0])
    grad_ffn_input = back_project(grad_before, ffn_in)
    grad_after_cross = grad_encoded + norm_back(
        grad_ffn_input, ffn_unit, ffn_inverse, norm_gains[2]
    )
    grad_cross_low = to_low(grad_after_cross)
    cross_out_grad = outer_sum(cross_mix, grad_cross_low)
    grad_cross_mix = to_low(back_project(grad_cross_low, cross_out))
    grad_cross_probs = grad_probs_of(grad_cross_mix, cross_value)
    cross_delta = jnp.sum(cross_probs * grad_cross_probs, axis=-1)
    grad_cross_scores = to_low(cross_probs * (grad_cross_probs - cross_delta[..., None]))
    cross_query_grad = to_low(to_queries(grad_cross_scores, cross_key)) * query_scale
    cross_key_part = to_keys(grad_cross_scores, cross_query)
    cross_value_part = to_keys(cross_low, grad_cross_mix)
    grad_cross_input = back_project(cross_query_grad, cross_qkv[0])
    grad_after_self = grad_after_cross + norm_back(
        grad_cross_input, cross_unit, cross_inverse, norm_gains[1]
    )
    query_sum, key_sum, value_sum = (
        lax.psum(query_token_part.astype(jnp.bfloat16), "seq").astype(jnp.float32),
        lax.psum(cross_key_part.astype(jnp.bfloat16), "seq").astype(jnp.float32),
        lax.psum(cross_value_part.astype(jnp.bfloat16), "seq").astype(jnp.float32),
    )
    writer_query_grad = to_low(query_sum + query_slot_part) * query_scale
    cross_key_grad = to_low(key_sum)
    cross_value_grad = to_low(value_sum)
    grad_slot_input = (
        back_project(writer_query_grad, writer_qkv[0])
        + back_project(grad_slot_key, writer_qkv[1])
        + back_project(grad_slot_value, writer_qkv[2])
    )
    grad_slot_input = (
        grad_slot_input
        + back_project(cross_key_grad, cross_qkv[1])
        + back_project(cross_value_grad, cross_qkv[2])
    )
    memory_grad = grad_new + norm_back(grad_slot_input, slot_unit, slot_inverse, norm_gains[3])
    grad_self_low = to_low(grad_after_self)
    self_out_grad = outer_sum(self_mix, grad_self_low)
    grad_self_mix = to_low(back_project(grad_self_low, self_out))
    self_probs = jnp.exp(scores_of(self_query, key_all, self_open) - self_lse)
    grad_self_probs = grad_probs_of(grad_self_mix, value_all)
    self_delta = jnp.sum(self_probs * grad_self_probs, axis=-1)
    grad_self_scores = to_low(self_probs * (grad_self_probs - self_delta[..., None]))
    self_query_grad = to_low(to_queries(grad_self_scores, key_all)) * query_scale
    key_term = to_keys(grad_self_scores, self_query)
    value_term = to_keys(to_low(self_probs), grad_self_mix)
    key_grad_sum, value_grad_sum = (
        lax.psum_scatter(
            key_term.astype(jnp.bfloat16), "seq", scatter_dimension=1, tiled=True
        ).astype(jnp.float32),
        lax.psum_scatter(
            value_term.astype(jnp.bfloat16), "seq", scatter_dimension=1, tiled=True
        ).astype(jnp.float32),
    )
    self_key_grad = to_low(key_grad_sum)
    self_value_grad = to_low(value_grad_sum)
    grad_self_input = (
        back_project(self_query_grad, self_qkv[0])
        + back_project(self_key_grad, self_qkv[1])
        + back_project(self_value_grad, self_qkv[2])
    )
    input_grad = grad_after_self + norm_back(
        grad_self_input, self_unit, self_inverse, norm_gains[0]
    )
    own_input = own_slots(slot_input)
    self_qkv_grad = jnp.stack(
        [
            outer_sum(self_input, self_query_grad),
            outer_sum(self_input, self_key_grad),
            outer_sum(self_input, self_value_grad),
        ]
    )
    cross_qkv_grad = jnp.stack(
        [
            outer_sum(cross_input, cross_query_grad),
            outer_sum(own_input, own_slots(cross_key_grad)),
            outer_sum(own_input, own_slots(cross_value_grad)),
        ]
    )
    writer_key_grad = outer_sum(writer_input, grad_token_key) + outer_sum(
        own_input, own_slots(grad_slot_key)
    )
    writer_value_grad = outer_sum(writer_input, grad_token_value) + outer_sum(
        own_input, own_slots(grad_slot_value)
    )
    writer_qkv_grad = jnp.stack(
        [outer_sum(own_input, own_slots(writer_query_grad)), writer_key_grad, writer_value_grad]
    )
    gains_grad = jnp.stack(
        [
            jnp.sum(grad_self_input * self_unit, axis=(0, 1)),
            jnp.sum(grad_cross_input * cross_unit, axis=(0, 1)),
            jnp.sum(grad_ffn_input * ffn_unit, axis=(0, 1)),
            jnp.sum(own_slots(grad_slot_input * slot_unit), axis=(0, 1)),
            jnp.sum(grad_writer_input * writer_unit, axis=(0, 1)),
        ]
    )
    ffn_in_blocks = [
        outer_sum(ffn_input, grad_before[..., c * D : (c + 1) * D]) for c in range(ffn_in.shape[1] // D)
    ]
    pieces = [
        self_qkv_grad.reshape(-1, D),
        self_out_grad,
        cross_qkv_grad.reshape(-1, D),
        cross_out_grad,
        *ffn_in_blocks,
        ffn_out_grad,
        writer_qkv_grad.reshape(-1, D),
        writer_out_grad,
        jnp.pad(gains_grad, ((0, 512 - gains_grad.shape[0]), (0, 0))),
    ]
    flat = jnp.concatenate([to_low(piece) for piece in pieces], axis=0)
    summed = reduce_weights(flat, lax.axis_size("docs")).astype(jnp.float32)
    results = [
        summed[0:1536].reshape(3, D, D),
        summed[1536:2048],
        summed[2048:3584].reshape(3, D, D),
        summed[3584:4096],
        jnp.concatenate([summed[4096 + c * D : 4096 + (c + 1) * D] for c in range(4)], axis=1),
        summed[6144:8192],
        summed[8192:9728].reshape(3, D, D),
        summed[9728:10240],
        summed[10240:10245],
    ]
    return (
        to_low(encoded),
        to_low(updated),
        input_grad,
        memory_grad,
        results[0],
        results[1],
        results[2],
        results[3],
        results[4],
        results[5],
        results[6],
        results[7],
        results[8],
    )


def solution(mesh):
    placed = (
        P("docs", "seq", None),
        P("docs", None, None),
        P("docs"),
        P("docs"),
        P(),
        P(),
        P(),
        P(),
        P(),
        P(),
        P(),
        P(),
        P(),
        P("docs", "seq", None),
        P("docs", None, None),
    )
    return jax.shard_map(
        on_device,
        mesh=mesh,
        in_specs=placed,
        out_specs=(
            P("docs", "seq", None),
            P("docs", None, None),
            P("docs", "seq", None),
            P("docs", None, None),
            P(),
            P(),
            P(),
            P(),
            P(),
            P(),
            P(),
            P(),
            P(),
        ),
        check_vma=False,
    )
```

```python
import functools
import types

import jax
import jax.numpy as jnp
from jax import lax
from jax.experimental import pallas as pl
from jax.experimental.pallas import tpu as pltpu
from jax.sharding import PartitionSpec as P

MESH = pl.DeviceIdType.MESH
F32, LOW = jnp.float32, jnp.bfloat16
D = 512
HD = 64
SEG = 512
SHUT = -1e30
SCALE = HD ** (-0.5)

CORE, X, Y, Z0, Z1 = ("seq", 1), ("seq", 2), ("docs", 1), ("docs", 2), ("docs", 4)
ORDERS = (
    (CORE, X, Y, Z0, Z1),
    (CORE, Y, X, Z0, Z1),
    (CORE, Z0, Z1, X, Y),
)
GROUP = 8


def place_of(stage):
    axis, stride = stage
    index = lax.axis_index(axis)
    bit = lax.rem(lax.div(index, stride), 2)
    return bit, {axis: index + stride * (1 - 2 * bit)}


def greet(docs_count):
    barrier = pltpu.get_barrier_semaphore()
    partners = [place_of(stage)[1] for stage in ORDERS[0]] + outer_partners(docs_count)
    for partner in partners:
        pl.semaphore_signal(barrier, inc=1, device_id=partner, device_id_type=MESH)
    pl.semaphore_wait(barrier, len(partners))


def outer_partners(docs_count):
    index = lax.axis_index("docs")
    return [{"docs": lax.rem(index + GROUP * k, docs_count)} for k in range(1, docs_count // GROUP)]


def add_rows(total, start, rows, landed, first):
    tile = 16

    def turn(t, carry):
        here = pl.ds(pl.multiple_of(start + t * tile, tile), tile)
        there = pl.ds(pl.multiple_of(first + t * tile, tile), tile)
        total[here, :] = (
            total[here, :].astype(jnp.float32) + landed[there, :].astype(jnp.float32)
        ).astype(total.dtype)
        return carry

    lax.fori_loop(0, rows // tile, turn, 0)


def reduce_kernel(docs_count, chunks, flat_ref, out_ref, total, landed, outer, load_sem, ss, rs, gs, gr, os, orr, store_sem):
    loads = []
    for c, (base, rows, order) in enumerate(chunks):
        load = pltpu.make_async_copy(flat_ref.at[pl.ds(base, rows)], total.at[pl.ds(base, rows)], load_sem.at[c])
        load.start()
        loads.append(load)
    greet(docs_count)
    stages = len(ORDERS[0])
    state = []
    flying = [None] * len(chunks)

    def send(c, j, start, size):
        base, rows, order = chunks[c]
        bit, partner = place_of(ORDERS[order][j])
        half = size // 2
        keep = start + bit * half
        give = start + (1 - bit) * half
        first = base + rows - size
        copy = pltpu.make_async_remote_copy(
            src_ref=total.at[pl.ds(pl.multiple_of(give, 16), half)],
            dst_ref=landed.at[pl.ds(first, half)],
            send_sem=ss.at[c, j],
            recv_sem=rs.at[c, j],
            device_id=partner,
            device_id_type=MESH,
        )
        copy.start()
        flying[c] = (copy, keep, half, first)

    for c, (base, rows, order) in enumerate(chunks):
        loads[c].wait()
        send(c, 0, base, rows)
    for j in range(stages):
        for c in range(len(chunks)):
            copy, keep, half, first = flying[c]
            copy.wait()
            add_rows(total, keep, half, landed, first)
            if j + 1 < stages:
                send(c, j + 1, keep, half)
            else:
                flying[c] = (keep, half)
    others = outer_partners(docs_count)
    if others:
        copies = []
        mine = lax.div(lax.axis_index("docs"), GROUP)
        for c in range(len(chunks)):
            keep, half = flying[c]
            share = pl.ds(chunks[c][0] // 32, half)
            piece = total.at[pl.ds(pl.multiple_of(keep, 16), half)]
            outer[mine, share, :] = piece[...]
            for k, partner in enumerate(others):
                copy = pltpu.make_async_remote_copy(
                    src_ref=piece,
                    dst_ref=outer.at[mine, share],
                    send_sem=os.at[c, k],
                    recv_sem=orr.at[c, k],
                    device_id=partner,
                    device_id_type=MESH,
                )
                copy.start()
                copies.append(copy)
        for copy in copies:
            copy.wait()
        for c in range(len(chunks)):
            keep, half = flying[c]
            share = pl.ds(chunks[c][0] // 32, half)
            parts = [outer[k, share, :].astype(jnp.float32) for k in range(len(others) + 1)]
            total[pl.ds(pl.multiple_of(keep, 16), half), :] = sum(parts).astype(total.dtype)

    def spread(c, j, start, size):
        base, rows, order = chunks[c]
        bit, partner = place_of(ORDERS[order][j])
        here = pl.ds(pl.multiple_of(start, 16), size)
        copy = pltpu.make_async_remote_copy(
            src_ref=(total if j == stages - 1 else out_ref).at[here],
            dst_ref=out_ref.at[here],
            send_sem=gs.at[c, j],
            recv_sem=gr.at[c, j],
            device_id=partner,
            device_id_type=MESH,
        )
        copy.start()
        flying[c] = (copy, start - bit * size, 2 * size)

    stores = []
    for c in range(len(chunks)):
        start, size = flying[c]
        here = pl.ds(pl.multiple_of(start, 16), size)
        store = pltpu.make_async_copy(total.at[here], out_ref.at[here], store_sem.at[c])
        store.start()
        stores.append(store)
        spread(c, stages - 1, start, size)
    for j in reversed(range(stages)):
        for c in range(len(chunks)):
            copy, start, size = flying[c]
            copy.wait()
            if j == stages - 1:
                stores[c].wait()
            if j > 0:
                spread(c, j - 1, start, size)


def reduce_weights(flat, docs_count):
    chunks = [(1024 * c, 1024, (0, 1, 0, 1, 2)[c % 5]) for c in range(10)] + [(10240, 512, 0)]
    count, stages, outers = len(chunks), len(ORDERS[0]), max(1, docs_count // GROUP)
    return pl.pallas_call(
        functools.partial(reduce_kernel, docs_count, chunks),
        out_shape=jax.ShapeDtypeStruct(flat.shape, flat.dtype),
        in_specs=[pl.BlockSpec(memory_space=pl.ANY)],
        out_specs=pl.BlockSpec(memory_space=pl.ANY),
        scratch_shapes=[
            pltpu.VMEM(flat.shape, flat.dtype),
            pltpu.VMEM(flat.shape, flat.dtype),
            pltpu.VMEM((outers, flat.shape[0] // 32, flat.shape[1]), flat.dtype),
            pltpu.SemaphoreType.DMA((count,)),
            pltpu.SemaphoreType.DMA((count, stages)),
            pltpu.SemaphoreType.DMA((count, stages)),
            pltpu.SemaphoreType.DMA((count, stages)),
            pltpu.SemaphoreType.DMA((count, stages)),
            pltpu.SemaphoreType.DMA((count, outers)),
            pltpu.SemaphoreType.DMA((count, outers)),
            pltpu.SemaphoreType.DMA((count,)),
        ],
        compiler_params=pltpu.CompilerParams(
            collective_id=0, has_side_effects=True, vmem_limit_bytes=56 << 20
        ),
    )(flat)


def dot(left, right, left_dim, right_dim):
    return lax.dot_general(
        left, right, (((left_dim,), (right_dim,)), ((), ())), preferred_element_type=F32
    )


def nn(left, right):
    return dot(left, right, 1, 0)


def nt(left, right):
    return dot(left, right, 1, 1)


def tn(left, right):
    return dot(left, right, 0, 0)


def tiles(rows, tile, body):
    def turn(t, carry):
        body(pl.ds(pl.multiple_of(t * tile, tile), tile), t)
        return carry

    lax.fori_loop(0, rows // tile, turn, 0)


def each(count, body):
    def turn(k, carry):
        body(k)
        return carry

    lax.fori_loop(0, count, turn, 0)


def rows_at(start, size):
    return pl.ds(pl.multiple_of(start, 16), size)


def norm_rows(values, gain_row):
    centered = values - jnp.mean(values, axis=-1, keepdims=True)
    inverse = lax.rsqrt(jnp.mean(centered * centered, axis=-1, keepdims=True) + 1e-05)
    unit = centered * inverse
    return (unit * gain_row).astype(LOW), unit, inverse


def norm_back(grad, unit, inverse, gain_row):
    scaled = grad * gain_row
    adjusted = (
        scaled
        - jnp.mean(scaled, axis=-1, keepdims=True)
        - unit * jnp.mean(scaled * unit, axis=-1, keepdims=True)
    )
    return adjusted * inverse


def same_head():
    left = lax.div(lax.broadcasted_iota(jnp.int32, (256, 256), 0), HD)
    right = lax.div(lax.broadcasted_iota(jnp.int32, (256, 256), 1), HD)
    return left == right


def four_heads(values):
    return jnp.where(same_head(), jnp.concatenate([values] * 4, axis=0), 0.0)


def own_blocks(values):
    return jnp.sum(jnp.where(same_head(), values, 0.0).reshape(4, HD, 256), axis=0)


def swap(values):
    return own_blocks(four_heads(values).T)


def head_stack(values):
    low_half = lax.broadcasted_iota(jnp.int32, values.shape, 1) < HD
    return jnp.concatenate(
        [jnp.where(low_half, values, 0.0), jnp.where(low_half, 0.0, values)], axis=0
    )


def head_pick(values):
    low_half = lax.broadcasted_iota(jnp.int32, (128, 128), 0) < HD
    return jnp.where(low_half, values[:, :128], values[:, 128:])


BLOCKS = SEG // 128
BLOCK_ROWS = [sum(128 * (k + 1) for k in range(i)) for i in range(BLOCKS + 1)]
TILE = 64

INPUTS = (
    "x", "memory", "lengths", "seg_index", "self_qkv", "self_out", "cross_qkv", "cross_out",
    "ffn_in", "ffn_out", "writer_qkv", "writer_out", "gains", "out_cot", "mem_cot",
)
OUTPUTS = ("enc_out", "new_memory", "input_grad", "memory_grad", "grads")
GRAD = dict(
    self_qkv=0, self_out=1536, cross_qkv=2048, cross_out=3584, ffn_in=4096, ffn_out=6144,
    writer_qkv=8192, writer_out=9728, gains=10240,
)
GRAD_ROWS = 10752


def scratch_of(docs, rows, slots):
    tokens, slot_rows = docs * rows, docs * slots
    own = slot_rows // 4
    pairs = 2 * docs
    dma = pltpu.SemaphoreType.DMA
    return dict(
        hall=pltpu.VMEM((docs * SEG, D), LOW),
        my_qkv=pltpu.VMEM((D, 384), LOW),
        unit0=pltpu.VMEM((tokens, D), F32),
        unit1=pltpu.VMEM((tokens, D), F32),
        unit2=pltpu.VMEM((tokens, D), F32),
        unit4=pltpu.VMEM((tokens, D), F32),
        unit3=pltpu.VMEM((slot_rows, D), F32),
        inv0=pltpu.VMEM((tokens, 1), F32),
        inv1=pltpu.VMEM((tokens, 1), F32),
        inv2=pltpu.VMEM((tokens, 1), F32),
        inv4=pltpu.VMEM((tokens, 1), F32),
        inv3=pltpu.VMEM((slot_rows, 1), F32),
        hm=pltpu.VMEM((slot_rows, D), LOW),
        query=pltpu.VMEM((docs, 2 * SEG, 128), LOW),
        key=pltpu.VMEM((docs, SEG, 128), LOW),
        value=pltpu.VMEM((docs, SEG, 128), LOW),
        prob=pltpu.VMEM((docs, BLOCK_ROWS[-1], 256), LOW),
        mix_t=pltpu.VMEM((docs, SEG, 128), F32),
        mix_out=pltpu.VMEM((docs, SEG, 128), LOW),
        mix=pltpu.VMEM((tokens, D), LOW),
        acc=pltpu.VMEM((tokens, D), F32),
        res=pltpu.VMEM((tokens, D), F32),
        h1=pltpu.VMEM((tokens, D), LOW),
        h2=pltpu.VMEM((tokens, D), LOW),
        cq=pltpu.VMEM((tokens, D), LOW),
        cross_k=pltpu.VMEM((pairs, 256, 256), LOW),
        cross_v=pltpu.VMEM((pairs, 256, 256), LOW),
        cross_p=pltpu.VMEM((pairs, 256, 128), LOW),
        co=pltpu.VMEM((tokens, D), LOW),
        z=pltpu.VMEM((4, tokens, D), LOW),
        slope=pltpu.VMEM((4, tokens, D), LOW),
        src=pltpu.VMEM((tokens + own, D), LOW),
        wkey=pltpu.VMEM((tokens + own, D), LOW),
        wvalue=pltpu.VMEM((tokens + own, D), LOW),
        dkey=pltpu.VMEM((tokens + own, D), LOW),
        dvalue=pltpu.VMEM((tokens + own, D), LOW),
        wquery=pltpu.VMEM((pairs, 256, 256), LOW),
        dmix=pltpu.VMEM((pairs, 256, 256), LOW),
        dmix_t=pltpu.VMEM((pairs, HD, 256), F32),
        wscore=pltpu.VMEM((pairs, rows + slots // 4, 256), F32),
        wdprob=pltpu.VMEM((pairs, rows + slots // 4, 256), F32),
        wpart=pltpu.VMEM((4, pairs * HD, 256), LOW),
        wstat=pltpu.VMEM((4, pairs * 8, 256), F32),
        wo=pltpu.VMEM((slot_rows, D), LOW),
        low=pltpu.VMEM((tokens, D), LOW),
        dsend=pltpu.VMEM((tokens, D), LOW),
        dcq=pltpu.VMEM((tokens, D), LOW),
        parts=pltpu.VMEM((4, 3 * own, D), LOW),
        landed_parts=pltpu.VMEM((4, 3 * own, D), LOW),
        slot_sum=pltpu.VMEM((3 * own, D), LOW),
        mgrad=pltpu.VMEM((4, own, D), LOW),
        dmix_all=pltpu.VMEM((docs * SEG, 128), LOW),
        dk=pltpu.VMEM((SEG, 128), F32),
        dv=pltpu.VMEM((SEG, 128), F32),
        dqkv=pltpu.VMEM((SEG, 384), LOW),
        qkv_grad=pltpu.VMEM((D, 384), F32),
        dh=pltpu.VMEM((docs * SEG, D), LOW),
        dh_near=pltpu.VMEM((docs, 2 * rows, D), LOW),
        dh_pass=pltpu.VMEM((docs, rows, D), LOW),
        dh_far=pltpu.VMEM((docs, rows, D), LOW),
        gain_sum=pltpu.VMEM((5, 8, D), F32),
        grad=pltpu.VMEM((GRAD_ROWS, D), LOW),
        hs=dma((docs, 3)),
        hr=dma((docs, 3)),
        os=dma((docs, 3)),
        orr=dma((docs, 3)),
        ws=dma((2, 3)),
        wr=dma((2, 3)),
        ps=dma((3,)),
        pr=dma((3,)),
        ms=dma((3,)),
        mr=dma((3,)),
        ds=dma((docs, 3)),
        dr=dma((docs, 3)),
        ns=dma((docs, 3)),
        nr=dma((docs, 3)),
        out_sem=dma((1,)),
    )


def layer_kernel(docs, rows, slots, names, *refs):
    r = types.SimpleNamespace(**dict(zip(names, refs)))
    tokens, slot_rows = docs * rows, docs * slots
    own = slots // 4
    owned = docs * own
    s = lax.axis_index("seq")
    bit0, bit1 = lax.rem(s, 2), lax.div(s, 2)
    near = s + 1 - 2 * bit0
    far = s + 2 - 4 * bit1
    across = near + 2 - 4 * bit1
    peers = (near, far, across)

    def remote(source, target, send_sem, recv_sem, to):
        return pltpu.make_async_remote_copy(
            src_ref=source, dst_ref=target, send_sem=send_sem, recv_sem=recv_sem,
            device_id={"seq": to}, device_id_type=MESH,
        )

    def valid(d):
        return jnp.minimum(r.lengths[d] - r.seg_index[d] * SEG, SEG)

    def gain(k):
        return r.gains[k : k + 1, :]

    def add_gain(k, values):
        r.gain_sum[k] += jnp.sum(values.reshape(-1, 8, D), axis=0)

    barrier = pltpu.get_barrier_semaphore()
    for peer in peers:
        pl.semaphore_signal(barrier, inc=1, device_id={"seq": peer}, device_id_type=MESH)

    r.gain_sum[...] = jnp.zeros_like(r.gain_sum)

    def first(here, t):
        low, unit, inverse = norm_rows(r.x[here, :].astype(F32), gain(0))
        r.unit0[here, :] = unit
        r.inv0[here, :] = inverse
        per = rows // TILE
        r.hall[rows_at(lax.div(t, per) * SEG + s * rows + lax.rem(t, per) * TILE, TILE), :] = low

    tiles(tokens, TILE, first)
    pl.semaphore_wait(barrier, 3)

    def h_copy(d, kind):
        place = r.hall.at[rows_at(d * SEG + (s, s, far)[kind] * rows, rows)]
        return remote(place, place, r.hs.at[d, kind], r.hr.at[d, kind], (near, far, near)[kind])

    for d in range(docs):
        h_copy(d, 0).start()
        h_copy(d, 1).start()

    for i in range(3):
        r.my_qkv[:, i * 128 : (i + 1) * 128] = r.self_qkv[i, :, pl.ds(pl.multiple_of(s * 128, 128), 128)]

    def slot_norm(here, t):
        low, unit, inverse = norm_rows(r.memory[here, :].astype(F32), gain(3))
        r.unit3[here, :] = unit
        r.inv3[here, :] = inverse
        r.hm[here, :] = low

    tiles(slot_rows, TILE, slot_norm)
    for d in range(docs):
        r.src[tokens + d * own : tokens + (d + 1) * own, :] = r.hm[rows_at(d * slots + s * own, own), :]
    hm = r.hm[...]
    hm_own = r.src[tokens:, :]
    r.wkey[tokens:, :] = nn(hm_own, r.writer_qkv[1]).astype(LOW)
    r.wvalue[tokens:, :] = nn(hm_own, r.writer_qkv[2]).astype(LOW)

    def place_heads(target, values):
        values = values.astype(LOW).astype(F32)
        for d in range(docs):
            for g in range(2):
                piece = values[d * slots : (d + 1) * slots, g * 256 : (g + 1) * 256]
                target[2 * d + g] = four_heads(piece).astype(LOW)

    place_heads(r.cross_k, nn(hm, r.cross_qkv[1]))
    place_heads(r.cross_v, nn(hm, r.cross_qkv[2]))
    place_heads(r.wquery, nn(hm, r.writer_qkv[0]) * SCALE)
    dwo = nt(r.mem_cot[...], r.writer_out[...]).astype(LOW).astype(F32)
    for d in range(docs):
        for g in range(2):
            piece = dwo[d * slots : (d + 1) * slots, g * 256 : (g + 1) * 256]
            spread = four_heads(piece)
            r.dmix[2 * d + g] = spread.astype(LOW)
            r.dmix_t[2 * d + g] = own_blocks(spread.T)

    def o_copy(d, k):
        to = peers[k]
        return remote(
            r.mix_out.at[d, rows_at(to * rows, rows)],
            r.mix.at[rows_at(d * rows, rows), pl.ds(pl.multiple_of(s * 128, 128), 128)],
            r.os.at[d, k], r.orr.at[d, k], to,
        )

    h_copy(0, 1).wait_recv()
    h_copy(0, 2).start()

    def attend(d):
        h_copy(d, 0).wait_recv()
        h_copy(d, 2).wait_recv()
        normed = r.hall[rows_at(d * SEG, SEG), :]
        full = nn(normed, r.my_qkv[...])
        r.key[d] = full[:, 128:256].astype(LOW)
        r.value[d] = full[:, 256:].astype(LOW)
        live = valid(d)
        for i in range(BLOCKS):
            depth = 128 * (i + 1)
            queries = (full[i * 128 : (i + 1) * 128, :128] * SCALE).astype(LOW).astype(F32)
            stacked = head_stack(queries).astype(LOW)
            r.query[d, i * 256 : (i + 1) * 256, :] = stacked
            scores = nt(r.key[d, :depth, :], stacked)
            key_pos = lax.broadcasted_iota(jnp.int32, scores.shape, 0)
            query_pos = i * 128 + lax.rem(lax.broadcasted_iota(jnp.int32, scores.shape, 1), 128)
            scores = jnp.where((key_pos <= query_pos) & (key_pos < live), scores, SHUT)
            powers = jnp.exp(scores - jnp.max(scores, axis=0, keepdims=True))
            inverse = 1.0 / jnp.sum(powers, axis=0, keepdims=True)
            probs = (powers * inverse).astype(LOW)
            r.prob[d, BLOCK_ROWS[i] : BLOCK_ROWS[i + 1], :] = probs
            mixed = head_pick(tn(r.value[d, :depth, :], probs))
            r.mix_t[d, i * 128 : (i + 1) * 128, :] = mixed
            r.mix_out[d, i * 128 : (i + 1) * 128, :] = mixed.T.astype(LOW)
        for k in range(3):
            o_copy(d, k).start()
        r.mix[rows_at(d * rows, rows), pl.ds(pl.multiple_of(s * 128, 128), 128)] = r.mix_out[
            d, rows_at(s * rows, rows), :
        ]

        @pl.when(d < docs - 1)
        def _():
            h_copy(d + 1, 1).wait_recv()
            h_copy(d + 1, 2).start()

    each(docs, attend)
    for d in range(docs):
        for k in range(3):
            h_copy(d, k).wait_send()
    for d in range(docs):
        for k in range(3):
            o_copy(d, k).wait()

    r.acc[...] = nn(r.mix[...], r.self_out[...])

    def second(here, t):
        total = r.x[here, :].astype(F32) + r.acc[here, :]
        r.res[here, :] = total
        low, unit, inverse = norm_rows(total, gain(1))
        r.unit1[here, :] = unit
        r.inv1[here, :] = inverse
        r.h1[here, :] = low

    tiles(tokens, TILE, second)
    r.cq[...] = (nn(r.h1[...], r.cross_qkv[0]) * SCALE).astype(LOW)

    def cross(d):
        here = rows_at(d * rows, rows)
        for g in range(2):
            columns = slice(g * 256, (g + 1) * 256)
            scores = nt(r.cross_k[2 * d + g], r.cq[here, columns]).reshape(4, slots, rows)
            powers = jnp.exp(scores - jnp.max(scores, axis=1, keepdims=True))
            inverse = 1.0 / jnp.sum(powers, axis=1, keepdims=True)
            probs = (powers * inverse).reshape(256, rows).astype(LOW)
            r.cross_p[2 * d + g] = probs
            r.co[here, columns] = tn(probs, r.cross_v[2 * d + g]).astype(LOW)

    each(docs, cross)
    r.acc[...] = nn(r.co[...], r.cross_out[...])

    def third(here, t):
        total = r.res[here, :] + r.acc[here, :]
        r.res[here, :] = total
        low, unit, inverse = norm_rows(total, gain(2))
        r.unit2[here, :] = unit
        r.inv2[here, :] = inverse
        r.h2[here, :] = low

    tiles(tokens, TILE, third)

    rate, cube = 0.7978845608028654, 0.044715

    def feed(c):
        columns = pl.ds(pl.multiple_of(c * D, D), D)
        r.acc[...] = nn(r.h2[...], r.ffn_in[:, columns])

        def gelu(here, t):
            u = r.acc[here, :]
            square = u * u
            bend = jnp.tanh(rate * u * (1.0 + cube * square))
            half = 0.5 * (1.0 + bend)
            r.z[c, here, :] = (u * half).astype(LOW)
            slope = half + (0.5 * rate) * u * (1.0 - bend * bend) * (1.0 + 3.0 * cube * square)
            r.slope[c, here, :] = slope.astype(LOW)

        tiles(tokens, TILE, gelu)
        r.res[...] += nn(r.z[c], r.ffn_out[columns, :])

    each(4, feed)

    def fourth(here, t):
        total = r.res[here, :]
        r.enc_out[here, :] = total.astype(LOW)
        low, unit, inverse = norm_rows(total, gain(4))
        r.unit4[here, :] = unit
        r.inv4[here, :] = inverse
        r.src[here, :] = low

    tiles(tokens, TILE, fourth)

    written = r.src[:tokens, :]
    r.wkey[:tokens, :] = nn(written, r.writer_qkv[1]).astype(LOW)
    r.wvalue[:tokens, :] = nn(written, r.writer_qkv[2]).astype(LOW)

    def of_doc(ref, d, columns):
        return jnp.concatenate(
            [ref[rows_at(d * rows, rows), columns], ref[rows_at(tokens + d * own, own), columns]], axis=0
        )

    def write(d):
        live = valid(d)
        for g in range(2):
            pair = 2 * d + g
            columns = slice(g * 256, (g + 1) * 256)
            scores = nt(of_doc(r.wkey, d, columns), r.wquery[pair])
            key_pos = lax.broadcasted_iota(jnp.int32, scores.shape, 0)
            scores = jnp.where((key_pos >= rows) | (s * rows + key_pos < live), scores, SHUT)
            top = jnp.max(scores, axis=0, keepdims=True)
            powers = jnp.exp(scores - top)
            total = jnp.sum(powers, axis=0, keepdims=True)
            r.wscore[pair] = scores
            part = own_blocks(tn(of_doc(r.wvalue, d, columns), powers.astype(LOW)))
            r.wpart[s, rows_at(pair * HD, HD), :] = (part * (1.0 / total)).astype(LOW)
            r.wstat[s, pl.ds(pl.multiple_of(pair * 8, 8), 8), :] = jnp.broadcast_to(
                top + jnp.log(total), (8, 256)
            )

    each(docs, write)

    def w_copy(which, kind):
        place = (r.wpart, r.wstat)[which].at[(s, s, far)[kind]]
        return remote(place, place, r.ws.at[which, kind], r.wr.at[which, kind], (near, far, near)[kind])

    for kind in (1, 0):
        for which in range(2):
            w_copy(which, kind).start()

    def write_back_early(d):
        for g in range(2):
            columns = slice(g * 256, (g + 1) * 256)
            r.wdprob[2 * d + g] = nt(of_doc(r.wvalue, d, columns), r.dmix[2 * d + g])

    each(docs, write_back_early)
    for which in range(2):
        w_copy(which, 1).wait_recv()
        w_copy(which, 2).start()
    for which in range(2):
        w_copy(which, 0).wait_recv()
        w_copy(which, 2).wait_recv()

    def write_back(d):
        for g in range(2):
            pair = 2 * d + g
            columns = slice(g * 256, (g + 1) * 256)
            stats = [r.wstat[k, pl.ds(pl.multiple_of(pair * 8, 8), 8), :][0:1] for k in range(4)]
            top = functools.reduce(jnp.maximum, stats)
            weights = [jnp.exp(stat - top) for stat in stats]
            total = sum(weights)
            inverse = 1.0 / total
            mixed = sum(
                (weights[k] * inverse) * r.wpart[k, rows_at(pair * HD, HD), :].astype(F32) for k in range(4)
            )
            delta = jnp.sum(mixed * r.dmix_t[pair], axis=0, keepdims=True)
            probs = jnp.exp(r.wscore[pair] - (top + jnp.log(total)))
            slopes = (probs * (r.wdprob[pair] - delta)).astype(LOW)
            dkey = nn(slopes, r.wquery[pair]).astype(LOW)
            dvalue = nn(probs.astype(LOW), r.dmix[pair]).astype(LOW)
            r.dkey[rows_at(d * rows, rows), columns] = dkey[:rows]
            r.dkey[rows_at(tokens + d * own, own), columns] = dkey[rows:]
            r.dvalue[rows_at(d * rows, rows), columns] = dvalue[:rows]
            r.dvalue[rows_at(tokens + d * own, own), columns] = dvalue[rows:]
            dquery = own_blocks(tn(slopes, of_doc(r.wkey, d, columns))).astype(LOW)
            for k in range(4):
                r.parts[k, rows_at(d * own, own), columns] = dquery[k * own : (k + 1) * own]
            r.wo[rows_at(d * slots, slots), columns] = swap(mixed.astype(LOW).astype(F32)).astype(LOW)

    each(docs, write_back)
    for which in range(2):
        for kind in range(3):
            w_copy(which, kind).wait_send()

    r.acc[...] = nt(r.dkey[:tokens, :], r.writer_qkv[1]) + nt(r.dvalue[:tokens, :], r.writer_qkv[2])

    def fourth_back(here, t):
        grad, unit = r.acc[here, :], r.unit4[here, :]
        add_gain(4, grad * unit)
        total = r.out_cot[here, :].astype(F32) + norm_back(grad, unit, r.inv4[here, :], gain(4))
        r.res[here, :] = total
        r.low[here, :] = total.astype(LOW)

    tiles(tokens, TILE, fourth_back)

    def put(base, values):
        r.grad[base : base + D, :] = values.astype(LOW)

    put(GRAD["writer_qkv"] + D, tn(r.src[...], r.dkey[...]))
    put(GRAD["writer_qkv"] + 2 * D, tn(r.src[...], r.dvalue[...]))

    def feed_back(c):
        columns = pl.ds(pl.multiple_of(c * D, D), D)
        r.unit4[...] = nt(r.low[...], r.ffn_out[columns, :])
        r.grad[pl.ds(pl.multiple_of(GRAD["ffn_out"] + c * D, D), D), :] = tn(r.z[c], r.low[...]).astype(LOW)

        def bent(here, t):
            r.z[c, here, :] = (r.unit4[here, :] * r.slope[c, here, :].astype(F32)).astype(LOW)

        tiles(tokens, TILE, bent)
        du = r.z[c]
        r.grad[pl.ds(pl.multiple_of(GRAD["ffn_in"] + c * D, D), D), :] = tn(r.h2[...], du).astype(LOW)
        back = nt(du, r.ffn_in[:, columns])

        @pl.when(c == 0)
        def _():
            r.acc[...] = back

        @pl.when(c > 0)
        def _():
            r.acc[...] += back

    each(4, feed_back)

    def third_back(here, t):
        grad, unit = r.acc[here, :], r.unit2[here, :]
        add_gain(2, grad * unit)
        total = r.res[here, :] + norm_back(grad, unit, r.inv2[here, :], gain(2))
        r.res[here, :] = total
        r.low[here, :] = total.astype(LOW)

    tiles(tokens, TILE, third_back)

    r.dsend[...] = nt(r.low[...], r.cross_out[...]).astype(LOW)
    put(GRAD["cross_out"], tn(r.co[...], r.low[...]))

    def cross_back(d):
        here = rows_at(d * rows, rows)
        for g in range(2):
            pair = 2 * d + g
            columns = slice(g * 256, (g + 1) * 256)
            dmix = r.dsend[here, columns]
            dprobs = nt(r.cross_v[pair], dmix)
            probs = r.cross_p[pair].astype(F32)
            delta = jnp.sum((probs * dprobs).reshape(4, slots, rows), axis=1, keepdims=True)
            slopes = (probs * (dprobs.reshape(4, slots, rows) - delta).reshape(256, rows)).astype(LOW)
            r.dcq[here, columns] = (
                tn(slopes, r.cross_k[pair]).astype(LOW).astype(F32) * SCALE
            ).astype(LOW)
            dkey = own_blocks(nn(slopes, r.cq[here, columns])).astype(LOW)
            dvalue = own_blocks(nn(r.cross_p[pair], dmix)).astype(LOW)
            for k in range(4):
                r.parts[k, rows_at(owned + d * own, own), columns] = dkey[k * own : (k + 1) * own]
                r.parts[k, rows_at(2 * owned + d * own, own), columns] = dvalue[k * own : (k + 1) * own]

    each(docs, cross_back)

    def p_copy(k):
        return remote(r.parts.at[peers[k]], r.landed_parts.at[s], r.ps.at[k], r.pr.at[k], peers[k])

    r.acc[...] = nt(r.dcq[...], r.cross_qkv[0])

    def second_back(here, t):
        grad, unit = r.acc[here, :], r.unit1[here, :]
        add_gain(1, grad * unit)
        total = r.res[here, :] + norm_back(grad, unit, r.inv1[here, :], gain(1))
        r.res[here, :] = total
        r.low[here, :] = total.astype(LOW)

    tiles(tokens, TILE, second_back)

    r.dsend[...] = nt(r.low[...], r.self_out[...]).astype(LOW)

    def d_copy(d, k):
        to = peers[k]
        return remote(
            r.dsend.at[rows_at(d * rows, rows), pl.ds(pl.multiple_of(to * 128, 128), 128)],
            r.dmix_all.at[rows_at(d * SEG + s * rows, rows)],
            r.ds.at[d, k], r.dr.at[d, k], to,
        )

    for d in range(docs):
        for k in range(3):
            d_copy(d, k).start()
        r.dmix_all[rows_at(d * SEG + s * rows, rows), :] = r.dsend[
            d * rows : (d + 1) * rows, pl.ds(pl.multiple_of(s * 128, 128), 128)
        ]
    for k in range(3):
        p_copy(k).start()
    put(GRAD["cross_qkv"], tn(r.h1[...], r.dcq[...]))
    put(GRAD["self_out"], tn(r.mix[...], r.low[...]))
    r.new_memory[...] = (r.memory[...].astype(F32) + nn(r.wo[...], r.writer_out[...])).astype(LOW)

    def n_copy(d, kind):
        source = (
            r.dh.at[rows_at(d * SEG + near * rows, rows)],
            r.dh.at[rows_at(d * SEG + across * rows, rows)],
            r.dh_pass.at[d],
        )[kind]
        target = (r.dh_near.at[d, pl.ds(0, rows)], r.dh_near.at[d, pl.ds(rows, rows)], r.dh_far.at[d])[kind]
        return remote(source, target, r.ns.at[d, kind], r.nr.at[d, kind], (near, near, far)[kind])

    def pass_on(d):
        n_copy(d, 1).wait_recv()
        r.dh_pass[d] = (
            r.dh[rows_at(d * SEG + far * rows, rows), :].astype(F32)
            + r.dh_near[d, rows : 2 * rows, :].astype(F32)
        ).astype(LOW)
        n_copy(d, 2).start()

    r.qkv_grad[...] = jnp.zeros_like(r.qkv_grad)

    def attend_back(d):
        for k in range(3):
            d_copy(d, k).wait_recv()
        r.dk[...] = jnp.zeros_like(r.dk)
        r.dv[...] = jnp.zeros_like(r.dv)
        for i in range(BLOCKS):
            depth = 128 * (i + 1)
            dmix = r.dmix_all[rows_at(d * SEG + i * 128, 128), :].astype(F32)
            stacked = head_stack(dmix).astype(LOW)
            queries = r.query[d, i * 256 : (i + 1) * 256, :]
            product = dmix.T * r.mix_t[d, i * 128 : (i + 1) * 128, :]
            delta = jnp.concatenate(
                [
                    jnp.sum(product[:HD], axis=0, keepdims=True),
                    jnp.sum(product[HD:], axis=0, keepdims=True),
                ],
                axis=1,
            )
            probs = r.prob[d, BLOCK_ROWS[i] : BLOCK_ROWS[i + 1], :]
            dprobs = nt(r.value[d, :depth, :], stacked)
            slopes = (probs.astype(F32) * (dprobs - delta)).astype(LOW)
            r.dk[:depth, :] += nn(slopes, queries)
            r.dv[:depth, :] += nn(probs, stacked)
            dquery = head_pick(tn(r.key[d, :depth, :], slopes)).T
            r.dqkv[i * 128 : (i + 1) * 128, :128] = (dquery.astype(LOW).astype(F32) * SCALE).astype(LOW)
        r.dqkv[:, 128:256] = r.dk[...].astype(LOW)
        r.dqkv[:, 256:] = r.dv[...].astype(LOW)
        r.dh[rows_at(d * SEG, SEG), :] = nt(r.dqkv[...], r.my_qkv[...]).astype(LOW)
        n_copy(d, 1).start()
        n_copy(d, 0).start()
        r.qkv_grad[...] += tn(r.hall[rows_at(d * SEG, SEG), :], r.dqkv[...])

        @pl.when(d > 0)
        def _():
            pass_on(d - 1)

    each(docs, attend_back)
    pass_on(docs - 1)
    for i in range(3):
        base = GRAD["self_qkv"] + i * D
        r.grad[base : base + D, :] = jnp.zeros((D, D), LOW)
        r.grad[base : base + D, pl.ds(pl.multiple_of(s * 128, 128), 128)] = r.qkv_grad[
            :, i * 128 : (i + 1) * 128
        ].astype(LOW)

    for k in range(3):
        p_copy(k).wait()
    r.landed_parts[s] = r.parts[s]
    r.slot_sum[...] = sum(r.landed_parts[k].astype(F32) for k in range(4)).astype(LOW)
    r.slot_sum[:owned, :] = (r.slot_sum[:owned, :].astype(F32) * SCALE).astype(LOW)
    dwq, dck, dcv = (r.slot_sum[k * owned : (k + 1) * owned, :] for k in range(3))
    dhm = (
        nt(dwq, r.writer_qkv[0])
        + nt(r.dkey[tokens:, :], r.writer_qkv[1])
        + nt(r.dvalue[tokens:, :], r.writer_qkv[2])
        + nt(dck, r.cross_qkv[1])
        + nt(dcv, r.cross_qkv[2])
    )
    for d in range(docs):
        here = rows_at(d * slots + s * own, own)
        grad, unit = dhm[d * own : (d + 1) * own], r.unit3[here, :]
        add_gain(3, grad * unit)
        total = r.mem_cot[here, :].astype(F32) + norm_back(grad, unit, r.inv3[here, :], gain(3))
        r.mgrad[s, d * own : (d + 1) * own, :] = total.astype(LOW)

    def m_copy(k):
        place = r.mgrad.at[s]
        return remote(place, place, r.ms.at[k], r.mr.at[k], peers[k])

    for k in range(3):
        m_copy(k).start()
    hm_own = r.src[tokens:, :]
    put(GRAD["writer_qkv"], tn(hm_own, dwq))
    put(GRAD["cross_qkv"] + D, tn(hm_own, dck))
    put(GRAD["cross_qkv"] + 2 * D, tn(hm_own, dcv))
    wo_own = jnp.concatenate([r.wo[rows_at(d * slots + s * own, own), :] for d in range(docs)], axis=0)
    r4_own = jnp.concatenate([r.mem_cot[rows_at(d * slots + s * own, own), :] for d in range(docs)], axis=0)
    put(GRAD["writer_out"], tn(wo_own, r4_own))

    for d in range(docs):
        n_copy(d, 0).wait()
        n_copy(d, 1).wait_send()
        n_copy(d, 2).wait()

    def first_back(here, t):
        per = rows // TILE
        d, at = lax.div(t, per), lax.rem(t, per) * TILE
        grad = (
            r.dh[rows_at(d * SEG + s * rows + at, TILE), :].astype(F32)
            + r.dh_near[d, rows_at(at, TILE), :].astype(F32)
            + r.dh_far[d, rows_at(at, TILE), :].astype(F32)
        )
        unit = r.unit0[here, :]
        add_gain(0, grad * unit)
        r.input_grad[here, :] = r.res[here, :] + norm_back(grad, unit, r.inv0[here, :], gain(0))

    tiles(tokens, TILE, first_back)
    for d in range(docs):
        for k in range(3):
            d_copy(d, k).wait_send()
    for k in range(3):
        m_copy(k).wait()
    for k in range(4):
        for d in range(docs):
            r.memory_grad[d * slots + k * own : d * slots + (k + 1) * own, :] = r.mgrad[
                k, d * own : (d + 1) * own, :
            ].astype(F32)
    r.grad[GRAD["gains"] :, :] = jnp.zeros((GRAD_ROWS - GRAD["gains"], D), LOW)
    r.grad[GRAD["gains"] : GRAD["gains"] + 16, :] = jnp.concatenate(
        [jnp.sum(r.gain_sum[k], axis=0, keepdims=True) for k in range(5)] + [jnp.zeros((11, D), F32)], axis=0
    ).astype(LOW)
    store = pltpu.make_async_copy(r.grad, r.grads, r.out_sem.at[0])
    store.start()
    store.wait()


def on_device(*arguments):
    seg_input, memory = arguments[0], arguments[1]
    docs, rows, _ = seg_input.shape
    slots = memory.shape[1]
    scratch = scratch_of(docs, rows, slots)
    vmem, smem, anywhere = (pl.BlockSpec(memory_space=m) for m in (pltpu.VMEM, pltpu.SMEM, pl.ANY))
    arguments = list(arguments)
    for k in (0, 1, 13, 14):
        arguments[k] = arguments[k].reshape(-1, D)
    names = INPUTS + OUTPUTS + tuple(scratch)
    encoded, updated, input_grad, memory_grad, flat = pl.pallas_call(
        functools.partial(layer_kernel, docs, rows, slots, names),
        out_shape=(
            jax.ShapeDtypeStruct((docs * rows, D), LOW),
            jax.ShapeDtypeStruct((docs * slots, D), LOW),
            jax.ShapeDtypeStruct((docs * rows, D), F32),
            jax.ShapeDtypeStruct((docs * slots, D), F32),
            jax.ShapeDtypeStruct((GRAD_ROWS, D), LOW),
        ),
        in_specs=[smem if name in ("lengths", "seg_index") else vmem for name in INPUTS],
        out_specs=(vmem, vmem, vmem, vmem, anywhere),
        scratch_shapes=list(scratch.values()),
        compiler_params=pltpu.CompilerParams(
            collective_id=1, has_side_effects=True, vmem_limit_bytes=60 << 20
        ),
    )(*arguments)
    summed = reduce_weights(flat, lax.axis_size("docs")).astype(F32)
    return (
        encoded.reshape(docs, rows, D),
        updated.reshape(docs, slots, D),
        input_grad.reshape(docs, rows, D),
        memory_grad.reshape(docs, slots, D),
        summed[0:1536].reshape(3, D, D),
        summed[1536:2048],
        summed[2048:3584].reshape(3, D, D),
        summed[3584:4096],
        jnp.concatenate([summed[4096 + c * D : 4096 + (c + 1) * D] for c in range(4)], axis=1),
        summed[6144:8192],
        summed[8192:9728].reshape(3, D, D),
        summed[9728:10240],
        summed[10240:10245],
    )


def solution(mesh):
    row, slot, whole = P("docs", "seq", None), P("docs", None, None), P()
    return jax.shard_map(
        on_device,
        mesh=mesh,
        in_specs=(row, slot, P("docs"), P("docs")) + (whole,) * 9 + (row, slot),
        out_specs=(row, slot, row, slot) + (whole,) * 9,
        check_vma=False,
    )
```

```python
import functools
import types

import jax
import jax.numpy as jnp
from jax import lax
from jax.experimental import pallas as pl
from jax.experimental.pallas import tpu as pltpu
from jax.sharding import PartitionSpec as P

MESH = pl.DeviceIdType.MESH
F32, LOW = jnp.float32, jnp.bfloat16
D = 512
HD = 64
SEG = 512
SHUT = -1e30
SCALE = HD ** (-0.5)

CORE, X, Y, Z0, Z1 = ("seq", 1), ("seq", 2), ("docs", 1), ("docs", 2), ("docs", 4)
ORDERS = (
    (CORE, X, Y, Z0, Z1),
    (CORE, Y, X, Z0, Z1),
    (CORE, Z0, Z1, X, Y),
)
GROUP = 8


def place_of(stage):
    axis, stride = stage
    index = lax.axis_index(axis)
    bit = lax.rem(lax.div(index, stride), 2)
    return bit, {axis: index + stride * (1 - 2 * bit)}


def greet(docs_count):
    barrier = pltpu.get_barrier_semaphore()
    partners = [place_of(stage)[1] for stage in ORDERS[0]] + outer_partners(docs_count)
    for partner in partners:
        pl.semaphore_signal(barrier, inc=1, device_id=partner, device_id_type=MESH)
    pl.semaphore_wait(barrier, len(partners))


def outer_partners(docs_count):
    index = lax.axis_index("docs")
    return [{"docs": lax.rem(index + GROUP * k, docs_count)} for k in range(1, docs_count // GROUP)]


def add_rows(total, start, rows, landed, first, share=None):
    tile = 16

    def turn(t, carry):
        here = pl.ds(pl.multiple_of(start + t * tile, tile), tile)
        there = pl.ds(pl.multiple_of(first + t * tile, tile), tile)
        more = landed[there, :].astype(F32)
        if share is not None:
            more = more * share
        total[here, :] = (total[here, :].astype(F32) + more).astype(total.dtype)
        return carry

    lax.fori_loop(0, rows // tile, turn, 0)


def reduce_kernel(docs_count, chunks, flat_ref, out_ref, total, landed, outer, load_sem, ss, rs, gs, gr, os, orr, store_sem):
    loads = []
    for c, (base, rows, order) in enumerate(chunks):
        load = pltpu.make_async_copy(flat_ref.at[pl.ds(base, rows)], total.at[pl.ds(base, rows)], load_sem.at[c])
        load.start()
        loads.append(load)
    greet(docs_count)
    share = 1.0 - lax.div(lax.axis_index("seq"), 2).astype(F32)
    stages = len(ORDERS[0])
    state = []
    flying = [None] * len(chunks)

    def send(c, j, start, size):
        base, rows, order = chunks[c]
        bit, partner = place_of(ORDERS[order][j])
        half = size // 2
        keep = start + bit * half
        give = start + (1 - bit) * half
        first = base + rows - size
        copy = pltpu.make_async_remote_copy(
            src_ref=total.at[pl.ds(pl.multiple_of(give, 16), half)],
            dst_ref=landed.at[pl.ds(first, half)],
            send_sem=ss.at[c, j],
            recv_sem=rs.at[c, j],
            device_id=partner,
            device_id_type=MESH,
        )
        copy.start()
        flying[c] = (copy, keep, half, first)

    for c, (base, rows, order) in enumerate(chunks):
        loads[c].wait()
        send(c, 0, base, rows)
    for j in range(stages):
        for c in range(len(chunks)):
            copy, keep, half, first = flying[c]
            copy.wait()
            add_rows(total, keep, half, landed, first, share if j == 0 else None)
            if j + 1 < stages:
                send(c, j + 1, keep, half)
            else:
                flying[c] = (keep, half)
    others = outer_partners(docs_count)
    if others:
        copies = []
        mine = lax.div(lax.axis_index("docs"), GROUP)
        for c in range(len(chunks)):
            keep, half = flying[c]
            share = pl.ds(chunks[c][0] // 32, half)
            piece = total.at[pl.ds(pl.multiple_of(keep, 16), half)]
            outer[mine, share, :] = piece[...]
            for k, partner in enumerate(others):
                copy = pltpu.make_async_remote_copy(
                    src_ref=piece,
                    dst_ref=outer.at[mine, share],
                    send_sem=os.at[c, k],
                    recv_sem=orr.at[c, k],
                    device_id=partner,
                    device_id_type=MESH,
                )
                copy.start()
                copies.append(copy)
        for copy in copies:
            copy.wait()
        for c in range(len(chunks)):
            keep, half = flying[c]
            share = pl.ds(chunks[c][0] // 32, half)
            parts = [outer[k, share, :].astype(jnp.float32) for k in range(len(others) + 1)]
            total[pl.ds(pl.multiple_of(keep, 16), half), :] = sum(parts).astype(total.dtype)

    def spread(c, j, start, size):
        base, rows, order = chunks[c]
        bit, partner = place_of(ORDERS[order][j])
        here = pl.ds(pl.multiple_of(start, 16), size)
        copy = pltpu.make_async_remote_copy(
            src_ref=(total if j == stages - 1 else out_ref).at[here],
            dst_ref=out_ref.at[here],
            send_sem=gs.at[c, j],
            recv_sem=gr.at[c, j],
            device_id=partner,
            device_id_type=MESH,
        )
        copy.start()
        flying[c] = (copy, start - bit * size, 2 * size)

    stores = []
    for c in range(len(chunks)):
        start, size = flying[c]
        here = pl.ds(pl.multiple_of(start, 16), size)
        store = pltpu.make_async_copy(total.at[here], out_ref.at[here], store_sem.at[c])
        store.start()
        stores.append(store)
        spread(c, stages - 1, start, size)
    for j in reversed(range(stages)):
        for c in range(len(chunks)):
            copy, start, size = flying[c]
            copy.wait()
            if j == stages - 1:
                stores[c].wait()
            if j > 0:
                spread(c, j - 1, start, size)


def reduce_weights(flat, docs_count):
    chunks = [(1024 * c, 1024, (0, 1, 0, 1, 2)[c % 5]) for c in range(10)] + [(10240, 512, 0)]
    count, stages, outers = len(chunks), len(ORDERS[0]), max(1, docs_count // GROUP)
    return pl.pallas_call(
        functools.partial(reduce_kernel, docs_count, chunks),
        out_shape=jax.ShapeDtypeStruct(flat.shape, flat.dtype),
        in_specs=[pl.BlockSpec(memory_space=pl.ANY)],
        out_specs=pl.BlockSpec(memory_space=pl.ANY),
        scratch_shapes=[
            pltpu.VMEM(flat.shape, flat.dtype),
            pltpu.VMEM(flat.shape, flat.dtype),
            pltpu.VMEM((outers, flat.shape[0] // 32, flat.shape[1]), flat.dtype),
            pltpu.SemaphoreType.DMA((count,)),
            pltpu.SemaphoreType.DMA((count, stages)),
            pltpu.SemaphoreType.DMA((count, stages)),
            pltpu.SemaphoreType.DMA((count, stages)),
            pltpu.SemaphoreType.DMA((count, stages)),
            pltpu.SemaphoreType.DMA((count, outers)),
            pltpu.SemaphoreType.DMA((count, outers)),
            pltpu.SemaphoreType.DMA((count,)),
        ],
        compiler_params=pltpu.CompilerParams(
            collective_id=0, has_side_effects=True, vmem_limit_bytes=56 << 20
        ),
    )(flat)


def dot(left, right, left_dim, right_dim):
    return lax.dot_general(
        left, right, (((left_dim,), (right_dim,)), ((), ())), preferred_element_type=F32
    )


def nn(left, right):
    return dot(left, right, 1, 0)


def nt(left, right):
    return dot(left, right, 1, 1)


def tn(left, right):
    return dot(left, right, 0, 0)


def tiles(rows, tile, body):
    def turn(t, carry):
        body(pl.ds(pl.multiple_of(t * tile, tile), tile), t)
        return carry

    lax.fori_loop(0, rows // tile, turn, 0)


def each(count, body):
    def turn(k, carry):
        body(k)
        return carry

    lax.fori_loop(0, count, turn, 0)


def rows_at(start, size):
    return pl.ds(pl.multiple_of(start, 16), size)


def norm_rows(values, gain_row):
    centered = values - jnp.mean(values, axis=-1, keepdims=True)
    inverse = lax.rsqrt(jnp.mean(centered * centered, axis=-1, keepdims=True) + 1e-05)
    unit = centered * inverse
    return (unit * gain_row).astype(LOW), unit, inverse


def norm_back(grad, unit, inverse, gain_row):
    scaled = grad * gain_row
    adjusted = (
        scaled
        - jnp.mean(scaled, axis=-1, keepdims=True)
        - unit * jnp.mean(scaled * unit, axis=-1, keepdims=True)
    )
    return adjusted * inverse


def same_head():
    left = lax.div(lax.broadcasted_iota(jnp.int32, (256, 256), 0), HD)
    right = lax.div(lax.broadcasted_iota(jnp.int32, (256, 256), 1), HD)
    return left == right


def four_heads(values):
    return jnp.where(same_head(), jnp.concatenate([values] * 4, axis=0), 0.0)


def own_blocks(values):
    return jnp.sum(jnp.where(same_head(), values, 0.0).reshape(4, HD, 256), axis=0)


def swap(values):
    return own_blocks(four_heads(values).T)


def head_stack(values):
    low_half = lax.broadcasted_iota(jnp.int32, values.shape, 1) < HD
    return jnp.concatenate(
        [jnp.where(low_half, values, 0.0), jnp.where(low_half, 0.0, values)], axis=0
    )


def head_pick(values):
    low_half = lax.broadcasted_iota(jnp.int32, (128, 128), 0) < HD
    return jnp.where(low_half, values[:, :128], values[:, 128:])


BLOCKS = SEG // 128
BLOCK_ROWS = [sum(128 * (k + 1) for k in range(i)) for i in range(BLOCKS + 1)]
PAIRS = D // 128
TILE = 64

WEIGHTS = (
    "self_qkv", "cross_qkv", "writer_qkv", "writer_out", "self_out", "cross_out", "ffn_in", "ffn_out",
)
INPUTS = (
    "x", "memory", "lengths", "seg_index", "self_qkv", "self_out", "cross_qkv", "cross_out",
    "ffn_in", "ffn_out", "writer_qkv", "writer_out", "gains", "out_cot", "mem_cot",
)
OUTPUTS = ("enc_out", "new_memory", "input_grad", "memory_grad", "grads")
GRAD = dict(
    self_qkv=0, self_out=1536, cross_qkv=2048, cross_out=3584, ffn_in=4096, ffn_out=6144,
    writer_qkv=8192, writer_out=9728, gains=10240,
)
GRAD_ROWS = 10752


def scratch_of(docs, rows, slots, weights):
    keys = SEG + slots
    dma = pltpu.SemaphoreType.DMA
    low = lambda *shape: pltpu.VMEM(shape, LOW)
    full = lambda *shape: pltpu.VMEM(shape, F32)
    fetched = {"w_" + name: pltpu.VMEM(weights[name].shape, LOW) for name in WEIGHTS}
    return dict(
        **fetched,
        x_all=low(SEG, D),
        cot_all=low(SEG, D),
        enc=low(SEG, D),
        in_grad=low(SEG, D),
        in_grad_all=low(docs * rows, D),
        slot_grad_all=low(docs * slots, D),
        unit0=full(SEG, D),
        unit1=full(SEG, D),
        unit2=full(SEG, D),
        unit4=full(SEG, D),
        unit3=full(slots, D),
        inv0=full(SEG, 1),
        inv1=full(SEG, 1),
        inv2=full(SEG, 1),
        inv4=full(SEG, 1),
        inv3=full(slots, 1),
        h0=low(SEG, D),
        h1=low(SEG, D),
        h2=low(SEG, D),
        src=low(keys, D),
        q=low(SEG, D),
        k=low(SEG, D),
        v=low(SEG, D),
        query=low(PAIRS, 2 * SEG, 128),
        prob=low(PAIRS, BLOCK_ROWS[-1], 256),
        mix_t=full(PAIRS, SEG, 128),
        mix=low(SEG, D),
        acc=full(SEG, D),
        res=full(SEG, D),
        cq=low(SEG, D),
        cross_k=low(2, 256, 256),
        cross_v=low(2, 256, 256),
        cross_p=low(2 * BLOCKS, 256, 128),
        cross_dk=full(2, 256, 256),
        cross_dv=full(2, 256, 256),
        co=low(SEG, D),
        z=low(4, SEG, D),
        slope=low(4, SEG, D),
        wkey=low(keys, D),
        wvalue=low(keys, D),
        dkey=low(keys, D),
        dvalue=low(keys, D),
        wquery=low(2, 256, 256),
        dmix=low(2, 256, 256),
        wo=low(slots, D),
        dwq=low(slots, D),
        dck=low(slots, D),
        dcv=low(slots, D),
        low=low(SEG, D),
        dsend=low(SEG, D),
        dcq=low(SEG, D),
        dq=low(SEG, D),
        dk=low(SEG, D),
        dv=low(SEG, D),
        dk_sum=full(SEG, 128),
        dv_sum=full(SEG, 128),
        gain_sum=full(5, 8, D),
        grad=low(GRAD_ROWS, D),
        load_sem=dma((len(WEIGHTS),)),
        xs=dma((3,)),
        xr=dma((3,)),
        cs=dma((3,)),
        cr=dma((3,)),
        es=dma((3,)),
        er=dma((3,)),
        us=dma((3,)),
        ur=dma((3,)),
        gs=dma((3,)),
        gr=dma((3,)),
        ms=dma((3,)),
        mr=dma((3,)),
        out_sem=dma((1,)),
    )


def layer_kernel(docs, rows, slots, names, *refs):
    r = types.SimpleNamespace(**dict(zip(names, refs)))
    s = lax.axis_index("seq")
    bit0, bit1 = lax.rem(s, 2), lax.div(s, 2)
    near = s + 1 - 2 * bit0
    far = s + 2 - 4 * bit1
    across = near + 2 - 4 * bit1
    peers = (near, far, across)

    def doc_of(index):
        return jnp.minimum(index, docs - 1)

    mine = doc_of(s)

    def remote(source, target, send_sem, recv_sem, to):
        return pltpu.make_async_remote_copy(
            src_ref=source, dst_ref=target, send_sem=send_sem, recv_sem=recv_sem,
            device_id={"seq": to}, device_id_type=MESH,
        )

    def gain(k):
        return r.gains[k : k + 1, :]

    def add_gain(k, values):
        r.gain_sum[k] += jnp.sum(values.reshape(-1, 8, D), axis=0)

    loads = {}
    for k, name in enumerate(WEIGHTS):
        loads[name] = pltpu.make_async_copy(getattr(r, name), getattr(r, "w_" + name), r.load_sem.at[k])
        loads[name].start()
    barrier = pltpu.get_barrier_semaphore()
    for peer in peers:
        pl.semaphore_signal(barrier, inc=1, device_id={"seq": peer}, device_id_type=MESH)
    r.gain_sum[...] = jnp.zeros_like(r.gain_sum)

    def slot_norm(here, t):
        low, unit, inverse = norm_rows(
            r.memory[rows_at(mine * slots + t * TILE, TILE), :].astype(F32), gain(3)
        )
        r.unit3[here, :] = unit
        r.inv3[here, :] = inverse
        r.src[rows_at(SEG + t * TILE, TILE), :] = low

    tiles(slots, TILE, slot_norm)
    pl.semaphore_wait(barrier, 3)

    def gather_copy(source, target, send_sem, recv_sem, k):
        return remote(
            source.at[rows_at(doc_of(peers[k]) * rows, rows)],
            target.at[rows_at(s * rows, rows)], send_sem.at[k], recv_sem.at[k], peers[k],
        )

    for k in range(3):
        gather_copy(r.x, r.x_all, r.xs, r.xr, k).start()
    own_rows = rows_at(s * rows, rows)
    r.x_all[own_rows, :] = r.x[rows_at(mine * rows, rows), :]
    r.cot_all[own_rows, :] = r.out_cot[rows_at(mine * rows, rows), :]

    def spread_copy(source, target, size, own, send_sem, recv_sem, k):
        start = mine * size
        if own:
            piece = source.at[rows_at(peers[k] * size, size)]
        else:
            piece = source.at[rows_at(start, size)]
        return remote(piece, target.at[rows_at(start, size)], send_sem.at[k], recv_sem.at[k], peers[k])

    def spread(*where):
        spread_copy(*where, 1).start()

        @pl.when(bit1 == 0)
        def _():
            spread_copy(*where, 0).start()
            spread_copy(*where, 2).start()

    def spread_wait(*where):
        spread_copy(*where, 1).wait()

        @pl.when(bit1 == 0)
        def _():
            spread_copy(*where, 0).wait()
            spread_copy(*where, 2).wait_send()

        @pl.when(bit1 == 1)
        def _():
            spread_copy(*where, 2).wait_recv()

    slot_range = pl.ds(SEG, slots)
    hm = r.src[slot_range, :]

    def place_heads(target, values):
        for g in range(2):
            piece = values[:, g * 256 : (g + 1) * 256].astype(LOW).astype(F32)
            target[g] = four_heads(piece).astype(LOW)

    loads["cross_qkv"].wait()
    place_heads(r.cross_k, nn(hm, r.w_cross_qkv[1]))
    place_heads(r.cross_v, nn(hm, r.w_cross_qkv[2]))
    loads["writer_qkv"].wait()
    r.wkey[slot_range, :] = nn(hm, r.w_writer_qkv[1]).astype(LOW)
    r.wvalue[slot_range, :] = nn(hm, r.w_writer_qkv[2]).astype(LOW)
    place_heads(r.wquery, nn(hm, r.w_writer_qkv[0]) * SCALE)
    loads["writer_out"].wait()
    mem_cot = r.mem_cot[rows_at(mine * slots, slots), :]
    place_heads(r.dmix, nt(mem_cot, r.w_writer_out[...]))

    def first(here, t):
        low, unit, inverse = norm_rows(r.x_all[here, :].astype(F32), gain(0))
        r.unit0[here, :] = unit
        r.inv0[here, :] = inverse
        r.h0[here, :] = low

    for k in range(3):
        gather_copy(r.x, r.x_all, r.xs, r.xr, k).wait()
    for k in range(3):
        gather_copy(r.out_cot, r.cot_all, r.cs, r.cr, k).start()
    tiles(SEG, TILE, first)
    loads["self_qkv"].wait()
    r.q[...] = (nn(r.h0[...], r.w_self_qkv[0]) * SCALE).astype(LOW)
    r.k[...] = nn(r.h0[...], r.w_self_qkv[1]).astype(LOW)
    r.v[...] = nn(r.h0[...], r.w_self_qkv[2]).astype(LOW)
    live = jnp.minimum(r.lengths[mine] - r.seg_index[mine] * SEG, SEG)

    def columns_of(p):
        return pl.ds(pl.multiple_of(p * 128, 128), 128)

    def attend(p):
        columns = columns_of(p)
        for i in range(BLOCKS):
            depth = 128 * (i + 1)
            here = slice(i * 128, (i + 1) * 128)
            stacked = head_stack(r.q[here, columns].astype(F32)).astype(LOW)
            r.query[p, i * 256 : (i + 1) * 256, :] = stacked
            scores = nt(r.k[:depth, columns], stacked)
            key_pos = lax.broadcasted_iota(jnp.int32, scores.shape, 0)
            query_pos = i * 128 + lax.rem(lax.broadcasted_iota(jnp.int32, scores.shape, 1), 128)
            scores = jnp.where((key_pos <= query_pos) & (key_pos < live), scores, SHUT)
            powers = jnp.exp(scores - jnp.max(scores, axis=0, keepdims=True))
            inverse = 1.0 / jnp.sum(powers, axis=0, keepdims=True)
            probs = (powers * inverse).astype(LOW)
            r.prob[p, BLOCK_ROWS[i] : BLOCK_ROWS[i + 1], :] = probs
            mixed = head_pick(tn(r.v[:depth, columns], probs))
            r.mix_t[p, here, :] = mixed
            r.mix[here, columns] = mixed.T.astype(LOW)

    each(PAIRS, attend)

    loads["self_out"].wait()
    r.acc[...] = nn(r.mix[...], r.w_self_out[...])

    def second(here, t):
        total = r.x_all[here, :].astype(F32) + r.acc[here, :]
        r.res[here, :] = total
        low, unit, inverse = norm_rows(total, gain(1))
        r.unit1[here, :] = unit
        r.inv1[here, :] = inverse
        r.h1[here, :] = low

    tiles(SEG, TILE, second)
    r.cq[...] = (nn(r.h1[...], r.w_cross_qkv[0]) * SCALE).astype(LOW)

    def cross(i):
        here = rows_at(i * 128, 128)
        for g in range(2):
            columns = slice(g * 256, (g + 1) * 256)
            scores = nt(r.cross_k[g], r.cq[here, columns]).reshape(4, slots, 128)
            powers = jnp.exp(scores - jnp.max(scores, axis=1, keepdims=True))
            inverse = 1.0 / jnp.sum(powers, axis=1, keepdims=True)
            probs = (powers * inverse).reshape(256, 128).astype(LOW)
            r.cross_p[2 * i + g] = probs
            r.co[here, columns] = tn(probs, r.cross_v[g]).astype(LOW)

    each(BLOCKS, cross)
    loads["cross_out"].wait()
    r.acc[...] = nn(r.co[...], r.w_cross_out[...])

    def third(here, t):
        total = r.res[here, :] + r.acc[here, :]
        r.res[here, :] = total
        low, unit, inverse = norm_rows(total, gain(2))
        r.unit2[here, :] = unit
        r.inv2[here, :] = inverse
        r.h2[here, :] = low

    tiles(SEG, TILE, third)

    rate, cube = 0.7978845608028654, 0.044715
    loads["ffn_in"].wait()
    loads["ffn_out"].wait()

    def feed(c):
        columns = pl.ds(pl.multiple_of(c * D, D), D)
        r.acc[...] = nn(r.h2[...], r.w_ffn_in[:, columns])

        def gelu(here, t):
            u = r.acc[here, :]
            square = u * u
            bend = jnp.tanh(rate * u * (1.0 + cube * square))
            half = 0.5 * (1.0 + bend)
            r.z[c, here, :] = (u * half).astype(LOW)
            slope = half + (0.5 * rate) * u * (1.0 - bend * bend) * (1.0 + 3.0 * cube * square)
            r.slope[c, here, :] = slope.astype(LOW)

        tiles(SEG, TILE, gelu)
        r.res[...] += nn(r.z[c], r.w_ffn_out[columns, :])

    each(4, feed)

    def fourth(here, t):
        total = r.res[here, :]
        r.enc[here, :] = total.astype(LOW)
        low, unit, inverse = norm_rows(total, gain(4))
        r.unit4[here, :] = unit
        r.inv4[here, :] = inverse
        r.src[here, :] = low

    tiles(SEG, TILE, fourth)
    enc_way = (r.enc, r.enc_out, rows, True, r.es, r.er)
    spread(*enc_way)

    written = r.src[:SEG, :]
    r.wkey[:SEG, :] = nn(written, r.w_writer_qkv[1]).astype(LOW)
    r.wvalue[:SEG, :] = nn(written, r.w_writer_qkv[2]).astype(LOW)
    for g in range(2):
        columns = slice(g * 256, (g + 1) * 256)
        scores = nt(r.wkey[:, columns], r.wquery[g])
        key_pos = lax.broadcasted_iota(jnp.int32, scores.shape, 0)
        scores = jnp.where((key_pos >= SEG) | (key_pos < live), scores, SHUT)
        powers = jnp.exp(scores - jnp.max(scores, axis=0, keepdims=True))
        probs = powers * (1.0 / jnp.sum(powers, axis=0, keepdims=True))
        probs_low = probs.astype(LOW)
        mixed = own_blocks(tn(r.wvalue[:, columns], probs_low)).astype(LOW).astype(F32)
        r.wo[:, columns] = swap(mixed).astype(LOW)
        dprobs = nt(r.wvalue[:, columns], r.dmix[g])
        delta = jnp.sum(probs * dprobs, axis=0, keepdims=True)
        slopes = (probs * (dprobs - delta)).astype(LOW)
        r.dkey[:, columns] = nn(slopes, r.wquery[g]).astype(LOW)
        r.dvalue[:, columns] = nn(probs_low, r.dmix[g]).astype(LOW)
        dquery = own_blocks(tn(slopes, r.wkey[:, columns])).astype(LOW).astype(F32)
        r.dwq[:, columns] = (dquery * SCALE).astype(LOW)

    r.new_memory[rows_at(mine * slots, slots), :] = (
        r.memory[rows_at(mine * slots, slots), :].astype(F32) + nn(r.wo[...], r.w_writer_out[...])
    ).astype(LOW)
    new_way = (r.new_memory, r.new_memory, slots, False, r.us, r.ur)
    spread(*new_way)

    def put(base, values):
        r.grad[base : base + D, :] = values.astype(LOW)

    r.acc[...] = nt(r.dkey[:SEG, :], r.w_writer_qkv[1]) + nt(r.dvalue[:SEG, :], r.w_writer_qkv[2])
    for k in range(3):
        gather_copy(r.out_cot, r.cot_all, r.cs, r.cr, k).wait()

    def fourth_back(here, t):
        grad, unit = r.acc[here, :], r.unit4[here, :]
        add_gain(4, grad * unit)
        total = r.cot_all[here, :].astype(F32) + norm_back(grad, unit, r.inv4[here, :], gain(4))
        r.res[here, :] = total
        r.low[here, :] = total.astype(LOW)

    tiles(SEG, TILE, fourth_back)
    put(GRAD["writer_qkv"], tn(hm, r.dwq[...]))
    put(GRAD["writer_qkv"] + D, tn(r.src[...], r.dkey[...]))
    put(GRAD["writer_qkv"] + 2 * D, tn(r.src[...], r.dvalue[...]))
    put(GRAD["writer_out"], tn(r.wo[...], mem_cot))

    def feed_back(c):
        columns = pl.ds(pl.multiple_of(c * D, D), D)
        r.unit4[...] = nt(r.low[...], r.w_ffn_out[columns, :])
        r.grad[pl.ds(pl.multiple_of(GRAD["ffn_out"] + c * D, D), D), :] = tn(r.z[c], r.low[...]).astype(LOW)

        def bent(here, t):
            r.z[c, here, :] = (r.unit4[here, :] * r.slope[c, here, :].astype(F32)).astype(LOW)

        tiles(SEG, TILE, bent)
        du = r.z[c]
        r.grad[pl.ds(pl.multiple_of(GRAD["ffn_in"] + c * D, D), D), :] = tn(r.h2[...], du).astype(LOW)
        back = nt(du, r.w_ffn_in[:, columns])

        @pl.when(c == 0)
        def _():
            r.acc[...] = back

        @pl.when(c > 0)
        def _():
            r.acc[...] += back

    each(4, feed_back)

    def third_back(here, t):
        grad, unit = r.acc[here, :], r.unit2[here, :]
        add_gain(2, grad * unit)
        total = r.res[here, :] + norm_back(grad, unit, r.inv2[here, :], gain(2))
        r.res[here, :] = total
        r.low[here, :] = total.astype(LOW)

    tiles(SEG, TILE, third_back)

    r.dsend[...] = nt(r.low[...], r.w_cross_out[...]).astype(LOW)
    put(GRAD["cross_out"], tn(r.co[...], r.low[...]))
    r.cross_dk[...] = jnp.zeros_like(r.cross_dk)
    r.cross_dv[...] = jnp.zeros_like(r.cross_dv)

    def cross_back(i):
        here = rows_at(i * 128, 128)
        for g in range(2):
            columns = slice(g * 256, (g + 1) * 256)
            dmix = r.dsend[here, columns]
            dprobs = nt(r.cross_v[g], dmix)
            probs = r.cross_p[2 * i + g].astype(F32)
            delta = jnp.sum((probs * dprobs).reshape(4, slots, 128), axis=1, keepdims=True)
            slopes = (probs * (dprobs.reshape(4, slots, 128) - delta).reshape(256, 128)).astype(LOW)
            r.dcq[here, columns] = (
                tn(slopes, r.cross_k[g]).astype(LOW).astype(F32) * SCALE
            ).astype(LOW)
            r.cross_dk[g] += nn(slopes, r.cq[here, columns])
            r.cross_dv[g] += nn(r.cross_p[2 * i + g], dmix)

    each(BLOCKS, cross_back)
    for g in range(2):
        columns = slice(g * 256, (g + 1) * 256)
        r.dck[:, columns] = own_blocks(r.cross_dk[g]).astype(LOW)
        r.dcv[:, columns] = own_blocks(r.cross_dv[g]).astype(LOW)
    r.acc[...] = nt(r.dcq[...], r.w_cross_qkv[0])

    def second_back(here, t):
        grad, unit = r.acc[here, :], r.unit1[here, :]
        add_gain(1, grad * unit)
        total = r.res[here, :] + norm_back(grad, unit, r.inv1[here, :], gain(1))
        r.res[here, :] = total
        r.low[here, :] = total.astype(LOW)

    tiles(SEG, TILE, second_back)
    put(GRAD["cross_qkv"], tn(r.h1[...], r.dcq[...]))
    put(GRAD["cross_qkv"] + D, tn(hm, r.dck[...]))
    put(GRAD["cross_qkv"] + 2 * D, tn(hm, r.dcv[...]))

    r.dsend[...] = nt(r.low[...], r.w_self_out[...]).astype(LOW)
    put(GRAD["self_out"], tn(r.mix[...], r.low[...]))

    def attend_back(p):
        columns = columns_of(p)
        r.dk_sum[...] = jnp.zeros_like(r.dk_sum)
        r.dv_sum[...] = jnp.zeros_like(r.dv_sum)
        for i in range(BLOCKS):
            depth = 128 * (i + 1)
            here = slice(i * 128, (i + 1) * 128)
            dmix = r.dsend[here, columns].astype(F32)
            stacked = head_stack(dmix).astype(LOW)
            queries = r.query[p, i * 256 : (i + 1) * 256, :]
            product = dmix.T * r.mix_t[p, here, :]
            delta = jnp.concatenate(
                [
                    jnp.sum(product[:HD], axis=0, keepdims=True),
                    jnp.sum(product[HD:], axis=0, keepdims=True),
                ],
                axis=1,
            )
            probs = r.prob[p, BLOCK_ROWS[i] : BLOCK_ROWS[i + 1], :]
            dprobs = nt(r.v[:depth, columns], stacked)
            slopes = (probs.astype(F32) * (dprobs - delta)).astype(LOW)
            r.dk_sum[:depth, :] += nn(slopes, queries)
            r.dv_sum[:depth, :] += nn(probs, stacked)
            dquery = head_pick(tn(r.k[:depth, columns], slopes)).T
            r.dq[here, columns] = (dquery.astype(LOW).astype(F32) * SCALE).astype(LOW)
        r.dk[:, columns] = r.dk_sum[...].astype(LOW)
        r.dv[:, columns] = r.dv_sum[...].astype(LOW)

    each(PAIRS, attend_back)
    for k, grad in enumerate((r.dq, r.dk, r.dv)):
        put(GRAD["self_qkv"] + k * D, tn(r.h0[...], grad[...]))
    r.acc[...] = (
        nt(r.dq[...], r.w_self_qkv[0]) + nt(r.dk[...], r.w_self_qkv[1]) + nt(r.dv[...], r.w_self_qkv[2])
    )

    def first_back(here, t):
        grad, unit = r.acc[here, :], r.unit0[here, :]
        add_gain(0, grad * unit)
        total = r.res[here, :] + norm_back(grad, unit, r.inv0[here, :], gain(0))
        r.in_grad[here, :] = total.astype(LOW)

    tiles(SEG, TILE, first_back)
    grad_way = (r.in_grad, r.in_grad_all, rows, True, r.gs, r.gr)
    spread(*grad_way)

    dhm = (
        nt(r.dwq[...], r.w_writer_qkv[0])
        + nt(r.dkey[slot_range, :], r.w_writer_qkv[1])
        + nt(r.dvalue[slot_range, :], r.w_writer_qkv[2])
        + nt(r.dck[...], r.w_cross_qkv[1])
        + nt(r.dcv[...], r.w_cross_qkv[2])
    )
    unit = r.unit3[...]
    add_gain(3, dhm * unit)
    r.slot_grad_all[rows_at(mine * slots, slots), :] = (
        mem_cot.astype(F32) + norm_back(dhm, unit, r.inv3[...], gain(3))
    ).astype(LOW)
    slot_way = (r.slot_grad_all, r.slot_grad_all, slots, False, r.ms, r.mr)
    spread(*slot_way)
    r.grad[GRAD["gains"] :, :] = jnp.zeros((GRAD_ROWS - GRAD["gains"], D), LOW)
    r.grad[GRAD["gains"] : GRAD["gains"] + 16, :] = jnp.concatenate(
        [jnp.sum(r.gain_sum[k], axis=0, keepdims=True) for k in range(5)] + [jnp.zeros((11, D), F32)], axis=0
    ).astype(LOW)
    store = pltpu.make_async_copy(r.grad, r.grads, r.out_sem.at[0])
    store.start()
    spread_wait(*enc_way)
    spread_wait(*new_way)
    spread_wait(*grad_way)
    spread_wait(*slot_way)
    here = rows_at(mine * rows, rows)
    r.enc_out[here, :] = r.enc[own_rows, :]
    r.in_grad_all[here, :] = r.in_grad[own_rows, :]
    r.input_grad[...] = r.in_grad_all[...].astype(F32)
    r.memory_grad[...] = r.slot_grad_all[...].astype(F32)
    store.wait()


def on_device(*arguments):
    seg_input, memory = arguments[0], arguments[1]
    docs, rows, _ = seg_input.shape
    slots = memory.shape[1]
    scratch = scratch_of(docs, rows, slots, dict(zip(INPUTS, arguments)))
    vmem, smem, anywhere = (pl.BlockSpec(memory_space=m) for m in (pltpu.VMEM, pltpu.SMEM, pl.ANY))
    arguments = list(arguments)
    for k in (0, 1, 13, 14):
        arguments[k] = arguments[k].reshape(-1, D)
    names = INPUTS + OUTPUTS + tuple(scratch)
    encoded, updated, input_grad, memory_grad, flat = pl.pallas_call(
        functools.partial(layer_kernel, docs, rows, slots, names),
        out_shape=(
            jax.ShapeDtypeStruct((docs * rows, D), LOW),
            jax.ShapeDtypeStruct((docs * slots, D), LOW),
            jax.ShapeDtypeStruct((docs * rows, D), F32),
            jax.ShapeDtypeStruct((docs * slots, D), F32),
            jax.ShapeDtypeStruct((GRAD_ROWS, D), LOW),
        ),
        in_specs=[
            smem if name in ("lengths", "seg_index") else anywhere if name in WEIGHTS else vmem for name in INPUTS
        ],
        out_specs=(vmem, vmem, vmem, vmem, anywhere),
        scratch_shapes=list(scratch.values()),
        compiler_params=pltpu.CompilerParams(
            collective_id=1, has_side_effects=True, vmem_limit_bytes=60 << 20
        ),
    )(*arguments)
    summed = reduce_weights(flat, lax.axis_size("docs")).astype(F32)
    return (
        encoded.reshape(docs, rows, D),
        updated.reshape(docs, slots, D),
        input_grad.reshape(docs, rows, D),
        memory_grad.reshape(docs, slots, D),
        summed[0:1536].reshape(3, D, D),
        summed[1536:2048],
        summed[2048:3584].reshape(3, D, D),
        summed[3584:4096],
        jnp.concatenate([summed[4096 + c * D : 4096 + (c + 1) * D] for c in range(4)], axis=1),
        summed[6144:8192],
        summed[8192:9728].reshape(3, D, D),
        summed[9728:10240],
        summed[10240:10245],
    )


def solution(mesh):
    row, slot, whole = P("docs", "seq", None), P("docs", None, None), P()
    return jax.shard_map(
        on_device,
        mesh=mesh,
        in_specs=(row, slot, P("docs"), P("docs")) + (whole,) * 9 + (row, slot),
        out_specs=(row, slot, row, slot) + (whole,) * 9,
        check_vma=False,
    )
```

```python
import functools
import types

import jax
import jax.numpy as jnp
from jax import lax
from jax.experimental import pallas as pl
from jax.experimental.pallas import tpu as pltpu
from jax.sharding import PartitionSpec as P

MESH = pl.DeviceIdType.MESH
F32, LOW = jnp.float32, jnp.bfloat16
VMEM_BYTES = 63 << 20
D = 512
HD = 64
SEG = 512
SHUT = -1e30
SCALE = HD ** (-0.5)

CORE, X, Y, Z0, Z1 = ("seq", 1), ("seq", 2), ("docs", 1), ("docs", 2), ("docs", 4)
ORDERS = dict(
    X=(CORE, X, Y, Z0, Z1), Y=(CORE, Y, X, Z0, Z1), Z=(CORE, Z0, Z1, X, Y), U=(CORE, Y, Z0, Z1, X),
    V=(CORE, X, Z0, Z1, Y), T=(CORE, Z0, Z1, Y, X), A=(CORE, Z0, X, Y, Z1), B=(CORE, Z0, Y, X, Z1),
)
UNITS = {
    "W1": (0, 1024, "Y"),
    "W0": (1024, 1024, "Y"),
    "F00": (2048, 512, "V"),
    "F01": (2560, 512, "X"),
    "F10": (3072, 1024, "X"),
    "F20": (4096, 1024, "A"),
    "F31": (5120, 512, "X"),
    "F30": (5632, 512, "B"),
    "X0": (6144, 512, "U"),
    "X2": (6656, 1024, "Y"),
    "X1": (7680, 512, "V"),
    "S0": (8192, 512, "B"),
    "Q0": (8704, 1024, "X"),
    "Q1": (9728, 512, "Y"),
}
SCHEDULE = (
    ("W1", "W0",),
    (),
    ("F00", "F01", "W1",),
    ("W0",),
    ("F10", "F00", "F01",),
    (),
    ("F20", "F10",),
    (),
    ("F31", "F30", "F20", "F00", "W1",),
    ("F31",),
    ("F30", "F01",),
    (),
    ("W0", "F01",),
    ("X0", "X2", "X1", "F20", "F10",),
    ("S0", "F00",),
    ("X0", "W1",),
    ("X2", "F30", "X1", "F01", "S0",),
    ("F31", "F10", "F00",),
    ("W1",),
    ("W0", "F01", "X0",),
    (),
    ("S0", "F20",),
    ("F10",),
    ("Q0", "Q1", "W1", "W0", "X1", "X2",),
    ("F01", "X0", "F30", "Q0",),
    ("F10", "Q1", "F31", "F00", "W1", "S0", "X1",),
    (
        "gains", "X2", "W0", "F01", "F20", "F30", "X0", "F31", "F10", "W1", "Q1", "gains", "F00", "X1",
        "F01", "X2", "Q0", "S0", "W0", "X0", "X1", "F20", "gains", "F30", "F31", "F10", "W1", "F00", "X2",
        "Q0", "Q1", "X1", "S0", "gains", "W0", "F20", "F30", "F01", "F10", "X0", "F31", "F00", "F01", "X2",
        "gains", "Q0", "W0", "Q1", "F30", "X1", "S0", "W1", "X0", "F31", "F20", "gains", "X2", "W1", "Q0",
        "Q1", "F10", "X1", "X0", "F10", "F00", "W0", "S0", "Q0", "Q1", "F00", "F30", "W0", "F31", "F20",
        "Q0", "Q1", "X0", "X2", "S0", "X0", "F30", "X1", "F30", "Q0", "X1", "F31", "Q1", "F20", "F31", "X2",
        "F20", "S0", "X2", "Q1", "Q0", "S0", "Q1", "Q0",
    ),
)
GROUP = 8


def place_of(stage):
    axis, stride = stage
    index = lax.axis_index(axis)
    bit = lax.rem(lax.div(index, stride), 2)
    return bit, {axis: index + stride * (1 - 2 * bit)}


def outer_partners(docs_count):
    index = lax.axis_index("docs")
    return [{"docs": lax.rem(index + GROUP * k, docs_count)} for k in range(1, docs_count // GROUP)]


def partners_of(docs_count):
    return [place_of(stage)[1] for stage in ORDERS["X"]] + outer_partners(docs_count)


BLOCK = dict(
    writer_qkv=0, writer_out=3, ffn=4, cross_out=12, cross_qkv=13, self_out=16, self_qkv=17,
)
GRAD_ROWS = 20 * 512
STAGES = 5


class Summer:
    def __init__(self, r, docs_count, share):
        self.r, self.share, self.docs_count = r, share, docs_count
        self.index = {name: k for k, name in enumerate(UNITS)}
        self.at = {}

    def remote(self, source, target, sems, name, j, partner):
        k = self.index.get(name, 0)
        return pltpu.make_async_remote_copy(
            src_ref=source, dst_ref=target, send_sem=sems[0].at[k, j], recv_sem=sems[1].at[k, j],
            device_id=partner, device_id_type=MESH,
        )

    def give(self, name, j, start, size):
        r = self.r
        base, rows, order = UNITS[name]
        bit, partner = place_of(ORDERS[order][j])
        half = size // 2
        first = base + rows - size
        copy = self.remote(
            r.grad.at[rows_at(start + (1 - bit) * half, half)], r.landed.at[pl.ds(first, half)],
            (r.rs, r.rr), name, j, partner,
        )
        copy.start()
        self.at[name] = ("give", j, copy, start + bit * half, half, first)

    def spread(self, name, j, start, size):
        r = self.r
        bit, partner = place_of(ORDERS[UNITS[name][2]][j])
        here = rows_at(start, size)
        source = r.grad if j == STAGES - 1 else r.grads
        copy = self.remote(source.at[here], r.grads.at[here], (r.as_, r.ar), name, j, partner)
        copy.start()
        self.at[name] = ("spread", j, copy, start - bit * size, 2 * size, None)

    def own(self, name, start, size):
        here = rows_at(start, size)
        return pltpu.make_async_copy(
            self.r.grad.at[here], self.r.grads.at[here], self.r.own_sem.at[self.index[name]]
        )

    def step(self, name):
        r = self.r
        if name == "gains":
            return self.step_gains()
        if name not in self.at:
            base, rows, order = UNITS[name]
            return self.give(name, 0, base, rows)
        kind, j, copy, start, size, first = self.at[name]
        copy.wait()
        if kind == "give":
            add_rows(r.grad, start, size, r.landed, first, self.share if j == 0 else None)
            if j + 1 < STAGES:
                return self.give(name, j + 1, start, size)
            self.outer(name, start, size)
            store = self.own(name, start, size)
            store.start()
            self.spread(name, j, start, size)
            self.store = getattr(self, "store", {})
            self.store[name] = store
        else:
            if j == STAGES - 1:
                self.store[name].wait()
            if j > 0:
                self.spread(name, j - 1, start, size)
            else:
                self.at[name] = None

    def outer(self, name, start, size):
        others = outer_partners(self.docs_count)
        if not others:
            return
        r = self.r
        mine = lax.div(lax.axis_index("docs"), GROUP)
        here = rows_at(start, size)
        share = pl.ds(UNITS[name][0] // 32, size)
        r.outer[mine, share, :] = r.grad[here, :]
        copies = [
            self.remote(r.grad.at[here], r.outer.at[mine, share], (r.outer_s, r.outer_r), name, k, partner)
            for k, partner in enumerate(others)
        ]
        for copy in copies:
            copy.start()
        for copy in copies:
            copy.wait()
        parts = [r.outer[k, share, :].astype(F32) for k in range(len(others) + 1)]
        r.grad[here, :] = sum(parts).astype(LOW)

    def step_gains(self):
        r = self.r
        j = self.at.get("gains", 0)
        if j > 0:
            self.gain_copy(j - 1).wait()
            more = r.gain_landed[j - 1]
            if j == 1:
                more = more * self.share
            r.gain_steps[j] = r.gain_steps[j - 1] + more
        if j < STAGES:
            self.gain_copy(j).start()
        else:
            others = outer_partners(self.docs_count)
            if others:
                mine = lax.div(lax.axis_index("docs"), GROUP)
                r.gain_outer[mine] = r.gain_steps[j]
                copies = [
                    self.remote(
                        r.gain_steps.at[j], r.gain_outer.at[mine], (r.gain_os, r.gain_or), "gains", k, partner
                    )
                    for k, partner in enumerate(others)
                ]
                for copy in copies:
                    copy.start()
                for copy in copies:
                    copy.wait()
                r.gain_steps[j] = sum(r.gain_outer[k] for k in range(len(others) + 1))
        self.at["gains"] = j + 1

    def gain_copy(self, j):
        r = self.r
        partner = place_of(ORDERS["X"][j])[1]
        return self.remote(r.gain_steps.at[j], r.gain_landed.at[j], (r.gain_s, r.gain_r), "gains", j, partner)


def add_rows(total, start, rows, landed, first, share=None):
    tile = min(rows, 64)

    def turn(t, carry):
        here = rows_at(start + t * tile, tile)
        more = landed[rows_at(first + t * tile, tile), :].astype(F32)
        if share is not None:
            more = more * share
        total[here, :] = (total[here, :].astype(F32) + more).astype(total.dtype)
        return carry

    lax.fori_loop(0, rows // tile, turn, 0)


def dot(left, right, left_dim, right_dim):
    return lax.dot_general(
        left, right, (((left_dim,), (right_dim,)), ((), ())), preferred_element_type=F32
    )


def nn(left, right):
    return dot(left, right, 1, 0)


def nt(left, right):
    return dot(left, right, 1, 1)


def tn(left, right):
    return dot(left, right, 0, 0)


def tiles(rows, tile, body):
    def turn(t, carry):
        body(pl.ds(pl.multiple_of(t * tile, tile), tile), t)
        return carry

    lax.fori_loop(0, rows // tile, turn, 0)


def each(count, body):
    def turn(k, carry):
        body(k)
        return carry

    lax.fori_loop(0, count, turn, 0)


def rows_at(start, size):
    return pl.ds(pl.multiple_of(start, 16), size)


def norm_rows(values, gain_row):
    centered = values - jnp.mean(values, axis=-1, keepdims=True)
    inverse = lax.rsqrt(jnp.mean(centered * centered, axis=-1, keepdims=True) + 1e-05)
    unit = centered * inverse
    return (unit * gain_row).astype(LOW), unit, inverse


def norm_back(grad, unit, inverse, gain_row):
    scaled = grad * gain_row
    adjusted = (
        scaled
        - jnp.mean(scaled, axis=-1, keepdims=True)
        - unit * jnp.mean(scaled * unit, axis=-1, keepdims=True)
    )
    return adjusted * inverse


def same_head():
    left = lax.div(lax.broadcasted_iota(jnp.int32, (256, 256), 0), HD)
    right = lax.div(lax.broadcasted_iota(jnp.int32, (256, 256), 1), HD)
    return left == right


def four_heads(values):
    return jnp.where(same_head(), jnp.concatenate([values] * 4, axis=0), 0.0)


def own_blocks(values):
    return jnp.sum(jnp.where(same_head(), values, 0.0).reshape(4, HD, 256), axis=0)


def swap(values):
    return own_blocks(four_heads(values).T)


def head_stack(values):
    low_half = lax.broadcasted_iota(jnp.int32, values.shape, 1) < HD
    return jnp.concatenate(
        [jnp.where(low_half, values, 0.0), jnp.where(low_half, 0.0, values)], axis=0
    )


def head_pick(values):
    low_half = lax.broadcasted_iota(jnp.int32, (128, 128), 0) < HD
    return jnp.where(low_half, values[:, :128], values[:, 128:])


BLOCKS = SEG // 128
BLOCK_ROWS = [sum(128 * (k + 1) for k in range(i)) for i in range(BLOCKS + 1)]
PAIRS = D // 128
TILE = 64

WEIGHTS = (
    "self_qkv", "cross_qkv", "writer_qkv", "writer_out", "self_out", "cross_out", "ffn_in", "ffn_out",
)
INPUTS = (
    "x", "memory", "lengths", "seg_index", "self_qkv", "self_out", "cross_qkv", "cross_out",
    "ffn_in", "ffn_out", "writer_qkv", "writer_out", "gains", "out_cot", "mem_cot",
)
OUTPUTS = ("enc_out", "new_memory", "input_grad", "memory_grad", "grads", "gains_grad")
def scratch_of(docs, rows, slots, weights, docs_count):
    keys = SEG + slots
    units, outers = len(UNITS), max(1, docs_count // GROUP)
    dma = pltpu.SemaphoreType.DMA
    low = lambda *shape: pltpu.VMEM(shape, LOW)
    full = lambda *shape: pltpu.VMEM(shape, F32)
    fetched = {"w_" + name: pltpu.VMEM(weights[name].shape, LOW) for name in WEIGHTS}
    return dict(
        **fetched,
        x_all=low(SEG, D),
        cot_all=low(SEG, D),
        enc=low(SEG, D),
        slot_grad=low(slots, D),
        new_slots=low(slots, D),
        unit0=full(SEG, D),
        unit1=full(SEG, D),
        unit2=full(SEG, D),
        unit4=full(SEG, D),
        unit3=full(slots, D),
        inv0=full(SEG, 1),
        inv1=full(SEG, 1),
        inv2=full(SEG, 1),
        inv4=full(SEG, 1),
        inv3=full(slots, 1),
        h0=low(SEG, D),
        h1=low(SEG, D),
        h2=low(SEG, D),
        src=low(keys, D),
        q=low(SEG, D),
        k=low(SEG, D),
        v=low(SEG, D),
        prob=low(PAIRS, BLOCK_ROWS[-1], 256),
        mix=low(SEG, D),
        acc=full(SEG, D),
        res=full(SEG, D),
        cq=low(SEG, D),
        cross_k=low(2, 256, 256),
        cross_v=low(2, 256, 256),
        cross_p=low(2 * BLOCKS, 256, 128),
        cross_dk=full(2, 256, 256),
        cross_dv=full(2, 256, 256),
        co=low(SEG, D),
        z=low(4, SEG, D),
        slope=low(4, SEG, D),
        wkey=low(keys, D),
        wvalue=low(keys, D),
        wquery=low(2, 256, 256),
        dmix=low(2, 256, 256),
        wo=low(slots, D),
        dwq=low(slots, D),
        dck=low(slots, D),
        dcv=low(slots, D),
        low=low(SEG, D),
        dsend=low(SEG, D),
        dk_sum=full(SEG, 128),
        dv_sum=full(SEG, 128),
        gain_sum=full(5, 8, D),
        gain_steps=full(STAGES + 1, 8, D),
        gain_landed=full(STAGES, 8, D),
        gain_outer=full(outers, 8, D),
        grad=low(GRAD_ROWS, D),
        landed=low(GRAD_ROWS, D),
        outer=low(outers, GRAD_ROWS // 32, D),
        rs=dma((units, STAGES)),
        rr=dma((units, STAGES)),
        as_=dma((units, STAGES)),
        ar=dma((units, STAGES)),
        own_sem=dma((units,)),
        outer_s=dma((units, outers)),
        outer_r=dma((units, outers)),
        gain_s=dma((1, STAGES)),
        gain_r=dma((1, STAGES)),
        gain_os=dma((1, outers)),
        gain_or=dma((1, outers)),
        load_sem=dma((len(WEIGHTS),)),
        xs=dma((3,)),
        xr=dma((3,)),
        cs=dma((3,)),
        cr=dma((3,)),
        es=dma((3,)),
        er=dma((3,)),
        us=dma((3,)),
        ur=dma((3,)),
        gs=dma((3,)),
        gr=dma((3,)),
        ms=dma((3,)),
        mr=dma((3,)),
        out_sem=dma((5,)),
    )


def layer_kernel(docs, rows, slots, docs_count, names, *refs):
    r = types.SimpleNamespace(**dict(zip(names, refs)))
    s = lax.axis_index("seq")
    bit0, bit1 = lax.rem(s, 2), lax.div(s, 2)
    near = s + 1 - 2 * bit0
    far = s + 2 - 4 * bit1
    across = near + 2 - 4 * bit1
    peers = (near, far, across)

    def doc_of(index):
        return jnp.minimum(index, docs - 1)

    mine = doc_of(s)

    def remote(source, target, send_sem, recv_sem, to):
        return pltpu.make_async_remote_copy(
            src_ref=source, dst_ref=target, send_sem=send_sem, recv_sem=recv_sem,
            device_id={"seq": to}, device_id_type=MESH,
        )

    def gain(k):
        return r.gains[k : k + 1, :]

    def add_gain(k, values):
        r.gain_sum[k] += jnp.sum(values.reshape(-1, 8, D), axis=0)

    loads = {}
    for k, name in enumerate(WEIGHTS):
        loads[name] = pltpu.make_async_copy(getattr(r, name), getattr(r, "w_" + name), r.load_sem.at[k])
        loads[name].start()
    barrier = pltpu.get_barrier_semaphore()
    greeted = [{"seq": across}] + partners_of(docs_count)
    for partner in greeted:
        pl.semaphore_signal(barrier, inc=1, device_id=partner, device_id_type=MESH)
    r.gain_sum[...] = jnp.zeros_like(r.gain_sum)

    def slot_norm(here, t):
        low, unit, inverse = norm_rows(
            r.memory[rows_at(mine * slots + t * TILE, TILE), :].astype(F32), gain(3)
        )
        r.unit3[here, :] = unit
        r.inv3[here, :] = inverse
        r.src[rows_at(SEG + t * TILE, TILE), :] = low

    tiles(slots, TILE, slot_norm)
    pl.semaphore_wait(barrier, len(greeted))

    def gather_copy(source, target, send_sem, recv_sem, k):
        return remote(
            source.at[rows_at(doc_of(peers[k]) * rows, rows)],
            target.at[rows_at(s * rows, rows)], send_sem.at[k], recv_sem.at[k], peers[k],
        )

    for k in range(3):
        gather_copy(r.x, r.x_all, r.xs, r.xr, k).start()
    own_rows = rows_at(s * rows, rows)
    r.x_all[own_rows, :] = r.x[rows_at(mine * rows, rows), :]
    r.cot_all[own_rows, :] = r.out_cot[rows_at(mine * rows, rows), :]

    def spread_copy(source, target, size, own, send_sem, recv_sem, k):
        piece = source.at[rows_at(peers[k] * size, size)] if own else source
        return remote(
            piece, target.at[rows_at(mine * size, size)], send_sem.at[k], recv_sem.at[k], peers[k]
        )

    def keep_copy(k, source, target, size, own, *sems):
        piece = source.at[rows_at(s * size, size)] if own else source
        return pltpu.make_async_copy(piece, target.at[rows_at(mine * size, size)], r.out_sem.at[k])

    summer = Summer(r, docs_count, 1.0 - bit1.astype(F32))
    ticks = iter(SCHEDULE)

    def tick():
        for name in next(ticks):
            summer.step(name)

    def spread(*where):
        spread_copy(*where, 1).start()

        @pl.when(bit1 == 0)
        def _():
            spread_copy(*where, 0).start()
            spread_copy(*where, 2).start()

    def spread_wait(*where):
        spread_copy(*where, 1).wait()

        @pl.when(bit1 == 0)
        def _():
            spread_copy(*where, 0).wait()
            spread_copy(*where, 2).wait_send()

        @pl.when(bit1 == 1)
        def _():
            spread_copy(*where, 2).wait_recv()

    slot_range = pl.ds(SEG, slots)
    hm = r.src[slot_range, :]

    def place_heads(target, values):
        for g in range(2):
            piece = values[:, g * 256 : (g + 1) * 256].astype(LOW).astype(F32)
            target[g] = four_heads(piece).astype(LOW)

    loads["cross_qkv"].wait()
    place_heads(r.cross_k, nn(hm, r.w_cross_qkv[1]))
    place_heads(r.cross_v, nn(hm, r.w_cross_qkv[2]))
    loads["writer_qkv"].wait()
    r.wkey[slot_range, :] = nn(hm, r.w_writer_qkv[1]).astype(LOW)
    r.wvalue[slot_range, :] = nn(hm, r.w_writer_qkv[2]).astype(LOW)
    place_heads(r.wquery, nn(hm, r.w_writer_qkv[0]) * SCALE)
    loads["writer_out"].wait()
    mem_cot = r.mem_cot[rows_at(mine * slots, slots), :]
    place_heads(r.dmix, nt(mem_cot, r.w_writer_out[...]))

    def first(here, t):
        low, unit, inverse = norm_rows(r.x_all[here, :].astype(F32), gain(0))
        r.unit0[here, :] = unit
        r.inv0[here, :] = inverse
        r.h0[here, :] = low

    for k in range(3):
        gather_copy(r.x, r.x_all, r.xs, r.xr, k).wait()
    for k in range(3):
        gather_copy(r.out_cot, r.cot_all, r.cs, r.cr, k).start()
    tiles(SEG, TILE, first)
    loads["self_qkv"].wait()
    r.q[...] = (nn(r.h0[...], r.w_self_qkv[0]) * SCALE).astype(LOW)
    r.k[...] = nn(r.h0[...], r.w_self_qkv[1]).astype(LOW)
    r.v[...] = nn(r.h0[...], r.w_self_qkv[2]).astype(LOW)
    live = jnp.minimum(r.lengths[mine] - r.seg_index[mine] * SEG, SEG)

    def columns_of(p):
        return pl.ds(pl.multiple_of(p * 128, 128), 128)

    def attend(p):
        columns = columns_of(p)
        for i in range(BLOCKS):
            depth = 128 * (i + 1)
            here = slice(i * 128, (i + 1) * 128)
            stacked = head_stack(r.q[here, columns].astype(F32)).astype(LOW)
            scores = nt(r.k[:depth, columns], stacked)
            key_pos = lax.broadcasted_iota(jnp.int32, scores.shape, 0)
            query_pos = i * 128 + lax.rem(lax.broadcasted_iota(jnp.int32, scores.shape, 1), 128)
            scores = jnp.where((key_pos <= query_pos) & (key_pos < live), scores, SHUT)
            powers = jnp.exp(scores - jnp.max(scores, axis=0, keepdims=True))
            inverse = 1.0 / jnp.sum(powers, axis=0, keepdims=True)
            probs = (powers * inverse).astype(LOW)
            r.prob[p, BLOCK_ROWS[i] : BLOCK_ROWS[i + 1], :] = probs
            mixed = head_pick(tn(r.v[:depth, columns], probs))
            r.mix[here, columns] = mixed.T.astype(LOW)

    each(PAIRS, attend)

    loads["self_out"].wait()
    r.acc[...] = nn(r.mix[...], r.w_self_out[...])

    def second(here, t):
        total = r.x_all[here, :].astype(F32) + r.acc[here, :]
        r.res[here, :] = total
        low, unit, inverse = norm_rows(total, gain(1))
        r.unit1[here, :] = unit
        r.inv1[here, :] = inverse
        r.h1[here, :] = low

    tiles(SEG, TILE, second)
    r.cq[...] = (nn(r.h1[...], r.w_cross_qkv[0]) * SCALE).astype(LOW)

    def cross(i):
        here = rows_at(i * 128, 128)
        for g in range(2):
            columns = slice(g * 256, (g + 1) * 256)
            scores = nt(r.cross_k[g], r.cq[here, columns]).reshape(4, slots, 128)
            powers = jnp.exp(scores - jnp.max(scores, axis=1, keepdims=True))
            inverse = 1.0 / jnp.sum(powers, axis=1, keepdims=True)
            probs = (powers * inverse).reshape(256, 128).astype(LOW)
            r.cross_p[2 * i + g] = probs
            r.co[here, columns] = tn(probs, r.cross_v[g]).astype(LOW)

    each(BLOCKS, cross)
    loads["cross_out"].wait()
    r.acc[...] = nn(r.co[...], r.w_cross_out[...])

    def third(here, t):
        total = r.res[here, :] + r.acc[here, :]
        r.res[here, :] = total
        low, unit, inverse = norm_rows(total, gain(2))
        r.unit2[here, :] = unit
        r.inv2[here, :] = inverse
        r.h2[here, :] = low

    tiles(SEG, TILE, third)

    rate, cube = 0.7978845608028654, 0.044715
    loads["ffn_in"].wait()
    loads["ffn_out"].wait()

    def feed(c):
        columns = pl.ds(pl.multiple_of(c * D, D), D)
        r.acc[...] = nn(r.h2[...], r.w_ffn_in[:, columns])

        def gelu(here, t):
            u = r.acc[here, :]
            square = u * u
            bend = jnp.tanh(rate * u * (1.0 + cube * square))
            half = 0.5 * (1.0 + bend)
            r.z[c, here, :] = (u * half).astype(LOW)
            slope = half + (0.5 * rate) * u * (1.0 - bend * bend) * (1.0 + 3.0 * cube * square)
            r.slope[c, here, :] = slope.astype(LOW)

        tiles(SEG, TILE, gelu)
        r.res[...] += nn(r.z[c], r.w_ffn_out[columns, :])

    each(4, feed)

    def fourth(here, t):
        total = r.res[here, :]
        r.enc[here, :] = total.astype(LOW)
        low, unit, inverse = norm_rows(total, gain(4))
        r.unit4[here, :] = unit
        r.inv4[here, :] = inverse
        r.src[here, :] = low

    tiles(SEG, TILE, fourth)
    enc_way = (r.enc, r.enc_out, rows, True, r.es, r.er)
    spread(*enc_way)
    keep_copy(0, *enc_way).start()

    written = r.src[:SEG, :]
    r.wkey[:SEG, :] = nn(written, r.w_writer_qkv[1]).astype(LOW)
    r.wvalue[:SEG, :] = nn(written, r.w_writer_qkv[2]).astype(LOW)
    for g in range(2):
        columns = slice(g * 256, (g + 1) * 256)
        keys = r.wkey[:, columns]
        scores = nt(keys, r.wquery[g])
        key_pos = lax.broadcasted_iota(jnp.int32, scores.shape, 0)
        scores = jnp.where((key_pos >= SEG) | (key_pos < live), scores, SHUT)
        powers = jnp.exp(scores - jnp.max(scores, axis=0, keepdims=True))
        probs = powers * (1.0 / jnp.sum(powers, axis=0, keepdims=True))
        probs_low = probs.astype(LOW)
        mixed = own_blocks(tn(r.wvalue[:, columns], probs_low)).astype(LOW).astype(F32)
        r.wo[:, columns] = swap(mixed).astype(LOW)
        dprobs = nt(r.wvalue[:, columns], r.dmix[g])
        delta = jnp.sum(probs * dprobs, axis=0, keepdims=True)
        slopes = (probs * (dprobs - delta)).astype(LOW)
        dquery = own_blocks(tn(slopes, keys)).astype(LOW).astype(F32)
        r.dwq[:, columns] = (dquery * SCALE).astype(LOW)
        r.wkey[:, columns] = nn(slopes, r.wquery[g]).astype(LOW)
        r.wvalue[:, columns] = nn(probs_low, r.dmix[g]).astype(LOW)

    r.new_slots[...] = (
        r.memory[rows_at(mine * slots, slots), :].astype(F32) + nn(r.wo[...], r.w_writer_out[...])
    ).astype(LOW)
    new_way = (r.new_slots, r.new_memory, slots, False, r.us, r.ur)
    spread(*new_way)
    keep_copy(1, *new_way).start()

    def put(block, values):
        r.grad[block * D : (block + 1) * D, :] = values.astype(LOW)

    r.acc[...] = nt(r.wkey[:SEG, :], r.w_writer_qkv[1]) + nt(r.wvalue[:SEG, :], r.w_writer_qkv[2])
    for k in range(3):
        gather_copy(r.out_cot, r.cot_all, r.cs, r.cr, k).wait()

    def fourth_back(here, t):
        grad, unit = r.acc[here, :], r.unit4[here, :]
        add_gain(4, grad * unit)
        total = r.cot_all[here, :].astype(F32) + norm_back(grad, unit, r.inv4[here, :], gain(4))
        r.res[here, :] = total
        r.low[here, :] = total.astype(LOW)

    tiles(SEG, TILE, fourth_back)
    put(BLOCK["writer_qkv"], tn(hm, r.dwq[...]))
    put(BLOCK["writer_qkv"] + 1, tn(r.src[...], r.wkey[...]))
    put(BLOCK["writer_qkv"] + 2, tn(r.src[...], r.wvalue[...]))
    put(BLOCK["writer_out"], tn(r.wo[...], mem_cot))
    tick()

    for c in range(4):
        columns = slice(c * D, (c + 1) * D)
        r.unit4[...] = nt(r.low[...], r.w_ffn_out[columns, :])
        put(BLOCK["ffn"] + 2 * c, tn(r.z[c], r.low[...]))
        tick()

        def bent(here, t):
            r.z[c, here, :] = (r.unit4[here, :] * r.slope[c, here, :].astype(F32)).astype(LOW)

        tiles(SEG, TILE, bent)
        put(BLOCK["ffn"] + 2 * c + 1, tn(r.h2[...], r.z[c]))
        back = nt(r.z[c], r.w_ffn_in[:, columns])
        r.acc[...] = back if c == 0 else r.acc[...] + back
        tick()

    def third_back(here, t):
        grad, unit = r.acc[here, :], r.unit2[here, :]
        add_gain(2, grad * unit)
        total = r.res[here, :] + norm_back(grad, unit, r.inv2[here, :], gain(2))
        r.res[here, :] = total
        r.low[here, :] = total.astype(LOW)

    tiles(SEG, TILE, third_back)
    tick()

    r.dsend[...] = nt(r.low[...], r.w_cross_out[...]).astype(LOW)
    put(BLOCK["cross_out"], tn(r.co[...], r.low[...]))
    tick()
    r.cross_dk[...] = jnp.zeros_like(r.cross_dk)
    r.cross_dv[...] = jnp.zeros_like(r.cross_dv)

    def cross_back(i):
        here = rows_at(i * 128, 128)
        for g in range(2):
            columns = slice(g * 256, (g + 1) * 256)
            dmix = r.dsend[here, columns]
            queries = r.cq[here, columns]
            dprobs = nt(r.cross_v[g], dmix)
            probs = r.cross_p[2 * i + g].astype(F32)
            delta = jnp.sum((probs * dprobs).reshape(4, slots, 128), axis=1, keepdims=True)
            slopes = (probs * (dprobs.reshape(4, slots, 128) - delta).reshape(256, 128)).astype(LOW)
            r.cross_dk[g] += nn(slopes, queries)
            r.cq[here, columns] = (
                tn(slopes, r.cross_k[g]).astype(LOW).astype(F32) * SCALE
            ).astype(LOW)
            r.cross_dv[g] += nn(r.cross_p[2 * i + g], dmix)

    each(BLOCKS, cross_back)
    for g in range(2):
        columns = slice(g * 256, (g + 1) * 256)
        r.dck[:, columns] = own_blocks(r.cross_dk[g]).astype(LOW)
        r.dcv[:, columns] = own_blocks(r.cross_dv[g]).astype(LOW)
    tick()
    r.acc[...] = nt(r.cq[...], r.w_cross_qkv[0])

    def second_back(here, t):
        grad, unit = r.acc[here, :], r.unit1[here, :]
        add_gain(1, grad * unit)
        total = r.res[here, :] + norm_back(grad, unit, r.inv1[here, :], gain(1))
        r.res[here, :] = total
        r.low[here, :] = total.astype(LOW)

    tiles(SEG, TILE, second_back)
    tick()
    put(BLOCK["cross_qkv"], tn(r.h1[...], r.cq[...]))
    put(BLOCK["cross_qkv"] + 1, tn(hm, r.dck[...]))
    put(BLOCK["cross_qkv"] + 2, tn(hm, r.dcv[...]))
    tick()

    r.dsend[...] = nt(r.low[...], r.w_self_out[...]).astype(LOW)
    put(BLOCK["self_out"], tn(r.mix[...], r.low[...]))
    tick()

    for p in range(PAIRS):
        columns = slice(p * 128, (p + 1) * 128)
        r.dk_sum[...] = jnp.zeros_like(r.dk_sum)
        r.dv_sum[...] = jnp.zeros_like(r.dv_sum)
        for i in range(BLOCKS):
            depth = 128 * (i + 1)
            here = slice(i * 128, (i + 1) * 128)
            stacked = head_stack(r.dsend[here, columns].astype(F32)).astype(LOW)
            queries = head_stack(r.q[here, columns].astype(F32)).astype(LOW)
            probs = r.prob[p, BLOCK_ROWS[i] : BLOCK_ROWS[i + 1], :]
            wide = probs.astype(F32)
            dprobs = nt(r.v[:depth, columns], stacked)
            delta = jnp.sum(wide * dprobs, axis=0, keepdims=True)
            slopes = (wide * (dprobs - delta)).astype(LOW)
            r.dk_sum[:depth, :] += nn(slopes, queries)
            r.dv_sum[:depth, :] += nn(probs, stacked)
            dquery = head_pick(tn(r.k[:depth, columns], slopes)).T
            r.q[here, columns] = (dquery.astype(LOW).astype(F32) * SCALE).astype(LOW)
            if i == 2:
                tick()
        r.k[:, columns] = r.dk_sum[...].astype(LOW)
        r.v[:, columns] = r.dv_sum[...].astype(LOW)
        tick()
    for k, grad in enumerate((r.q, r.k, r.v)):
        put(BLOCK["self_qkv"] + k, tn(r.h0[...], grad[...]))
    tick()
    r.acc[...] = (
        nt(r.q[...], r.w_self_qkv[0]) + nt(r.k[...], r.w_self_qkv[1]) + nt(r.v[...], r.w_self_qkv[2])
    )
    spread_wait(*enc_way)
    keep_copy(0, *enc_way).wait()

    def first_back(here, t):
        grad, unit = r.acc[here, :], r.unit0[here, :]
        add_gain(0, grad * unit)
        total = r.res[here, :] + norm_back(grad, unit, r.inv0[here, :], gain(0))
        r.enc[here, :] = total.astype(LOW)

    tiles(SEG, TILE, first_back)
    grad_way = (r.enc, r.input_grad, rows, True, r.gs, r.gr)
    spread(*grad_way)
    keep_copy(2, *grad_way).start()
    tick()

    dhm = (
        nt(r.dwq[...], r.w_writer_qkv[0])
        + nt(r.wkey[slot_range, :], r.w_writer_qkv[1])
        + nt(r.wvalue[slot_range, :], r.w_writer_qkv[2])
        + nt(r.dck[...], r.w_cross_qkv[1])
        + nt(r.dcv[...], r.w_cross_qkv[2])
    )
    unit = r.unit3[...]
    add_gain(3, dhm * unit)
    r.slot_grad[...] = (
        mem_cot.astype(F32) + norm_back(dhm, unit, r.inv3[...], gain(3))
    ).astype(LOW)
    slot_way = (r.slot_grad, r.memory_grad, slots, False, r.ms, r.mr)
    spread(*slot_way)
    keep_copy(3, *slot_way).start()
    r.gain_steps[0] = jnp.concatenate(
        [jnp.sum(r.gain_sum[k], axis=0, keepdims=True) for k in range(5)] + [jnp.zeros((3, D), F32)], axis=0
    )
    tick()
    tick()
    last = pltpu.make_async_copy(r.gain_steps.at[STAGES], r.gains_grad, r.out_sem.at[4])
    last.start()
    last.wait()
    for k, way in enumerate((enc_way, new_way, grad_way, slot_way)):
        if k > 0:
            spread_wait(*way)
            keep_copy(k, *way).wait()


def finish_kernel(enc, new, in_grad, mem_grad, grads, gains, *refs):
    outs, (low, wide, row_low, row_wide, slot_low, slot_wide, load_sem, store_sem, pass_sem) = refs[:13], refs[13:]
    (o_enc, o_new, o_in, o_mem, self_qkv, self_out, cross_qkv, cross_out, ffn_in, ffn_out, writer_qkv,
     writer_out, o_gains) = outs
    slots = wide.shape[0]

    def place(block):
        for name, ref in (("writer_qkv", writer_qkv), ("cross_qkv", cross_qkv), ("self_qkv", self_qkv)):
            if 0 <= block - BLOCK[name] < 3:
                return ref.at[block - BLOCK[name]]
        for name, ref in (("writer_out", writer_out), ("cross_out", cross_out), ("self_out", self_out)):
            if block == BLOCK[name]:
                return ref
        c, second = divmod(block - BLOCK["ffn"], 2)
        return (ffn_in.at[:, pl.ds(c * D, D)] if second else ffn_out.at[pl.ds(c * D, D), :])

    count = GRAD_ROWS // D
    loads = [
        pltpu.make_async_copy(grads.at[pl.ds(k * D, D)], low.at[pl.ds(k * D, D)], load_sem.at[k])
        for k in range(count)
    ]
    rest = [
        pltpu.make_async_copy(in_grad, row_low, pass_sem.at[0]),
        pltpu.make_async_copy(mem_grad, slot_low, pass_sem.at[1]),
        pltpu.make_async_copy(enc, o_enc, pass_sem.at[2]),
        pltpu.make_async_copy(new, o_new, pass_sem.at[3]),
        pltpu.make_async_copy(gains, o_gains, pass_sem.at[4]),
    ]
    for copy in loads + rest:
        copy.start()
    stores = []
    for k in range(count):
        loads[k].wait()
        if k >= slots:
            stores[k - slots].wait()

        def turn(here, t):
            wide[k % slots, here, :] = low[rows_at(k * D + t * 128, 128), :].astype(F32)

        tiles(D, 128, turn)
        stores.append(pltpu.make_async_copy(wide.at[k % slots], place(k), store_sem.at[k % slots]))
        stores[k].start()
    for k, (low_ref, wide_ref, out) in enumerate(((row_low, row_wide, o_in), (slot_low, slot_wide, o_mem))):
        rest[k].wait()
        wide_ref[...] = low_ref[...].astype(F32)
        stores.append(pltpu.make_async_copy(wide_ref, out, store_sem.at[slots + k]))
        stores[-1].start()
    for copy in rest[2:] + stores[count - slots :]:
        copy.wait()


def on_device(*arguments):
    seg_input, memory = arguments[0], arguments[1]
    docs, rows, _ = seg_input.shape
    slots = memory.shape[1]
    docs_count = lax.axis_size("docs")
    scratch = scratch_of(docs, rows, slots, dict(zip(INPUTS, arguments)), docs_count)
    vmem, smem, anywhere = (pl.BlockSpec(memory_space=m) for m in (pltpu.VMEM, pltpu.SMEM, pl.ANY))
    arguments = list(arguments)
    for k in (0, 1, 13, 14):
        arguments[k] = arguments[k].reshape(-1, D)
    names = INPUTS + OUTPUTS + tuple(scratch)
    low = lambda *shape: jax.ShapeDtypeStruct(shape, LOW)
    full = lambda *shape: jax.ShapeDtypeStruct(shape, F32)
    parts = pl.pallas_call(
        functools.partial(layer_kernel, docs, rows, slots, docs_count, names),
        out_shape=(
            low(docs * rows, D), low(docs * slots, D), low(docs * rows, D), low(docs * slots, D),
            low(GRAD_ROWS, D), full(8, D),
        ),
        in_specs=[
            smem if name in ("lengths", "seg_index") else anywhere if name in WEIGHTS else vmem for name in INPUTS
        ],
        out_specs=(anywhere,) * 6,
        scratch_shapes=list(scratch.values()),
        compiler_params=pltpu.CompilerParams(
            collective_id=1, has_side_effects=True, vmem_limit_bytes=VMEM_BYTES
        ),
    )(*arguments)
    shapes = dict(zip(INPUTS, (full(*argument.shape) for argument in arguments)))
    results = pl.pallas_call(
        finish_kernel,
        out_shape=(
            low(docs * rows, D), low(docs * slots, D), full(docs * rows, D), full(docs * slots, D),
            *(shapes[name] for name in INPUTS[4:12]), full(8, D),
        ),
        in_specs=[pl.BlockSpec(memory_space=pltpu.HBM)] * 6,
        out_specs=(pl.BlockSpec(memory_space=pltpu.HBM),) * 13,
        scratch_shapes=[
            pltpu.VMEM((GRAD_ROWS, D), LOW),
            pltpu.VMEM((6, D, D), F32),
            pltpu.VMEM((docs * rows, D), LOW),
            pltpu.VMEM((docs * rows, D), F32),
            pltpu.VMEM((docs * slots, D), LOW),
            pltpu.VMEM((docs * slots, D), F32),
            pltpu.SemaphoreType.DMA((GRAD_ROWS // D,)),
            pltpu.SemaphoreType.DMA((8,)),
            pltpu.SemaphoreType.DMA((5,)),
        ],
        compiler_params=pltpu.CompilerParams(vmem_limit_bytes=40 << 20),
    )(*parts)
    results = list(results)
    for k in (0, 2):
        results[k] = results[k].reshape(docs, rows, D)
    for k in (1, 3):
        results[k] = results[k].reshape(docs, slots, D)
    results[12] = results[12][:5]
    return tuple(results)


def solution(mesh):
    row, slot, whole = P("docs", "seq", None), P("docs", None, None), P()
    return jax.shard_map(
        on_device,
        mesh=mesh,
        in_specs=(row, slot, P("docs"), P("docs")) + (whole,) * 9 + (row, slot),
        out_specs=(row, slot, row, slot) + (whole,) * 9,
        check_vma=False,
    )
```

```python
import functools
import types

import jax
import jax.numpy as jnp
from jax import lax
from jax.experimental import pallas as pl
from jax.experimental.pallas import tpu as pltpu
from jax.sharding import PartitionSpec as P

MESH = pl.DeviceIdType.MESH
F32, LOW = jnp.float32, jnp.bfloat16
VMEM_BYTES = 63 << 20
D = 512
HD = 64
SEG = 512
SHUT = -1e30
SCALE = HD ** (-0.5)

CORE, X, Y, Z0, Z1 = ("seq", 1), ("seq", 2), ("docs", 1), ("docs", 2), ("docs", 4)
ORDERS = dict(
    X=(CORE, X, Y, Z0, Z1), Y=(CORE, Y, X, Z0, Z1), Z=(CORE, Z0, Z1, X, Y), U=(CORE, Y, Z0, Z1, X),
    V=(CORE, X, Z0, Z1, Y), T=(CORE, Z0, Z1, Y, X), A=(CORE, Z0, X, Y, Z1), B=(CORE, Z0, Y, X, Z1),
)
UNITS = {
    "W1": (0, 1024, "Y"),
    "W0": (1024, 1024, "Y"),
    "F00": (2048, 512, "V"),
    "F01": (2560, 512, "X"),
    "F10": (3072, 1024, "X"),
    "F20": (4096, 1024, "A"),
    "F31": (5120, 512, "X"),
    "F30": (5632, 512, "B"),
    "X0": (6144, 512, "U"),
    "X2": (6656, 1024, "Y"),
    "X1": (7680, 512, "V"),
    "S0": (8192, 512, "B"),
    "Q0": (8704, 1024, "X"),
    "Q1": (9728, 512, "Y"),
}
SCHEDULE = (
    ("W1", "W0",),
    (),
    ("F00", "F01", "W1",),
    ("W0",),
    ("F10", "F00", "F01",),
    (),
    ("F20", "F10",),
    (),
    ("F31", "F30", "F20", "F00", "W1",),
    ("F31",),
    ("F30", "F01",),
    (),
    ("W0", "F01",),
    ("X0", "X2", "X1", "F20", "F10",),
    ("S0", "F00",),
    ("X0", "W1",),
    ("X2", "F30", "X1", "F01", "S0",),
    ("F31", "F10", "F00",),
    ("W1",),
    ("W0", "F01", "X0",),
    (),
    ("S0", "F20",),
    ("F10",),
    ("Q0", "Q1", "W1", "W0", "X1", "X2",),
    ("F01", "X0", "F30", "Q0",),
    ("F10", "Q1", "F31", "F00", "W1", "S0", "X1",),
    (
        "gains", "X2", "W0", "F01", "F20", "F30", "X0", "F31", "F10", "W1", "Q1", "gains", "F00", "X1",
        "F01", "X2", "Q0", "S0", "W0", "X0", "X1", "F20", "gains", "F30", "F31", "F10", "W1", "F00", "X2",
        "Q0", "Q1", "X1", "S0", "gains", "W0", "F20", "F30", "F01", "F10", "X0", "F31", "F00", "F01", "X2",
        "gains", "Q0", "W0", "Q1", "F30", "X1", "S0", "W1", "X0", "F31", "F20", "gains", "X2", "W1", "Q0",
        "Q1", "F10", "X1", "X0", "F10", "F00", "W0", "S0", "Q0", "Q1", "F00", "F30", "W0", "F31", "F20",
        "Q0", "Q1", "X0", "X2", "S0", "X0", "F30", "X1", "F30", "Q0", "X1", "F31", "Q1", "F20", "F31", "X2",
        "F20", "S0", "X2", "Q1", "Q0", "S0", "Q1", "Q0",
    ),
)
GROUP = 8


def place_of(stage):
    axis, stride = stage
    index = lax.axis_index(axis)
    bit = lax.rem(lax.div(index, stride), 2)
    return bit, {axis: index + stride * (1 - 2 * bit)}


def outer_partners(docs_count):
    index = lax.axis_index("docs")
    return [{"docs": lax.rem(index + GROUP * k, docs_count)} for k in range(1, docs_count // GROUP)]


def partners_of(docs_count):
    return [place_of(stage)[1] for stage in ORDERS["X"]] + outer_partners(docs_count)


BLOCK = dict(
    writer_qkv=0, writer_out=3, ffn=4, cross_out=12, cross_qkv=13, self_out=16, self_qkv=17,
)
GRAD_ROWS = 20 * 512
STAGES = 5


class Summer:
    def __init__(self, r, docs_count, share):
        self.r, self.share, self.docs_count = r, share, docs_count
        self.index = {name: k for k, name in enumerate(UNITS)}
        self.at = {}

    def remote(self, source, target, name, j, partner):
        k = self.index[name]
        return pltpu.make_async_remote_copy(
            src_ref=source, dst_ref=target, send_sem=self.r.unit_s.at[k], recv_sem=self.r.unit_r.at[k, j],
            device_id=partner, device_id_type=MESH,
        )

    def other(self, source, target, sems, k, j, partner):
        return pltpu.make_async_remote_copy(
            src_ref=source, dst_ref=target, send_sem=sems[0].at[k, j], recv_sem=sems[1].at[k, j],
            device_id=partner, device_id_type=MESH,
        )

    def give(self, name, j, start, size):
        r = self.r
        base, rows, order = UNITS[name]
        bit, partner = place_of(ORDERS[order][j])
        half = size // 2
        first = base + rows - size
        copy = self.remote(
            r.grad.at[rows_at(start + (1 - bit) * half, half)], r.landed.at[pl.ds(first, half)],
            name, j, partner,
        )
        copy.start()
        self.at[name] = ("give", j, copy, start + bit * half, half, first)

    def spread(self, name, j, start, size):
        r = self.r
        bit, partner = place_of(ORDERS[UNITS[name][2]][j])
        here = rows_at(start, size)
        source = r.grad if j == STAGES - 1 else r.grads
        copy = self.remote(source.at[here], r.grads.at[here], name, 2 * STAGES - 1 - j, partner)
        copy.start()
        self.at[name] = ("spread", j, copy, start - bit * size, 2 * size, None)

    def own(self, name, start, size):
        here = rows_at(start, size)
        return pltpu.make_async_copy(
            self.r.grad.at[here], self.r.grads.at[here], self.r.own_sem.at[self.index[name]]
        )

    def step(self, name):
        r = self.r
        if name == "gains":
            return self.step_gains()
        if name not in self.at:
            base, rows, order = UNITS[name]
            return self.give(name, 0, base, rows)
        kind, j, copy, start, size, first = self.at[name]
        copy.wait()
        if kind == "give":
            add_rows(r.grad, start, size, r.landed, first, self.share if j == 0 else None)
            if j + 1 < STAGES:
                return self.give(name, j + 1, start, size)
            self.outer(name, start, size)
            store = self.own(name, start, size)
            store.start()
            self.spread(name, j, start, size)
            self.store = getattr(self, "store", {})
            self.store[name] = store
        else:
            if j == STAGES - 1:
                self.store[name].wait()
            if j > 0:
                self.spread(name, j - 1, start, size)
            else:
                self.at[name] = None

    def outer(self, name, start, size):
        others = outer_partners(self.docs_count)
        if not others:
            return
        r = self.r
        mine = lax.div(lax.axis_index("docs"), GROUP)
        here = rows_at(start, size)
        share = pl.ds(UNITS[name][0] // 32, size)
        r.outer[mine, share, :] = r.grad[here, :]
        copies = [
            self.other(
                r.grad.at[here], r.outer.at[mine, share], (r.outer_s, r.outer_r), self.index[name], k, partner
            )
            for k, partner in enumerate(others)
        ]
        for copy in copies:
            copy.start()
        for copy in copies:
            copy.wait()
        parts = [r.outer[k, share, :].astype(F32) for k in range(len(others) + 1)]
        r.grad[here, :] = sum(parts).astype(LOW)

    def step_gains(self):
        r = self.r
        j = self.at.get("gains", 0)
        if j > 0:
            self.gain_copy(j - 1).wait()
            more = r.gain_landed[j - 1]
            if j == 1:
                more = more * self.share
            r.gain_steps[j] = r.gain_steps[j - 1] + more
        if j < STAGES:
            self.gain_copy(j).start()
        else:
            others = outer_partners(self.docs_count)
            if others:
                mine = lax.div(lax.axis_index("docs"), GROUP)
                r.gain_outer[mine] = r.gain_steps[j]
                copies = [
                    self.other(r.gain_steps.at[j], r.gain_outer.at[mine], (r.gain_os, r.gain_or), 0, k, partner)
                    for k, partner in enumerate(others)
                ]
                for copy in copies:
                    copy.start()
                for copy in copies:
                    copy.wait()
                r.gain_steps[j] = sum(r.gain_outer[k] for k in range(len(others) + 1))
        self.at["gains"] = j + 1

    def gain_copy(self, j):
        r = self.r
        partner = place_of(ORDERS["X"][j])[1]
        return self.other(r.gain_steps.at[j], r.gain_landed.at[j], (r.gain_s, r.gain_r), 0, j, partner)


def add_rows(total, start, rows, landed, first, share=None):
    tile = min(rows, 128)

    def turn(t, carry):
        here = rows_at(start + t * tile, tile)
        more = landed[rows_at(first + t * tile, tile), :].astype(F32)
        if share is not None:
            more = more * share
        total[here, :] = (total[here, :].astype(F32) + more).astype(total.dtype)
        return carry

    lax.fori_loop(0, rows // tile, turn, 0)


def dot(left, right, left_dim, right_dim):
    return lax.dot_general(
        left, right, (((left_dim,), (right_dim,)), ((), ())), preferred_element_type=F32
    )


def nn(left, right):
    return dot(left, right, 1, 0)


def nt(left, right):
    return dot(left, right, 1, 1)


def tn(left, right):
    return dot(left, right, 0, 0)


def tiles(rows, tile, body):
    def turn(t, carry):
        body(pl.ds(pl.multiple_of(t * tile, tile), tile), t)
        return carry

    lax.fori_loop(0, rows // tile, turn, 0)


def rows_at(start, size):
    return pl.ds(pl.multiple_of(start, 16), size)


def norm_rows(values, gain_row):
    centered = values - jnp.mean(values, axis=-1, keepdims=True)
    inverse = lax.rsqrt(jnp.mean(centered * centered, axis=-1, keepdims=True) + 1e-05)
    unit = centered * inverse
    return (unit * gain_row).astype(LOW), unit, inverse


def norm_back(grad, unit, inverse, gain_row):
    scaled = grad * gain_row
    adjusted = (
        scaled
        - jnp.mean(scaled, axis=-1, keepdims=True)
        - unit * jnp.mean(scaled * unit, axis=-1, keepdims=True)
    )
    return adjusted * inverse


def same_head():
    left = lax.div(lax.broadcasted_iota(jnp.int32, (256, 256), 0), HD)
    right = lax.div(lax.broadcasted_iota(jnp.int32, (256, 256), 1), HD)
    return left == right


def four_heads(values):
    return jnp.where(same_head(), jnp.concatenate([values] * 4, axis=0), 0.0)


def own_blocks(values):
    return jnp.sum(jnp.where(same_head(), values, 0.0).reshape(4, HD, 256), axis=0)


def swap(values):
    return own_blocks(four_heads(values).T)


def head_stack(values):
    low_half = lax.broadcasted_iota(jnp.int32, values.shape, 1) < HD
    return jnp.concatenate(
        [jnp.where(low_half, values, 0.0), jnp.where(low_half, 0.0, values)], axis=0
    )


def head_pick(values):
    low_half = lax.broadcasted_iota(jnp.int32, (128, 128), 0) < HD
    return jnp.where(low_half, values[:, :128], values[:, 128:])


BLOCKS = SEG // 128
BLOCK_ROWS = [sum(128 * (k + 1) for k in range(i)) for i in range(BLOCKS + 1)]
PAIRS = D // 128

WEIGHTS = (
    "self_qkv", "cross_qkv", "writer_qkv", "writer_out", "self_out", "cross_out", "ffn_in", "ffn_out",
)
INPUTS = (
    "x", "memory", "lengths", "seg_index", "self_qkv", "self_out", "cross_qkv", "cross_out",
    "ffn_in", "ffn_out", "writer_qkv", "writer_out", "gains", "out_cot", "mem_cot",
)
OUTPUTS = ("enc_out", "new_memory", "input_grad", "memory_grad", "grads", "gains_grad")
def scratch_of(docs, rows, slots, weights, docs_count):
    keys = SEG + slots
    units, outers = len(UNITS), max(1, docs_count // GROUP)
    dma = pltpu.SemaphoreType.DMA
    low = lambda *shape: pltpu.VMEM(shape, LOW)
    full = lambda *shape: pltpu.VMEM(shape, F32)
    fetched = {"w_" + name: pltpu.VMEM(weights[name].shape, LOW) for name in WEIGHTS}
    return dict(
        **fetched,
        mem=low(slots, D),
        mem_back=low(slots, D),
        gain_rows=full(5, D),
        x_all=low(SEG, D),
        cot_all=low(SEG, D),
        enc=low(SEG, D),
        slot_grad=low(slots, D),
        new_slots=low(slots, D),
        unit0=full(SEG, D),
        unit1=full(SEG, D),
        unit2=full(SEG, D),
        unit4=full(SEG, D),
        unit3=full(slots, D),
        inv0=full(SEG, 1),
        inv1=full(SEG, 1),
        inv2=full(SEG, 1),
        inv4=full(SEG, 1),
        inv3=full(slots, 1),
        h0=low(SEG, D),
        h1=low(SEG, D),
        h2=low(SEG, D),
        src=low(keys, D),
        q=low(SEG, D),
        k=low(SEG, D),
        v=low(SEG, D),
        prob=low(PAIRS, BLOCK_ROWS[-1], 256),
        mix=low(SEG, D),
        acc=full(SEG, D),
        res=full(SEG, D),
        cq=low(SEG, D),
        cross_k=low(2, 256, 256),
        cross_v=low(2, 256, 256),
        cross_p=low(2 * BLOCKS, 256, 128),
        cross_dk=full(2, 256, 256),
        cross_dv=full(2, 256, 256),
        co=low(SEG, D),
        z=low(4, SEG, D),
        slope=low(4, SEG, D),
        wkey=low(keys, D),
        wvalue=low(keys, D),
        wquery=low(2, 256, 256),
        dmix=low(2, 256, 256),
        wo=low(slots, D),
        dwq=low(slots, D),
        dck=low(slots, D),
        dcv=low(slots, D),
        low=low(SEG, D),
        dsend=low(SEG, D),
        dk_sum=full(SEG, 128),
        dv_sum=full(SEG, 128),
        gain_sum=full(5, 8, D),
        gain_steps=full(STAGES + 1, 8, D),
        gain_landed=full(STAGES, 8, D),
        gain_outer=full(outers, 8, D),
        grad=low(GRAD_ROWS, D),
        landed=low(GRAD_ROWS, D),
        outer=low(outers, GRAD_ROWS // 32, D),
        unit_s=dma((units,)),
        unit_r=dma((units, 2 * STAGES)),
        own_sem=dma((units,)),
        outer_s=dma((units if outers > 1 else 1, outers)),
        outer_r=dma((units if outers > 1 else 1, outers)),
        gain_s=dma((1, STAGES)),
        gain_r=dma((1, STAGES)),
        gain_os=dma((1, outers)),
        gain_or=dma((1, outers)),
        load_sem=dma((len(WEIGHTS) + 5,)),
        xs=dma((3,)),
        xr=dma((3,)),
        cs=dma((3,)),
        cr=dma((3,)),
        es=dma((3,)),
        er=dma((3,)),
        us=dma((3,)),
        ur=dma((3,)),
        gs=dma((3,)),
        gr=dma((3,)),
        ms=dma((3,)),
        mr=dma((3,)),
        out_sem=dma((5,)),
    )


def layer_kernel(docs, rows, slots, docs_count, names, *refs):
    r = types.SimpleNamespace(**dict(zip(names, refs)))
    s = lax.axis_index("seq")
    bit0, bit1 = lax.rem(s, 2), lax.div(s, 2)
    near = s + 1 - 2 * bit0
    far = s + 2 - 4 * bit1
    across = near + 2 - 4 * bit1
    peers = (near, far, across)

    def doc_of(index):
        return jnp.minimum(index, docs - 1)

    mine = doc_of(s)

    def remote(source, target, send_sem, recv_sem, to):
        return pltpu.make_async_remote_copy(
            src_ref=source, dst_ref=target, send_sem=send_sem, recv_sem=recv_sem,
            device_id={"seq": to}, device_id_type=MESH,
        )

    def gain(k):
        return r.gain_rows[k : k + 1, :]

    def add_gain(k, values):
        r.gain_sum[k] += jnp.sum(values.reshape(-1, 8, D), axis=0)

    barrier = pltpu.get_barrier_semaphore()
    greeted = [{"seq": across}] + partners_of(docs_count)
    for partner in greeted:
        pl.semaphore_signal(barrier, inc=1, device_id=partner, device_id_type=MESH)
    own_rows = rows_at(s * rows, rows)
    doc_rows, doc_slots = rows_at(mine * rows, rows), rows_at(mine * slots, slots)
    fetched = dict(
        mem=(r.memory.at[doc_slots], r.mem),
        gains=(r.gains, r.gain_rows),
        x=(r.x.at[doc_rows], r.x_all.at[own_rows]),
        mem_cot=(r.mem_cot.at[doc_slots], r.mem_back),
        **{name: (getattr(r, name), getattr(r, "w_" + name)) for name in WEIGHTS},
        cot=(r.out_cot.at[doc_rows], r.cot_all.at[own_rows]),
    )
    loads = {}
    for k, (name, (source, target)) in enumerate(fetched.items()):
        loads[name] = pltpu.make_async_copy(source, target, r.load_sem.at[k])
        loads[name].start()
    r.gain_sum[...] = jnp.zeros_like(r.gain_sum)
    loads["mem"].wait()
    loads["gains"].wait()
    slot_range = pl.ds(SEG, slots)
    hm, r.unit3[...], r.inv3[...] = norm_rows(r.mem[...].astype(F32), gain(3))
    r.src[slot_range, :] = hm
    pl.semaphore_wait(barrier, len(greeted))

    def gather_copy(source, target, send_sem, recv_sem, k):
        return remote(
            source.at[rows_at(doc_of(peers[k]) * rows, rows)],
            target.at[rows_at(s * rows, rows)], send_sem.at[k], recv_sem.at[k], peers[k],
        )

    for k in range(3):
        gather_copy(r.x, r.x_all, r.xs, r.xr, k).start()

    def spread_copy(source, target, size, own, send_sem, recv_sem, k):
        piece = source.at[rows_at(peers[k] * size, size)] if own else source
        return remote(
            piece, target.at[rows_at(mine * size, size)], send_sem.at[k], recv_sem.at[k], peers[k]
        )

    def keep_copy(k, source, target, size, own, *sems):
        piece = source.at[rows_at(s * size, size)] if own else source
        return pltpu.make_async_copy(piece, target.at[rows_at(mine * size, size)], r.out_sem.at[k])

    summer = Summer(r, docs_count, 1.0 - bit1.astype(F32))
    ticks = iter(SCHEDULE)

    def tick():
        for name in next(ticks):
            summer.step(name)

    def spread(*where):
        spread_copy(*where, 1).start()

        @pl.when(bit1 == 0)
        def _():
            spread_copy(*where, 0).start()
            spread_copy(*where, 2).start()

    def spread_wait(*where):
        spread_copy(*where, 1).wait()

        @pl.when(bit1 == 0)
        def _():
            spread_copy(*where, 0).wait()
            spread_copy(*where, 2).wait_send()

        @pl.when(bit1 == 1)
        def _():
            spread_copy(*where, 2).wait_recv()

    def place_heads(target, values):
        for g in range(2):
            piece = values[:, g * 256 : (g + 1) * 256].astype(LOW).astype(F32)
            target[g] = four_heads(piece).astype(LOW)

    loads["cross_qkv"].wait()
    place_heads(r.cross_k, nn(hm, r.w_cross_qkv[1]))
    place_heads(r.cross_v, nn(hm, r.w_cross_qkv[2]))
    loads["writer_qkv"].wait()
    r.wkey[slot_range, :] = nn(hm, r.w_writer_qkv[1]).astype(LOW)
    r.wvalue[slot_range, :] = nn(hm, r.w_writer_qkv[2]).astype(LOW)
    place_heads(r.wquery, nn(hm, r.w_writer_qkv[0]) * SCALE)
    loads["writer_out"].wait()
    loads["mem_cot"].wait()
    mem_cot = r.mem_back[...]
    place_heads(r.dmix, nt(mem_cot, r.w_writer_out[...]))

    def enter(start):
        here = rows_at(start, SEG // 2)
        normed, unit, inverse = norm_rows(r.x_all[here, :].astype(F32), gain(0))
        r.unit0[here, :] = unit
        r.inv0[here, :] = inverse
        r.h0[here, :] = normed
        r.q[here, :] = (nn(normed, r.w_self_qkv[0]) * SCALE).astype(LOW)
        r.k[here, :] = nn(normed, r.w_self_qkv[1]).astype(LOW)
        r.v[here, :] = nn(normed, r.w_self_qkv[2]).astype(LOW)

    loads["x"].wait()
    loads["self_qkv"].wait()
    gather_copy(r.x, r.x_all, r.xs, r.xr, 0).wait_recv()
    enter(bit1 * (SEG // 2))
    for k in (1, 2):
        gather_copy(r.x, r.x_all, r.xs, r.xr, k).wait_recv()
    for k in range(3):
        gather_copy(r.out_cot, r.cot_all, r.cs, r.cr, k).start()
    enter((1 - bit1) * (SEG // 2))
    for k in range(3):
        gather_copy(r.x, r.x_all, r.xs, r.xr, k).wait_send()
    live = jnp.minimum(r.lengths[mine] - r.seg_index[mine] * SEG, SEG)

    for p in range(PAIRS):
        columns = slice(p * 128, (p + 1) * 128)
        for i in range(BLOCKS):
            depth = 128 * (i + 1)
            here = slice(i * 128, (i + 1) * 128)
            stacked = head_stack(r.q[here, columns].astype(F32)).astype(LOW)
            scores = nt(r.k[:depth, columns], stacked)
            key_pos = lax.broadcasted_iota(jnp.int32, scores.shape, 0)
            query_pos = i * 128 + lax.rem(lax.broadcasted_iota(jnp.int32, scores.shape, 1), 128)
            scores = jnp.where((key_pos <= query_pos) & (key_pos < live), scores, SHUT)
            powers = jnp.exp(scores - jnp.max(scores, axis=0, keepdims=True))
            inverse = 1.0 / jnp.sum(powers, axis=0, keepdims=True)
            probs = (powers * inverse).astype(LOW)
            r.prob[p, BLOCK_ROWS[i] : BLOCK_ROWS[i + 1], :] = probs
            mixed = head_pick(tn(r.v[:depth, columns], probs))
            r.mix[here, columns] = mixed.T.astype(LOW)

    loads["self_out"].wait()
    total = r.x_all[...].astype(F32) + nn(r.mix[...], r.w_self_out[...])
    r.res[...] = total
    r.h1[...], r.unit1[...], r.inv1[...] = norm_rows(total, gain(1))
    r.cq[...] = (nn(r.h1[...], r.w_cross_qkv[0]) * SCALE).astype(LOW)

    for i in range(BLOCKS):
        here = slice(i * 128, (i + 1) * 128)
        for g in range(2):
            columns = slice(g * 256, (g + 1) * 256)
            scores = nt(r.cross_k[g], r.cq[here, columns]).reshape(4, slots, 128)
            powers = jnp.exp(scores - jnp.max(scores, axis=1, keepdims=True))
            inverse = 1.0 / jnp.sum(powers, axis=1, keepdims=True)
            probs = (powers * inverse).reshape(256, 128).astype(LOW)
            r.cross_p[2 * i + g] = probs
            r.co[here, columns] = tn(probs, r.cross_v[g]).astype(LOW)

    loads["cross_out"].wait()
    total = r.res[...] + nn(r.co[...], r.w_cross_out[...])
    r.res[...] = total
    r.h2[...], r.unit2[...], r.inv2[...] = norm_rows(total, gain(2))

    rate, cube = 0.7978845608028654, 0.044715
    loads["ffn_in"].wait()
    loads["ffn_out"].wait()

    for c in range(4):
        columns = slice(c * D, (c + 1) * D)
        u = nn(r.h2[...], r.w_ffn_in[:, columns])
        square = u * u
        bend = jnp.tanh(rate * u * (1.0 + cube * square))
        half = 0.5 * (1.0 + bend)
        r.z[c] = (u * half).astype(LOW)
        slope = half + (0.5 * rate) * u * (1.0 - bend * bend) * (1.0 + 3.0 * cube * square)
        r.slope[c] = slope.astype(LOW)
        r.res[...] += nn(r.z[c], r.w_ffn_out[columns, :])

    total = r.res[...]
    r.enc[...] = total.astype(LOW)
    r.src[:SEG, :], r.unit4[...], r.inv4[...] = norm_rows(total, gain(4))
    enc_way = (r.enc, r.enc_out, rows, True, r.es, r.er)
    spread(*enc_way)
    keep_copy(0, *enc_way).start()

    written = r.src[:SEG, :]
    r.wkey[:SEG, :] = nn(written, r.w_writer_qkv[1]).astype(LOW)
    r.wvalue[:SEG, :] = nn(written, r.w_writer_qkv[2]).astype(LOW)
    for g in range(2):
        columns = slice(g * 256, (g + 1) * 256)
        keys = r.wkey[:, columns]
        scores = nt(keys, r.wquery[g])
        key_pos = lax.broadcasted_iota(jnp.int32, scores.shape, 0)
        scores = jnp.where((key_pos >= SEG) | (key_pos < live), scores, SHUT)
        powers = jnp.exp(scores - jnp.max(scores, axis=0, keepdims=True))
        probs = powers * (1.0 / jnp.sum(powers, axis=0, keepdims=True))
        probs_low = probs.astype(LOW)
        mixed = own_blocks(tn(r.wvalue[:, columns], probs_low)).astype(LOW).astype(F32)
        r.wo[:, columns] = swap(mixed).astype(LOW)
        dprobs = nt(r.wvalue[:, columns], r.dmix[g])
        delta = jnp.sum(probs * dprobs, axis=0, keepdims=True)
        slopes = (probs * (dprobs - delta)).astype(LOW)
        dquery = own_blocks(tn(slopes, keys)).astype(LOW).astype(F32)
        r.dwq[:, columns] = (dquery * SCALE).astype(LOW)
        r.wkey[:, columns] = nn(slopes, r.wquery[g]).astype(LOW)
        r.wvalue[:, columns] = nn(probs_low, r.dmix[g]).astype(LOW)

    r.new_slots[...] = (
        r.mem[...].astype(F32) + nn(r.wo[...], r.w_writer_out[...])
    ).astype(LOW)
    new_way = (r.new_slots, r.new_memory, slots, False, r.us, r.ur)
    spread(*new_way)
    keep_copy(1, *new_way).start()

    def put(block, values):
        r.grad[block * D : (block + 1) * D, :] = values.astype(LOW)

    grad = nt(r.wkey[:SEG, :], r.w_writer_qkv[1]) + nt(r.wvalue[:SEG, :], r.w_writer_qkv[2])
    loads["cot"].wait()
    for k in range(3):
        gather_copy(r.out_cot, r.cot_all, r.cs, r.cr, k).wait()
    add_gain(4, grad * r.unit4[...])
    total = r.cot_all[...].astype(F32) + norm_back(grad, r.unit4[...], r.inv4[...], gain(4))
    r.res[...] = total
    r.low[...] = total.astype(LOW)
    put(BLOCK["writer_qkv"], tn(hm, r.dwq[...]))
    put(BLOCK["writer_qkv"] + 1, tn(r.src[...], r.wkey[...]))
    put(BLOCK["writer_qkv"] + 2, tn(r.src[...], r.wvalue[...]))
    put(BLOCK["writer_out"], tn(r.wo[...], mem_cot))
    tick()

    for c in range(4):
        columns = slice(c * D, (c + 1) * D)
        put(BLOCK["ffn"] + 2 * c, tn(r.z[c], r.low[...]))
        tick()
        r.z[c] = (nt(r.low[...], r.w_ffn_out[columns, :]) * r.slope[c].astype(F32)).astype(LOW)
        put(BLOCK["ffn"] + 2 * c + 1, tn(r.h2[...], r.z[c]))
        back = nt(r.z[c], r.w_ffn_in[:, columns])
        r.acc[...] = back if c == 0 else r.acc[...] + back
        tick()

    grad, unit = r.acc[...], r.unit2[...]
    add_gain(2, grad * unit)
    total = r.res[...] + norm_back(grad, unit, r.inv2[...], gain(2))
    r.res[...] = total
    r.low[...] = total.astype(LOW)
    tick()

    r.dsend[...] = nt(r.low[...], r.w_cross_out[...]).astype(LOW)
    put(BLOCK["cross_out"], tn(r.co[...], r.low[...]))
    tick()
    r.cross_dk[...] = jnp.zeros_like(r.cross_dk)
    r.cross_dv[...] = jnp.zeros_like(r.cross_dv)

    for i in range(BLOCKS):
        here = slice(i * 128, (i + 1) * 128)
        for g in range(2):
            columns = slice(g * 256, (g + 1) * 256)
            dmix = r.dsend[here, columns]
            queries = r.cq[here, columns]
            dprobs = nt(r.cross_v[g], dmix)
            probs = r.cross_p[2 * i + g].astype(F32)
            delta = jnp.sum((probs * dprobs).reshape(4, slots, 128), axis=1, keepdims=True)
            slopes = (probs * (dprobs.reshape(4, slots, 128) - delta).reshape(256, 128)).astype(LOW)
            r.cross_dk[g] += nn(slopes, queries)
            r.cq[here, columns] = (
                tn(slopes, r.cross_k[g]).astype(LOW).astype(F32) * SCALE
            ).astype(LOW)
            r.cross_dv[g] += nn(r.cross_p[2 * i + g], dmix)

    for g in range(2):
        columns = slice(g * 256, (g + 1) * 256)
        r.dck[:, columns] = own_blocks(r.cross_dk[g]).astype(LOW)
        r.dcv[:, columns] = own_blocks(r.cross_dv[g]).astype(LOW)
    tick()
    r.acc[...] = nt(r.cq[...], r.w_cross_qkv[0])

    grad, unit = r.acc[...], r.unit1[...]
    add_gain(1, grad * unit)
    total = r.res[...] + norm_back(grad, unit, r.inv1[...], gain(1))
    r.res[...] = total
    r.low[...] = total.astype(LOW)
    tick()
    put(BLOCK["cross_qkv"], tn(r.h1[...], r.cq[...]))
    put(BLOCK["cross_qkv"] + 1, tn(hm, r.dck[...]))
    put(BLOCK["cross_qkv"] + 2, tn(hm, r.dcv[...]))
    tick()

    r.dsend[...] = nt(r.low[...], r.w_self_out[...]).astype(LOW)
    put(BLOCK["self_out"], tn(r.mix[...], r.low[...]))
    tick()

    for p in range(PAIRS):
        columns = slice(p * 128, (p + 1) * 128)
        r.dk_sum[...] = jnp.zeros_like(r.dk_sum)
        r.dv_sum[...] = jnp.zeros_like(r.dv_sum)
        for i in range(BLOCKS):
            depth = 128 * (i + 1)
            here = slice(i * 128, (i + 1) * 128)
            stacked = head_stack(r.dsend[here, columns].astype(F32)).astype(LOW)
            queries = head_stack(r.q[here, columns].astype(F32)).astype(LOW)
            probs = r.prob[p, BLOCK_ROWS[i] : BLOCK_ROWS[i + 1], :]
            wide = probs.astype(F32)
            dprobs = nt(r.v[:depth, columns], stacked)
            delta = jnp.sum(wide * dprobs, axis=0, keepdims=True)
            slopes = (wide * (dprobs - delta)).astype(LOW)
            r.dk_sum[:depth, :] += nn(slopes, queries)
            r.dv_sum[:depth, :] += nn(probs, stacked)
            dquery = head_pick(tn(r.k[:depth, columns], slopes)).T
            r.q[here, columns] = (dquery.astype(LOW).astype(F32) * SCALE).astype(LOW)
            if i == 2:
                tick()
        r.k[:, columns] = r.dk_sum[...].astype(LOW)
        r.v[:, columns] = r.dv_sum[...].astype(LOW)
        tick()
    for k, grad in enumerate((r.q, r.k, r.v)):
        put(BLOCK["self_qkv"] + k, tn(r.h0[...], grad[...]))
    tick()
    r.acc[...] = (
        nt(r.q[...], r.w_self_qkv[0]) + nt(r.k[...], r.w_self_qkv[1]) + nt(r.v[...], r.w_self_qkv[2])
    )
    spread_wait(*enc_way)
    keep_copy(0, *enc_way).wait()

    grad, unit = r.acc[...], r.unit0[...]
    add_gain(0, grad * unit)
    total = r.res[...] + norm_back(grad, unit, r.inv0[...], gain(0))
    r.enc[...] = total.astype(LOW)
    grad_way = (r.enc, r.input_grad, rows, True, r.gs, r.gr)
    spread(*grad_way)
    keep_copy(2, *grad_way).start()
    tick()

    dhm = (
        nt(r.dwq[...], r.w_writer_qkv[0])
        + nt(r.wkey[slot_range, :], r.w_writer_qkv[1])
        + nt(r.wvalue[slot_range, :], r.w_writer_qkv[2])
        + nt(r.dck[...], r.w_cross_qkv[1])
        + nt(r.dcv[...], r.w_cross_qkv[2])
    )
    unit = r.unit3[...]
    add_gain(3, dhm * unit)
    r.slot_grad[...] = (
        mem_cot.astype(F32) + norm_back(dhm, unit, r.inv3[...], gain(3))
    ).astype(LOW)
    slot_way = (r.slot_grad, r.memory_grad, slots, False, r.ms, r.mr)
    spread(*slot_way)
    keep_copy(3, *slot_way).start()
    r.gain_steps[0] = jnp.concatenate(
        [jnp.sum(r.gain_sum[k], axis=0, keepdims=True) for k in range(5)] + [jnp.zeros((3, D), F32)], axis=0
    )
    tick()
    tick()
    last = pltpu.make_async_copy(r.gain_steps.at[STAGES], r.gains_grad, r.out_sem.at[4])
    last.start()
    last.wait()
    for k, way in enumerate((enc_way, new_way, grad_way, slot_way)):
        if k > 0:
            spread_wait(*way)
            keep_copy(k, *way).wait()


def finish_kernel(enc, new, in_grad, mem_grad, grads, gains, *refs):
    outs, (low, wide, row_low, row_wide, slot_low, slot_wide, enc_low, new_low, gain_wide, load_sem, store_sem,
           pass_sem) = refs[:13], refs[13:]
    (o_enc, o_new, o_in, o_mem, self_qkv, self_out, cross_qkv, cross_out, ffn_in, ffn_out, writer_qkv,
     writer_out, o_gains) = outs
    slots = wide.shape[0]

    def place(block):
        for name, ref in (("writer_qkv", writer_qkv), ("cross_qkv", cross_qkv), ("self_qkv", self_qkv)):
            if 0 <= block - BLOCK[name] < 3:
                return ref.at[block - BLOCK[name]]
        for name, ref in (("writer_out", writer_out), ("cross_out", cross_out), ("self_out", self_out)):
            if block == BLOCK[name]:
                return ref
        c, second = divmod(block - BLOCK["ffn"], 2)
        return (ffn_in.at[:, pl.ds(c * D, D)] if second else ffn_out.at[pl.ds(c * D, D), :])

    count = GRAD_ROWS // D
    loads = [
        pltpu.make_async_copy(grads.at[pl.ds(k * D, D)], low.at[pl.ds(k * D, D)], load_sem.at[k])
        for k in range(count)
    ]
    rest = [
        pltpu.make_async_copy(source, target, pass_sem.at[k])
        for k, (source, target) in enumerate(
            ((in_grad, row_low), (mem_grad, slot_low), (enc, enc_low), (new, new_low), (gains, gain_wide))
        )
    ]
    for copy in loads + rest:
        copy.start()
    stores = []
    for k in range(count):
        loads[k].wait()
        if k >= slots:
            stores[k - slots].wait()

        def turn(here, t):
            wide[k % slots, here, :] = low[rows_at(k * D + t * 128, 128), :].astype(F32)

        tiles(D, 128, turn)
        stores.append(pltpu.make_async_copy(wide.at[k % slots], place(k), store_sem.at[k % slots]))
        stores[k].start()
    ways = (
        (row_low, row_wide, o_in), (slot_low, slot_wide, o_mem), (enc_low, enc_low, o_enc), (new_low, new_low, o_new),
        (gain_wide, gain_wide, o_gains),
    )
    for k, (read, held, out) in enumerate(ways):
        rest[k].wait()
        if read is not held:
            held[...] = read[...].astype(F32)
        stores.append(pltpu.make_async_copy(held, out, store_sem.at[slots + k]))
        stores[-1].start()
    for copy in stores[count - slots :]:
        copy.wait()


def on_device(*arguments):
    seg_input, memory = arguments[0], arguments[1]
    docs, rows, _ = seg_input.shape
    slots = memory.shape[1]
    docs_count = lax.axis_size("docs")
    scratch = scratch_of(docs, rows, slots, dict(zip(INPUTS, arguments)), docs_count)
    smem, anywhere = pl.BlockSpec(memory_space=pltpu.SMEM), pl.BlockSpec(memory_space=pl.ANY)
    arguments = list(arguments)
    for k in (0, 1, 13, 14):
        arguments[k] = arguments[k].reshape(-1, D)
    names = INPUTS + OUTPUTS + tuple(scratch)
    low = lambda *shape: jax.ShapeDtypeStruct(shape, LOW)
    full = lambda *shape: jax.ShapeDtypeStruct(shape, F32)
    parts = pl.pallas_call(
        functools.partial(layer_kernel, docs, rows, slots, docs_count, names),
        out_shape=(
            low(docs * rows, D), low(docs * slots, D), low(docs * rows, D), low(docs * slots, D),
            low(GRAD_ROWS, D), full(8, D),
        ),
        in_specs=[
            smem if name in ("lengths", "seg_index") else anywhere for name in INPUTS
        ],
        out_specs=(anywhere,) * 6,
        scratch_shapes=list(scratch.values()),
        compiler_params=pltpu.CompilerParams(
            collective_id=1, has_side_effects=True, vmem_limit_bytes=VMEM_BYTES
        ),
    )(*arguments)
    shapes = dict(zip(INPUTS, (full(*argument.shape) for argument in arguments)))
    results = pl.pallas_call(
        finish_kernel,
        out_shape=(
            low(docs * rows, D), low(docs * slots, D), full(docs * rows, D), full(docs * slots, D),
            *(shapes[name] for name in INPUTS[4:12]), full(8, D),
        ),
        in_specs=[pl.BlockSpec(memory_space=pltpu.HBM)] * 6,
        out_specs=(pl.BlockSpec(memory_space=pltpu.HBM),) * 13,
        scratch_shapes=[
            pltpu.VMEM((GRAD_ROWS, D), LOW),
            pltpu.VMEM((6, D, D), F32),
            pltpu.VMEM((docs * rows, D), LOW),
            pltpu.VMEM((docs * rows, D), F32),
            pltpu.VMEM((docs * slots, D), LOW),
            pltpu.VMEM((docs * slots, D), F32),
            pltpu.VMEM((docs * rows, D), LOW),
            pltpu.VMEM((docs * slots, D), LOW),
            pltpu.VMEM((8, D), F32),
            pltpu.SemaphoreType.DMA((GRAD_ROWS // D,)),
            pltpu.SemaphoreType.DMA((6 + 5,)),
            pltpu.SemaphoreType.DMA((5,)),
        ],
        compiler_params=pltpu.CompilerParams(vmem_limit_bytes=VMEM_BYTES),
    )(*parts)
    results = list(results)
    for k in (0, 2):
        results[k] = results[k].reshape(docs, rows, D)
    for k in (1, 3):
        results[k] = results[k].reshape(docs, slots, D)
    results[12] = results[12][:5]
    return tuple(results)


def solution(mesh):
    row, slot, whole = P("docs", "seq", None), P("docs", None, None), P()
    return jax.shard_map(
        on_device,
        mesh=mesh,
        in_specs=(row, slot, P("docs"), P("docs")) + (whole,) * 9 + (row, slot),
        out_specs=(row, slot, row, slot) + (whole,) * 9,
        check_vma=False,
    )
```

```python
import functools
import types

import jax
import jax.numpy as jnp
from jax import lax
from jax.experimental import pallas as pl
from jax.experimental.pallas import tpu as pltpu
from jax.sharding import PartitionSpec as P

MESH = pl.DeviceIdType.MESH
F32, LOW = jnp.float32, jnp.bfloat16
VMEM_BYTES = 63 << 20
D = 512
HD = 64
SEG = 512
SHUT = -1e30
SCALE = HD ** (-0.5)

CORE, X, Y, Z0, Z1 = ("seq", 1), ("seq", 2), ("docs", 1), ("docs", 2), ("docs", 4)
ORDERS = dict(
    X=(CORE, X, Y, Z0, Z1), Y=(CORE, Y, X, Z0, Z1), Z=(CORE, Z0, Z1, X, Y), U=(CORE, Y, Z0, Z1, X),
    V=(CORE, X, Z0, Z1, Y), T=(CORE, Z0, Z1, Y, X), A=(CORE, Z0, X, Y, Z1), B=(CORE, Z0, Y, X, Z1),
)
UNITS = {
    "Wa": (0, 1024, "X"),
    "Wb": (1024, 1024, "A"),
    "F0a": (2048, 1024, "Y"),
    "F1a": (3072, 1024, "X"),
    "F2a": (4096, 1024, "Z"),
    "F3a": (5120, 512, "A"),
    "F3b": (5632, 512, "U"),
    "Xa": (6144, 1024, "Y"),
    "Xb": (7168, 512, "X"),
    "Xc": (7680, 512, "Y"),
    "Sa": (8192, 512, "B"),
    "Qa": (8704, 512, "X"),
    "Qb": (9216, 512, "Y"),
    "Qc": (9728, 512, "Y"),
}
SCHEDULE = (
    ("Wb", "Wa",),
    (),
    ("F0a", "Wb",),
    ("Wa",),
    ("F1a", "F0a",),
    (),
    ("F2a", "F1a",),
    (),
    ("F3b", "F3a", "F2a",),
    (),
    (),
    ("Wb", "F3b", "F3a", "Wa", "F0a",),
    (),
    ("Xb", "Xc", "Xa",),
    ("Sa", "Xb", "Xc",),
    ("F2a", "Sa", "Xa", "F3b", "F1a",),
    (),
    ("F3a", "Wb", "Wa",),
    (),
    (),
    ("Xc", "F0a",),
    (),
    (),
    ("Qa", "Qb", "Qc", "F2a", "Sa", "Xb", "F3b", "F3a", "Qa", "Qb", "Qc", "Wa", "Xc", "Xa",),
    ("F0a", "F2a", "F3b", "F1a",),
    ("Xc", "Wa", "Wb", "Qa",),
    (
        "gains", "Sa", "F0a", "F1a", "Xb", "Xc", "Xa", "F3a", "Wa", "Wb", "Xb", "Qb", "gains", "F0a", "Xa",
        "F1a", "Xc", "F3b", "Qc", "Wa", "F3a", "F2a", "Wb", "Sa", "gains", "Qa", "Xb", "F0a", "Qb", "F3b",
        "Xa", "Xc", "Qc", "Wa", "F1a", "F2a", "gains", "F3a", "Qa", "Sa", "Qb", "Wb", "Xb", "F0a", "F3b",
        "F3a", "Xc", "Qc", "gains", "Xa", "F1a", "Qa", "Sa", "Qb", "Xb", "F3b", "Qc", "Wa", "F0a", "Xa",
        "gains", "F2a", "Qa", "Qb", "Wa", "F0a", "Qc", "Xc", "Wb", "Xc", "F3a", "Sa", "F1a", "Qa", "Qb",
        "Xb", "Qc", "Xa", "F2a", "F3b", "Sa", "F3b", "Qa", "Wb", "F1a", "Wb", "Qb", "F1a", "F3a", "F3a",
        "Xb", "Xa", "Qc", "Xb", "Xa", "Qb", "F2a", "Qa", "Qb", "F2a", "Qa", "Qc", "Sa", "Qc", "Sa",
    ),
)
GROUP = 8


def place_of(stage):
    axis, stride = stage
    index = lax.axis_index(axis)
    bit = lax.rem(lax.div(index, stride), 2)
    return bit, {axis: index + stride * (1 - 2 * bit)}


def outer_partners(docs_count):
    index = lax.axis_index("docs")
    return [{"docs": lax.rem(index + GROUP * k, docs_count)} for k in range(1, docs_count // GROUP)]


def partners_of(docs_count):
    return [place_of(stage)[1] for stage in ORDERS["X"]] + outer_partners(docs_count)


BLOCK = dict(
    writer_qkv=0, writer_out=3, ffn=4, cross_out=12, cross_qkv=13, self_out=16, self_qkv=17,
)
GRAD_ROWS = 20 * 512
STAGES = 5


class Summer:
    def __init__(self, r, docs_count, share):
        self.r, self.share, self.docs_count = r, share, docs_count
        self.index = {name: k for k, name in enumerate(UNITS)}
        self.at = {}

    def remote(self, source, target, name, j, partner):
        k = self.index[name]
        return pltpu.make_async_remote_copy(
            src_ref=source, dst_ref=target, send_sem=self.r.unit_s.at[k], recv_sem=self.r.unit_r.at[k, j],
            device_id=partner, device_id_type=MESH,
        )

    def other(self, source, target, sems, k, j, partner):
        return pltpu.make_async_remote_copy(
            src_ref=source, dst_ref=target, send_sem=sems[0].at[k, j], recv_sem=sems[1].at[k, j],
            device_id=partner, device_id_type=MESH,
        )

    def give(self, name, j, start, size):
        r = self.r
        base, rows, order = UNITS[name]
        bit, partner = place_of(ORDERS[order][j])
        half = size // 2
        first = base + rows - size
        copy = self.remote(
            r.grad.at[rows_at(start + (1 - bit) * half, half)], r.landed.at[pl.ds(first, half)],
            name, j, partner,
        )
        copy.start()
        self.at[name] = ("give", j, copy, start + bit * half, half, first)

    def spread(self, name, j, start, size):
        r = self.r
        bit, partner = place_of(ORDERS[UNITS[name][2]][j])
        here = rows_at(start, size)
        source = r.grad if j == STAGES - 1 else r.grads
        copy = self.remote(source.at[here], r.grads.at[here], name, 2 * STAGES - 1 - j, partner)
        copy.start()
        self.at[name] = ("spread", j, copy, start - bit * size, 2 * size, None)

    def own(self, name, start, size):
        here = rows_at(start, size)
        return pltpu.make_async_copy(
            self.r.grad.at[here], self.r.grads.at[here], self.r.own_sem.at[self.index[name]]
        )

    def step(self, name):
        r = self.r
        if name == "gains":
            return self.step_gains()
        if name not in self.at:
            base, rows, order = UNITS[name]
            return self.give(name, 0, base, rows)
        kind, j, copy, start, size, first = self.at[name]
        copy.wait()
        if kind == "give":
            add_rows(r.grad, start, size, r.landed, first, self.share if j == 0 else None)
            if j + 1 < STAGES:
                return self.give(name, j + 1, start, size)
            self.outer(name, start, size)
            store = self.own(name, start, size)
            store.start()
            self.spread(name, j, start, size)
            self.store = getattr(self, "store", {})
            self.store[name] = store
        else:
            if j == STAGES - 1:
                self.store[name].wait()
            if j > 0:
                self.spread(name, j - 1, start, size)
            else:
                self.at[name] = None

    def outer(self, name, start, size):
        others = outer_partners(self.docs_count)
        if not others:
            return
        r = self.r
        mine = lax.div(lax.axis_index("docs"), GROUP)
        here = rows_at(start, size)
        share = pl.ds(UNITS[name][0] // 32, size)
        r.outer[mine, share, :] = r.grad[here, :]
        copies = [
            self.other(
                r.grad.at[here], r.outer.at[mine, share], (r.outer_s, r.outer_r), self.index[name], k, partner
            )
            for k, partner in enumerate(others)
        ]
        for copy in copies:
            copy.start()
        for copy in copies:
            copy.wait()
        parts = [r.outer[k, share, :].astype(F32) for k in range(len(others) + 1)]
        r.grad[here, :] = sum(parts).astype(LOW)

    def step_gains(self):
        r = self.r
        j = self.at.get("gains", 0)
        if j > 0:
            self.gain_copy(j - 1).wait()
            more = r.gain_landed[j - 1]
            if j == 1:
                more = more * self.share
            r.gain_steps[j] = r.gain_steps[j - 1] + more
        if j < STAGES:
            self.gain_copy(j).start()
        else:
            others = outer_partners(self.docs_count)
            if others:
                mine = lax.div(lax.axis_index("docs"), GROUP)
                r.gain_outer[mine] = r.gain_steps[j]
                copies = [
                    self.other(r.gain_steps.at[j], r.gain_outer.at[mine], (r.gain_os, r.gain_or), 0, k, partner)
                    for k, partner in enumerate(others)
                ]
                for copy in copies:
                    copy.start()
                for copy in copies:
                    copy.wait()
                r.gain_steps[j] = sum(r.gain_outer[k] for k in range(len(others) + 1))
        self.at["gains"] = j + 1

    def gain_copy(self, j):
        r = self.r
        partner = place_of(ORDERS["X"][j])[1]
        return self.other(r.gain_steps.at[j], r.gain_landed.at[j], (r.gain_s, r.gain_r), 0, j, partner)


def add_rows(total, start, rows, landed, first, share=None):
    tile = min(rows, 128)

    def turn(t, carry):
        here = rows_at(start + t * tile, tile)
        more = landed[rows_at(first + t * tile, tile), :].astype(F32)
        if share is not None:
            more = more * share
        total[here, :] = (total[here, :].astype(F32) + more).astype(total.dtype)
        return carry

    lax.fori_loop(0, rows // tile, turn, 0)


def dot(left, right, left_dim, right_dim):
    return lax.dot_general(
        left, right, (((left_dim,), (right_dim,)), ((), ())), preferred_element_type=F32
    )


def nn(left, right):
    return dot(left, right, 1, 0)


def nt(left, right):
    return dot(left, right, 1, 1)


def tn(left, right):
    return dot(left, right, 0, 0)


def tiles(rows, tile, body):
    def turn(t, carry):
        body(pl.ds(pl.multiple_of(t * tile, tile), tile), t)
        return carry

    lax.fori_loop(0, rows // tile, turn, 0)


def rows_at(start, size):
    return pl.ds(pl.multiple_of(start, 16), size)


def norm_rows(values, gain_row):
    centered = values - jnp.mean(values, axis=-1, keepdims=True)
    inverse = lax.rsqrt(jnp.mean(centered * centered, axis=-1, keepdims=True) + 1e-05)
    unit = centered * inverse
    return (unit * gain_row).astype(LOW), unit, inverse


def norm_back(grad, unit, inverse, gain_row):
    scaled = grad * gain_row
    adjusted = (
        scaled
        - jnp.mean(scaled, axis=-1, keepdims=True)
        - unit * jnp.mean(scaled * unit, axis=-1, keepdims=True)
    )
    return adjusted * inverse


def same_head():
    left = lax.div(lax.broadcasted_iota(jnp.int32, (256, 256), 0), HD)
    right = lax.div(lax.broadcasted_iota(jnp.int32, (256, 256), 1), HD)
    return left == right


def four_heads(values):
    return jnp.where(same_head(), jnp.concatenate([values] * 4, axis=0), 0.0)


def own_blocks(values):
    return jnp.sum(jnp.where(same_head(), values, 0.0).reshape(4, HD, 256), axis=0)


def swap(values):
    return own_blocks(four_heads(values).T)


def head_stack(values):
    low_half = lax.broadcasted_iota(jnp.int32, values.shape, 1) < HD
    return jnp.concatenate(
        [jnp.where(low_half, values, 0.0), jnp.where(low_half, 0.0, values)], axis=0
    )


def head_pick(values):
    first_head = lax.broadcasted_iota(jnp.int32, (128, 128), 1) < HD
    return jnp.where(first_head, values[:128], values[128:])


BLOCKS = SEG // 128
BLOCK_ROWS = [sum(128 * (k + 1) for k in range(i)) for i in range(BLOCKS + 1)]
PAIRS = D // 128

WEIGHTS = (
    "self_qkv", "cross_qkv", "writer_qkv", "writer_out", "self_out", "cross_out", "ffn_in", "ffn_out",
)
INPUTS = (
    "x", "memory", "lengths", "seg_index", "self_qkv", "self_out", "cross_qkv", "cross_out",
    "ffn_in", "ffn_out", "writer_qkv", "writer_out", "gains", "out_cot", "mem_cot",
)
OUTPUTS = ("enc_out", "new_memory", "input_grad", "memory_grad", "grads", "gains_grad")
def scratch_of(docs, rows, slots, weights, docs_count):
    keys = SEG + slots
    units, outers = len(UNITS), max(1, docs_count // GROUP)
    dma = pltpu.SemaphoreType.DMA
    low = lambda *shape: pltpu.VMEM(shape, LOW)
    full = lambda *shape: pltpu.VMEM(shape, F32)
    fetched = {"w_" + name: pltpu.VMEM(weights[name].shape, LOW) for name in WEIGHTS}
    return dict(
        **fetched,
        mem=low(slots, D),
        mem_back=low(slots, D),
        gain_rows=full(5, D),
        x_all=low(SEG, D),
        cot_all=low(SEG, D),
        enc=low(SEG, D),
        slot_grad=low(slots, D),
        new_slots=low(slots, D),
        unit0=full(SEG, D),
        unit1=full(SEG, D),
        unit2=full(SEG, D),
        unit4=full(SEG, D),
        unit3=full(slots, D),
        inv0=full(SEG, 1),
        inv1=full(SEG, 1),
        inv2=full(SEG, 1),
        inv4=full(SEG, 1),
        inv3=full(slots, 1),
        h0=low(SEG, D),
        h1=low(SEG, D),
        h2=low(SEG, D),
        src=low(keys, D),
        q=low(SEG, D),
        k=low(SEG, D),
        v=low(SEG, D),
        prob=low(PAIRS, BLOCK_ROWS[-1], 256),
        mix=low(SEG, D),
        inv_total=full(SEG, D),
        acc=full(SEG, D),
        res=full(SEG, D),
        cq=low(SEG, D),
        cross_k=low(2, 256, 256),
        cross_v=low(2, 256, 256),
        cross_p=low(2, 256, SEG),
        co=low(SEG, D),
        z=low(4, SEG, D),
        slope=low(4, SEG, D),
        wkey=low(keys, D),
        wvalue=low(keys, D),
        wquery=low(2, 256, 256),
        dmix=low(2, 256, 256),
        wo=low(slots, D),
        dwq=low(slots, D),
        dck=low(slots, D),
        dcv=low(slots, D),
        low=low(SEG, D),
        dsend=low(SEG, D),
        delta=full(16, SEG),
        dk_sum=full(SEG, 128),
        dv_sum=full(SEG, 128),
        gain_sum=full(5, 8, D),
        gain_steps=full(STAGES + 1, 8, D),
        gain_landed=full(STAGES, 8, D),
        gain_outer=full(outers, 8, D),
        grad=low(GRAD_ROWS, D),
        landed=low(GRAD_ROWS, D),
        outer=low(outers, GRAD_ROWS // 32, D),
        unit_s=dma((units,)),
        unit_r=dma((units, 2 * STAGES)),
        own_sem=dma((units,)),
        outer_s=dma((units if outers > 1 else 1, outers)),
        outer_r=dma((units if outers > 1 else 1, outers)),
        gain_s=dma((1, STAGES)),
        gain_r=dma((1, STAGES)),
        gain_os=dma((1, outers)),
        gain_or=dma((1, outers)),
        load_sem=dma((len(WEIGHTS) + 5,)),
        xs=dma((3,)),
        xr=dma((3,)),
        cs=dma((3,)),
        cr=dma((3,)),
        es=dma((3,)),
        er=dma((3,)),
        us=dma((3,)),
        ur=dma((3,)),
        gs=dma((3,)),
        gr=dma((3,)),
        ms=dma((3,)),
        mr=dma((3,)),
        out_sem=dma((5,)),
    )


def layer_kernel(docs, rows, slots, docs_count, names, *refs):
    r = types.SimpleNamespace(**dict(zip(names, refs)))
    s = lax.axis_index("seq")
    bit0, bit1 = lax.rem(s, 2), lax.div(s, 2)
    near = s + 1 - 2 * bit0
    far = s + 2 - 4 * bit1
    across = near + 2 - 4 * bit1
    peers = (near, far, across)

    def doc_of(index):
        return jnp.minimum(index, docs - 1)

    mine = doc_of(s)

    def remote(source, target, send_sem, recv_sem, to):
        return pltpu.make_async_remote_copy(
            src_ref=source, dst_ref=target, send_sem=send_sem, recv_sem=recv_sem,
            device_id={"seq": to}, device_id_type=MESH,
        )

    def gain(k):
        return r.gain_rows[k : k + 1, :]

    def add_gain(k, values):
        r.gain_sum[k] += jnp.sum(values.reshape(-1, 8, D), axis=0)

    barrier = pltpu.get_barrier_semaphore()
    greeted = [{"seq": across}] + partners_of(docs_count)
    for partner in greeted:
        pl.semaphore_signal(barrier, inc=1, device_id=partner, device_id_type=MESH)
    own_rows = rows_at(s * rows, rows)
    doc_rows, doc_slots = rows_at(mine * rows, rows), rows_at(mine * slots, slots)
    fetched = dict(
        mem=(r.memory.at[doc_slots], r.mem),
        gains=(r.gains, r.gain_rows),
        x=(r.x.at[doc_rows], r.x_all.at[own_rows]),
        mem_cot=(r.mem_cot.at[doc_slots], r.mem_back),
        **{name: (getattr(r, name), getattr(r, "w_" + name)) for name in WEIGHTS},
        cot=(r.out_cot.at[doc_rows], r.cot_all.at[own_rows]),
    )
    loads = {}
    for k, (name, (source, target)) in enumerate(fetched.items()):
        loads[name] = pltpu.make_async_copy(source, target, r.load_sem.at[k])
        loads[name].start()
    r.gain_sum[...] = jnp.zeros_like(r.gain_sum)
    loads["mem"].wait()
    loads["gains"].wait()
    slot_range = pl.ds(SEG, slots)
    hm, r.unit3[...], r.inv3[...] = norm_rows(r.mem[...].astype(F32), gain(3))
    r.src[slot_range, :] = hm
    pl.semaphore_wait(barrier, len(greeted))

    def gather_copy(source, target, send_sem, recv_sem, k):
        return remote(
            source.at[rows_at(doc_of(peers[k]) * rows, rows)],
            target.at[rows_at(s * rows, rows)], send_sem.at[k], recv_sem.at[k], peers[k],
        )

    for k in range(3):
        gather_copy(r.x, r.x_all, r.xs, r.xr, k).start()

    def spread_copy(source, target, size, own, send_sem, recv_sem, k):
        piece = source.at[rows_at(peers[k] * size, size)] if own else source
        return remote(
            piece, target.at[rows_at(mine * size, size)], send_sem.at[k], recv_sem.at[k], peers[k]
        )

    def keep_copy(k, source, target, size, own, *sems):
        piece = source.at[rows_at(s * size, size)] if own else source
        return pltpu.make_async_copy(piece, target.at[rows_at(mine * size, size)], r.out_sem.at[k])

    summer = Summer(r, docs_count, 1.0 - bit1.astype(F32))
    ticks = iter(SCHEDULE)

    def tick():
        for name in next(ticks):
            summer.step(name)

    def spread(*where):
        spread_copy(*where, 1).start()

        @pl.when(bit1 == 0)
        def _():
            spread_copy(*where, 0).start()
            spread_copy(*where, 2).start()

    def spread_wait(*where):
        spread_copy(*where, 1).wait()

        @pl.when(bit1 == 0)
        def _():
            spread_copy(*where, 0).wait()
            spread_copy(*where, 2).wait_send()

        @pl.when(bit1 == 1)
        def _():
            spread_copy(*where, 2).wait_recv()

    def place_heads(target, values):
        for g in range(2):
            piece = values[:, g * 256 : (g + 1) * 256].astype(LOW).astype(F32)
            target[g] = four_heads(piece).astype(LOW)

    loads["cross_qkv"].wait()
    place_heads(r.cross_k, nn(hm, r.w_cross_qkv[1]))
    place_heads(r.cross_v, nn(hm, r.w_cross_qkv[2]))
    loads["writer_qkv"].wait()
    r.wkey[slot_range, :] = nn(hm, r.w_writer_qkv[1]).astype(LOW)
    r.wvalue[slot_range, :] = nn(hm, r.w_writer_qkv[2]).astype(LOW)
    place_heads(r.wquery, nn(hm, r.w_writer_qkv[0]) * SCALE)
    loads["writer_out"].wait()
    loads["mem_cot"].wait()
    mem_cot = r.mem_back[...]
    place_heads(r.dmix, nt(mem_cot, r.w_writer_out[...]))

    def enter(start):
        here = rows_at(start, SEG // 2)
        normed, unit, inverse = norm_rows(r.x_all[here, :].astype(F32), gain(0))
        r.unit0[here, :] = unit
        r.inv0[here, :] = inverse
        r.h0[here, :] = normed
        r.q[here, :] = (nn(normed, r.w_self_qkv[0]) * SCALE).astype(LOW)
        r.k[here, :] = nn(normed, r.w_self_qkv[1]).astype(LOW)
        r.v[here, :] = nn(normed, r.w_self_qkv[2]).astype(LOW)

    loads["x"].wait()
    loads["self_qkv"].wait()
    gather_copy(r.x, r.x_all, r.xs, r.xr, 0).wait_recv()
    enter(bit1 * (SEG // 2))
    for k in (1, 2):
        gather_copy(r.x, r.x_all, r.xs, r.xr, k).wait_recv()
    for k in range(3):
        gather_copy(r.out_cot, r.cot_all, r.cs, r.cr, k).start()
    enter((1 - bit1) * (SEG // 2))
    for k in range(3):
        gather_copy(r.x, r.x_all, r.xs, r.xr, k).wait_send()
    live = jnp.minimum(r.lengths[mine] - r.seg_index[mine] * SEG, SEG)

    ones = jnp.ones((SEG, 128), LOW)
    for p in range(PAIRS):
        columns = slice(p * 128, (p + 1) * 128)
        for i in range(BLOCKS):
            depth = 128 * (i + 1)
            here = slice(i * 128, (i + 1) * 128)
            stacked = head_stack(r.q[here, columns].astype(F32)).astype(LOW)
            scores = nt(r.k[:depth, columns], stacked)
            key_pos = lax.broadcasted_iota(jnp.int32, scores.shape, 0)
            query_pos = i * 128 + lax.rem(lax.broadcasted_iota(jnp.int32, scores.shape, 1), 128)
            scores = jnp.where((key_pos <= query_pos) & (key_pos < live), scores, SHUT)
            powers = jnp.exp(scores - jnp.max(scores, axis=0, keepdims=True)).astype(LOW)
            r.prob[p, BLOCK_ROWS[i] : BLOCK_ROWS[i + 1], :] = powers
            mixed = tn(powers, jnp.concatenate([r.v[:depth, columns], ones[:depth]], axis=1))
            inverse = 1.0 / head_pick(mixed[:, 128:])
            r.inv_total[here, columns] = inverse
            r.mix[here, columns] = (head_pick(mixed[:, :128]) * inverse).astype(LOW)

    loads["self_out"].wait()
    total = r.x_all[...].astype(F32) + nn(r.mix[...], r.w_self_out[...])
    r.res[...] = total
    r.h1[...], r.unit1[...], r.inv1[...] = norm_rows(total, gain(1))
    r.cq[...] = (nn(r.h1[...], r.w_cross_qkv[0]) * SCALE).astype(LOW)

    for g in range(2):
        columns = slice(g * 256, (g + 1) * 256)
        scores = nt(r.cross_k[g], r.cq[:, columns]).reshape(4, slots, SEG)
        powers = jnp.exp(scores - jnp.max(scores, axis=1, keepdims=True))
        inverse = 1.0 / jnp.sum(powers, axis=1, keepdims=True)
        r.cross_p[g] = (powers * inverse).reshape(256, SEG).astype(LOW)
        r.co[:, columns] = tn(r.cross_p[g], r.cross_v[g]).astype(LOW)

    loads["cross_out"].wait()
    total = r.res[...] + nn(r.co[...], r.w_cross_out[...])
    r.res[...] = total
    r.h2[...], r.unit2[...], r.inv2[...] = norm_rows(total, gain(2))

    rate, cube = 0.7978845608028654, 0.044715
    loads["ffn_in"].wait()
    loads["ffn_out"].wait()

    for c in range(4):
        columns = slice(c * D, (c + 1) * D)
        u = nn(r.h2[...], r.w_ffn_in[:, columns])
        square = u * u
        bend = jnp.tanh(rate * u * (1.0 + cube * square))
        half = 0.5 * (1.0 + bend)
        r.z[c] = (u * half).astype(LOW)
        slope = half + (0.5 * rate) * u * (1.0 - bend * bend) * (1.0 + 3.0 * cube * square)
        r.slope[c] = slope.astype(LOW)
        r.res[...] += nn(r.z[c], r.w_ffn_out[columns, :])

    total = r.res[...]
    r.enc[...] = total.astype(LOW)
    r.src[:SEG, :], r.unit4[...], r.inv4[...] = norm_rows(total, gain(4))
    enc_way = (r.enc, r.enc_out, rows, True, r.es, r.er)
    spread(*enc_way)
    keep_copy(0, *enc_way).start()

    written = r.src[:SEG, :]
    r.wkey[:SEG, :] = nn(written, r.w_writer_qkv[1]).astype(LOW)
    r.wvalue[:SEG, :] = nn(written, r.w_writer_qkv[2]).astype(LOW)
    for g in range(2):
        columns = slice(g * 256, (g + 1) * 256)
        keys = r.wkey[:, columns]
        scores = nt(keys, r.wquery[g])
        key_pos = lax.broadcasted_iota(jnp.int32, scores.shape, 0)
        scores = jnp.where((key_pos >= SEG) | (key_pos < live), scores, SHUT)
        powers = jnp.exp(scores - jnp.max(scores, axis=0, keepdims=True))
        probs = powers * (1.0 / jnp.sum(powers, axis=0, keepdims=True))
        probs_low = probs.astype(LOW)
        mixed = own_blocks(tn(r.wvalue[:, columns], probs_low)).astype(LOW).astype(F32)
        r.wo[:, columns] = swap(mixed).astype(LOW)
        dprobs = nt(r.wvalue[:, columns], r.dmix[g])
        delta = jnp.sum(probs * dprobs, axis=0, keepdims=True)
        slopes = (probs * (dprobs - delta)).astype(LOW)
        dquery = own_blocks(tn(slopes, keys)).astype(LOW).astype(F32)
        r.dwq[:, columns] = (dquery * SCALE).astype(LOW)
        r.wkey[:, columns] = nn(slopes, r.wquery[g]).astype(LOW)
        r.wvalue[:, columns] = nn(probs_low, r.dmix[g]).astype(LOW)

    r.new_slots[...] = (
        r.mem[...].astype(F32) + nn(r.wo[...], r.w_writer_out[...])
    ).astype(LOW)
    new_way = (r.new_slots, r.new_memory, slots, False, r.us, r.ur)
    spread(*new_way)
    keep_copy(1, *new_way).start()

    def put(block, values):
        r.grad[block * D : (block + 1) * D, :] = values.astype(LOW)

    grad = nt(r.wkey[:SEG, :], r.w_writer_qkv[1]) + nt(r.wvalue[:SEG, :], r.w_writer_qkv[2])
    loads["cot"].wait()
    for k in range(3):
        gather_copy(r.out_cot, r.cot_all, r.cs, r.cr, k).wait()
    add_gain(4, grad * r.unit4[...])
    total = r.cot_all[...].astype(F32) + norm_back(grad, r.unit4[...], r.inv4[...], gain(4))
    r.res[...] = total
    r.low[...] = total.astype(LOW)
    put(BLOCK["writer_qkv"], tn(hm, r.dwq[...]))
    put(BLOCK["writer_qkv"] + 1, tn(r.src[...], r.wkey[...]))
    put(BLOCK["writer_qkv"] + 2, tn(r.src[...], r.wvalue[...]))
    put(BLOCK["writer_out"], tn(r.wo[...], mem_cot))
    tick()

    for c in range(4):
        columns = slice(c * D, (c + 1) * D)
        put(BLOCK["ffn"] + 2 * c, tn(r.z[c], r.low[...]))
        tick()
        r.z[c] = (nt(r.low[...], r.w_ffn_out[columns, :]) * r.slope[c].astype(F32)).astype(LOW)
        put(BLOCK["ffn"] + 2 * c + 1, tn(r.h2[...], r.z[c]))
        back = nt(r.z[c], r.w_ffn_in[:, columns])
        r.acc[...] = back if c == 0 else r.acc[...] + back
        tick()

    grad, unit = r.acc[...], r.unit2[...]
    add_gain(2, grad * unit)
    total = r.res[...] + norm_back(grad, unit, r.inv2[...], gain(2))
    r.res[...] = total
    r.low[...] = total.astype(LOW)
    tick()

    r.dsend[...] = nt(r.low[...], r.w_cross_out[...]).astype(LOW)
    put(BLOCK["cross_out"], tn(r.co[...], r.low[...]))
    tick()
    for g in range(2):
        columns = slice(g * 256, (g + 1) * 256)
        dmix, queries = r.dsend[:, columns], r.cq[:, columns]
        dprobs = nt(r.cross_v[g], dmix)
        probs = r.cross_p[g].astype(F32)
        delta = jnp.sum((probs * dprobs).reshape(4, slots, SEG), axis=1, keepdims=True)
        slopes = (probs * (dprobs.reshape(4, slots, SEG) - delta).reshape(256, SEG)).astype(LOW)
        r.dck[:, columns] = own_blocks(nn(slopes, queries)).astype(LOW)
        r.dcv[:, columns] = own_blocks(nn(r.cross_p[g], dmix)).astype(LOW)
        r.cq[:, columns] = (tn(slopes, r.cross_k[g]).astype(LOW).astype(F32) * SCALE).astype(LOW)
    tick()
    r.acc[...] = nt(r.cq[...], r.w_cross_qkv[0])

    grad, unit = r.acc[...], r.unit1[...]
    add_gain(1, grad * unit)
    total = r.res[...] + norm_back(grad, unit, r.inv1[...], gain(1))
    r.res[...] = total
    r.low[...] = total.astype(LOW)
    tick()
    put(BLOCK["cross_qkv"], tn(r.h1[...], r.cq[...]))
    put(BLOCK["cross_qkv"] + 1, tn(hm, r.dck[...]))
    put(BLOCK["cross_qkv"] + 2, tn(hm, r.dcv[...]))
    tick()

    dmix = nt(r.low[...], r.w_self_out[...]).astype(LOW).astype(F32) * r.inv_total[...]
    r.dsend[...] = dmix.astype(LOW)
    product = dmix * r.mix[...].astype(F32)
    upper = product.astype(LOW)
    lower = (product - upper.astype(F32)).astype(LOW)
    head_rows = lax.div(lax.broadcasted_iota(jnp.int32, (16, D), 1), HD)
    head_rows = (head_rows == lax.broadcasted_iota(jnp.int32, (16, D), 0)).astype(F32).astype(LOW)
    r.delta[...] = nt(head_rows, upper) + nt(head_rows, lower)
    put(BLOCK["self_out"], tn(r.mix[...], r.low[...]))
    tick()

    for p in range(PAIRS):
        columns = slice(p * 128, (p + 1) * 128)
        r.dk_sum[...] = jnp.zeros_like(r.dk_sum)
        r.dv_sum[...] = jnp.zeros_like(r.dv_sum)
        for i in range(BLOCKS):
            depth = 128 * (i + 1)
            here = slice(i * 128, (i + 1) * 128)
            stacked = head_stack(r.dsend[here, columns].astype(F32)).astype(LOW)
            queries = head_stack(r.q[here, columns].astype(F32)).astype(LOW)
            probs = r.prob[p, BLOCK_ROWS[i] : BLOCK_ROWS[i + 1], :]
            dprobs = nt(r.v[:depth, columns], stacked)
            delta = jnp.concatenate([r.delta[2 * p + h : 2 * p + h + 1, here] for h in range(2)], axis=1)
            slopes = (probs.astype(F32) * (dprobs - delta)).astype(LOW)
            r.dk_sum[:depth, :] += nn(slopes, queries)
            r.dv_sum[:depth, :] += nn(probs, stacked)
            dquery = head_pick(tn(slopes, r.k[:depth, columns]))
            r.q[here, columns] = (dquery.astype(LOW).astype(F32) * SCALE).astype(LOW)
            if i == 2:
                tick()
        r.k[:, columns] = r.dk_sum[...].astype(LOW)
        r.v[:, columns] = r.dv_sum[...].astype(LOW)
        tick()
    for k, grad in enumerate((r.q, r.k, r.v)):
        put(BLOCK["self_qkv"] + k, tn(r.h0[...], grad[...]))
    tick()
    r.acc[...] = (
        nt(r.q[...], r.w_self_qkv[0]) + nt(r.k[...], r.w_self_qkv[1]) + nt(r.v[...], r.w_self_qkv[2])
    )
    spread_wait(*enc_way)
    keep_copy(0, *enc_way).wait()

    grad, unit = r.acc[...], r.unit0[...]
    add_gain(0, grad * unit)
    total = r.res[...] + norm_back(grad, unit, r.inv0[...], gain(0))
    r.enc[...] = total.astype(LOW)
    grad_way = (r.enc, r.input_grad, rows, True, r.gs, r.gr)
    spread(*grad_way)
    keep_copy(2, *grad_way).start()
    tick()

    dhm = (
        nt(r.dwq[...], r.w_writer_qkv[0])
        + nt(r.wkey[slot_range, :], r.w_writer_qkv[1])
        + nt(r.wvalue[slot_range, :], r.w_writer_qkv[2])
        + nt(r.dck[...], r.w_cross_qkv[1])
        + nt(r.dcv[...], r.w_cross_qkv[2])
    )
    unit = r.unit3[...]
    add_gain(3, dhm * unit)
    r.slot_grad[...] = (
        mem_cot.astype(F32) + norm_back(dhm, unit, r.inv3[...], gain(3))
    ).astype(LOW)
    slot_way = (r.slot_grad, r.memory_grad, slots, False, r.ms, r.mr)
    spread(*slot_way)
    keep_copy(3, *slot_way).start()
    r.gain_steps[0] = jnp.concatenate(
        [jnp.sum(r.gain_sum[k], axis=0, keepdims=True) for k in range(5)] + [jnp.zeros((3, D), F32)], axis=0
    )
    tick()
    tick()
    last = pltpu.make_async_copy(r.gain_steps.at[STAGES], r.gains_grad, r.out_sem.at[4])
    last.start()
    last.wait()
    for k, way in enumerate((enc_way, new_way, grad_way, slot_way)):
        if k > 0:
            spread_wait(*way)
            keep_copy(k, *way).wait()


def finish_kernel(enc, new, in_grad, mem_grad, grads, gains, *refs):
    outs, (low, wide, row_low, row_wide, slot_low, slot_wide, enc_low, new_low, gain_wide, load_sem, store_sem,
           pass_sem) = refs[:13], refs[13:]
    (o_enc, o_new, o_in, o_mem, self_qkv, self_out, cross_qkv, cross_out, ffn_in, ffn_out, writer_qkv,
     writer_out, o_gains) = outs
    slots = wide.shape[0]

    def place(block):
        for name, ref in (("writer_qkv", writer_qkv), ("cross_qkv", cross_qkv), ("self_qkv", self_qkv)):
            if 0 <= block - BLOCK[name] < 3:
                return ref.at[block - BLOCK[name]]
        for name, ref in (("writer_out", writer_out), ("cross_out", cross_out), ("self_out", self_out)):
            if block == BLOCK[name]:
                return ref
        c, second = divmod(block - BLOCK["ffn"], 2)
        return (ffn_in.at[:, pl.ds(c * D, D)] if second else ffn_out.at[pl.ds(c * D, D), :])

    count = GRAD_ROWS // D
    loads = [
        pltpu.make_async_copy(grads.at[pl.ds(k * D, D)], low.at[pl.ds(k * D, D)], load_sem.at[k])
        for k in range(count)
    ]
    rest = [
        pltpu.make_async_copy(source, target, pass_sem.at[k])
        for k, (source, target) in enumerate(
            ((in_grad, row_low), (mem_grad, slot_low), (enc, enc_low), (new, new_low), (gains, gain_wide))
        )
    ]
    for copy in loads + rest:
        copy.start()
    stores = []
    for k in range(count):
        loads[k].wait()
        if k >= slots:
            stores[k - slots].wait()

        def turn(here, t):
            wide[k % slots, here, :] = low[rows_at(k * D + t * 128, 128), :].astype(F32)

        tiles(D, 128, turn)
        stores.append(pltpu.make_async_copy(wide.at[k % slots], place(k), store_sem.at[k % slots]))
        stores[k].start()
    ways = (
        (row_low, row_wide, o_in), (slot_low, slot_wide, o_mem), (enc_low, enc_low, o_enc), (new_low, new_low, o_new),
        (gain_wide, gain_wide, o_gains),
    )
    for k, (read, held, out) in enumerate(ways):
        rest[k].wait()
        if read is not held:
            held[...] = read[...].astype(F32)
        stores.append(pltpu.make_async_copy(held, out, store_sem.at[slots + k]))
        stores[-1].start()
    for copy in stores[count - slots :]:
        copy.wait()


def on_device(*arguments):
    seg_input, memory = arguments[0], arguments[1]
    docs, rows, _ = seg_input.shape
    slots = memory.shape[1]
    docs_count = lax.axis_size("docs")
    scratch = scratch_of(docs, rows, slots, dict(zip(INPUTS, arguments)), docs_count)
    smem, anywhere = pl.BlockSpec(memory_space=pltpu.SMEM), pl.BlockSpec(memory_space=pl.ANY)
    arguments = list(arguments)
    for k in (0, 1, 13, 14):
        arguments[k] = arguments[k].reshape(-1, D)
    names = INPUTS + OUTPUTS + tuple(scratch)
    low = lambda *shape: jax.ShapeDtypeStruct(shape, LOW)
    full = lambda *shape: jax.ShapeDtypeStruct(shape, F32)
    parts = pl.pallas_call(
        functools.partial(layer_kernel, docs, rows, slots, docs_count, names),
        out_shape=(
            low(docs * rows, D), low(docs * slots, D), low(docs * rows, D), low(docs * slots, D),
            low(GRAD_ROWS, D), full(8, D),
        ),
        in_specs=[
            smem if name in ("lengths", "seg_index") else anywhere for name in INPUTS
        ],
        out_specs=(anywhere,) * 6,
        scratch_shapes=list(scratch.values()),
        compiler_params=pltpu.CompilerParams(
            collective_id=1, has_side_effects=True, vmem_limit_bytes=VMEM_BYTES
        ),
    )(*arguments)
    shapes = dict(zip(INPUTS, (full(*argument.shape) for argument in arguments)))
    results = pl.pallas_call(
        finish_kernel,
        out_shape=(
            low(docs * rows, D), low(docs * slots, D), full(docs * rows, D), full(docs * slots, D),
            *(shapes[name] for name in INPUTS[4:12]), full(8, D),
        ),
        in_specs=[pl.BlockSpec(memory_space=pltpu.HBM)] * 6,
        out_specs=(pl.BlockSpec(memory_space=pltpu.HBM),) * 13,
        scratch_shapes=[
            pltpu.VMEM((GRAD_ROWS, D), LOW),
            pltpu.VMEM((6, D, D), F32),
            pltpu.VMEM((docs * rows, D), LOW),
            pltpu.VMEM((docs * rows, D), F32),
            pltpu.VMEM((docs * slots, D), LOW),
            pltpu.VMEM((docs * slots, D), F32),
            pltpu.VMEM((docs * rows, D), LOW),
            pltpu.VMEM((docs * slots, D), LOW),
            pltpu.VMEM((8, D), F32),
            pltpu.SemaphoreType.DMA((GRAD_ROWS // D,)),
            pltpu.SemaphoreType.DMA((6 + 5,)),
            pltpu.SemaphoreType.DMA((5,)),
        ],
        compiler_params=pltpu.CompilerParams(vmem_limit_bytes=VMEM_BYTES),
    )(*parts)
    results = list(results)
    for k in (0, 2):
        results[k] = results[k].reshape(docs, rows, D)
    for k in (1, 3):
        results[k] = results[k].reshape(docs, slots, D)
    results[12] = results[12][:5]
    return tuple(results)


def solution(mesh):
    row, slot, whole = P("docs", "seq", None), P("docs", None, None), P()
    return jax.shard_map(
        on_device,
        mesh=mesh,
        in_specs=(row, slot, P("docs"), P("docs")) + (whole,) * 9 + (row, slot),
        out_specs=(row, slot, row, slot) + (whole,) * 9,
        check_vma=False,
    )
```

```python
import functools
import types

import jax
import jax.numpy as jnp
from jax import lax
from jax.experimental import pallas as pl
from jax.experimental.pallas import tpu as pltpu
from jax.sharding import PartitionSpec as P

MESH = pl.DeviceIdType.MESH
F32, LOW = jnp.float32, jnp.bfloat16
VMEM_BYTES = 63 << 20
D = 512
HD = 64
SEG = 512
SHUT = -1e30
SCALE = HD ** (-0.5)

CORE, X, Y, Z0, Z1 = ("seq", 1), ("seq", 2), ("docs", 1), ("docs", 2), ("docs", 4)
SINGLE = (CORE, X, Y, Z0, Z1)
PUSH, MIDDLE = "push", "middle"
ORDERS = dict(
    X=(CORE, X, Y, PUSH, MIDDLE), Y=(CORE, Y, X, PUSH, MIDDLE), A=(CORE, Z0, X, Y, Z1), B=(CORE, Z0, Y, X, Z1),
)
UNITS = {
    "Va": (0, 1024, "Y"),
    "Wa": (1024, 1024, "X"),
    "F0a": (2048, 512, "A"),
    "F0b": (2560, 512, "B"),
    "F1a": (3072, 512, "B"),
    "F1b": (3584, 512, "A"),
    "F2a": (4096, 1024, "Y"),
    "F3a": (5120, 1024, "X"),
    "Xa": (6144, 512, "A"),
    "Xb": (6656, 512, "B"),
    "Xc": (7168, 512, "Y"),
    "Xd": (7680, 512, "X"),
    "Sa": (8192, 512, "Y"),
    "Qa": (8704, 512, "X"),
    "Qb": (9216, 512, "B"),
    "Qc": (9728, 512, "Y"),
}
SCHEDULE = (
    ("Va",),
    (),
    ("Wa", "Va",),
    (),
    ("F0a", "F0b", "Wa",),
    ("F0a", "F0b",),
    ("F1a", "F1b",),
    (),
    ("F2a", "Va", "F1a", "F1b", "F0a",),
    ("F2a", "Wa",),
    ("F3a", "F0b",),
    (),
    (),
    ("F3a", "Va", "F1a", "F0a",),
    (),
    ("Xa", "Xb", "Xd", "Xc", "F2a", "F1b", "Xa", "Xb", "Xd", "Xc",),
    ("Sa", "Va", "Wa", "F3a",),
    ("Sa", "F0b",),
    ("Xa",),
    ("F1a",),
    ("Va", "F2a", "F0a",),
    (),
    ("Xb", "F1b",),
    ("Xc",),
    (),
    ("Qb", "Qa", "Qc", "Xd", "Va", "Wa", "F3a", "F0b", "Qb", "Qa", "Qc", "Xa", "F2a",),
    ("F1a", "Wa", "Sa", "F0a", "Xb", "Va", "Xc", "F3a", "F1b", "F2a", "Qa", "Xd", "F0b",),
    (),
    (
        "gains", "Wa", "Qb", "Qc", "F1a", "Xa", "F3a", "F0a", "Qa", "Xc", "F2a", "Qb", "gains", "F1b", "Sa",
        "Wa", "Xd", "Xb", "F0a", "F0b", "F1a", "F3a", "Va", "Xa", "gains", "Xc", "Qa", "F2a", "Xd", "Wa",
        "Qc", "Sa", "F1b", "Qb", "Xb", "Xc", "gains", "Qa", "F0a", "Xd", "F3a", "F0b", "Sa", "F1a", "Qc",
        "Xa", "Va", "Qb", "gains", "Qa", "F2a", "Xb", "F1b", "Va", "Xc", "Sa", "Qc", "F3a", "F0a", "F0b",
        "gains", "F0a", "Xd", "Wa", "Qc", "F1a", "Qb", "Xa", "Xb", "Qa", "Wa", "F1b", "Sa", "Xc", "F0b",
        "F2a", "F0b", "Qc", "F2a", "Xd", "F3a", "Xb", "F1a", "Qb", "F3a", "Qa", "F1a", "Xa", "F1b", "Sa",
        "Xc", "F1b", "Qc", "Xc", "Qb", "Xb", "Xb", "Xd", "Xa", "Sa", "Xd", "Xa", "Qa", "Sa", "Qb", "Qc",
        "Qa", "Qb", "Qc",
    ),
)
GROUP = 8


def bit_of(axis, stride):
    shift = stride.bit_length() - 1
    return lax.bitwise_and(lax.shift_right_logical(lax.axis_index(axis), jnp.int32(shift)), jnp.int32(1))


def in_middle():
    return bit_of("docs", 2) != bit_of("docs", 4)


def place_of(stage):
    if stage == MIDDLE:
        low_bit, bit = bit_of("docs", 2), bit_of("docs", 4)
        return bit, {"docs": lax.axis_index("docs") + 2 * (1 - 2 * low_bit) + 4 * (1 - 2 * bit)}
    axis, stride = Z0 if stage == PUSH else stage
    bit = bit_of(axis, stride)
    return bit, {axis: lax.axis_index(axis) + stride * (1 - 2 * bit)}


def outer_partners(docs_count):
    index = lax.axis_index("docs")
    return [{"docs": lax.rem(index + GROUP * k, docs_count)} for k in range(1, docs_count // GROUP)]


def outer_bits(docs_count):
    return (docs_count // GROUP).bit_length() - 1


def partners_of(docs_count):
    return [place_of(stage)[1] for stage in SINGLE + (MIDDLE,)] + outer_partners(docs_count)


BLOCK = dict(
    writer_kv=0, writer_q=2, writer_out=3, ffn=4, cross_out=12, cross_qkv=13, self_out=16, self_qkv=17,
)
GRAD_ROWS = 20 * 512
STAGES = 5
LANDING, LANDED_ROWS = {}, 0
for _name, (_base, _rows, _order) in UNITS.items():
    LANDING[_name] = LANDED_ROWS
    LANDED_ROWS += _rows + (_rows // 16 if PUSH in ORDERS[_order] else 0)


class Summer:
    def __init__(self, r, docs_count, share):
        self.r, self.share, self.docs_count = r, share, docs_count
        self.index = {name: k for k, name in enumerate(UNITS)}
        self.at, self.store = {}, {}
        self.middle = in_middle()
        self.edge = jnp.logical_not(self.middle)
        self.places = {stage: place_of(stage) for stage in SINGLE + (PUSH, MIDDLE)}

    def remote(self, source, target, name, j, partner):
        k = self.index[name]
        return pltpu.make_async_remote_copy(
            src_ref=source, dst_ref=target, send_sem=self.r.unit_s.at[k], recv_sem=self.r.unit_r.at[k, j],
            device_id=partner, device_id_type=MESH,
        )

    def other(self, source, target, sems, k, j, partner):
        return pltpu.make_async_remote_copy(
            src_ref=source, dst_ref=target, send_sem=sems[0].at[k, j], recv_sem=sems[1].at[k, j],
            device_id=partner, device_id_type=MESH,
        )

    def only(self, inside, body):
        if inside:
            pl.when(self.middle)(body)
        else:
            body()

    def lined(self, name):
        return PUSH in ORDERS[UNITS[name][2]]

    def give(self, name, j, start, size, first):
        r = self.r
        stage = ORDERS[UNITS[name][2]][j]
        bit, partner = self.places[stage]
        if stage == PUSH:
            half, sent, kept = size, start, start
        else:
            half = size // 2
            sent, kept = start + (1 - bit) * half, start + bit * half
        copy = self.remote(
            r.grad.at[rows_at(sent, half)], r.landed.at[pl.ds(first, half)], name, j, partner
        )
        if stage == PUSH:
            pl.when(self.edge)(copy.start)
        else:
            self.only(stage == MIDDLE, copy.start)
        self.at[name] = ("give", j, copy, kept, half, first)

    def given(self, name, j, copy, start, size, first):
        stage = ORDERS[UNITS[name][2]][j]

        def add():
            add_rows(self.r.grad, start, size, self.r.landed, first, self.share if j == 0 else None)

        if stage == PUSH:

            @pl.when(self.middle)
            def _():
                copy.wait_recv()
                add()

            pl.when(self.edge)(copy.wait_send)
        else:

            def both():
                copy.wait()
                add()

            self.only(stage == MIDDLE, both)

    def spread(self, name, j, start, size):
        r = self.r
        stage = ORDERS[UNITS[name][2]][j]
        bit, partner = self.places[stage]
        here = rows_at(start, size)
        source = r.grad if j == STAGES - 1 else r.grads
        copy = self.remote(source.at[here], r.grads.at[here], name, 2 * STAGES - 1 - j, partner)
        self.only(stage in (PUSH, MIDDLE), copy.start)
        if stage == PUSH:
            self.at[name] = ("spread", j, copy, start, size, None)
        else:
            self.at[name] = ("spread", j, copy, start - bit * size, 2 * size, None)

    def spread_done(self, name, j, copy):
        stage = ORDERS[UNITS[name][2]][j]
        if stage == PUSH:
            pl.when(self.middle)(copy.wait_send)
            pl.when(self.edge)(copy.wait_recv)
        else:
            self.only(stage == MIDDLE, copy.wait)
        if j == STAGES - 1:
            self.only(self.lined(name), self.store[name].wait)

    def own(self, name, start, size):
        here = rows_at(start, size)
        return pltpu.make_async_copy(
            self.r.grad.at[here], self.r.grads.at[here], self.r.own_sem.at[self.index[name]]
        )

    def step(self, name):
        if name == "gains":
            return self.step_gains()
        base, rows, order = UNITS[name]
        if name not in self.at:
            return self.give(name, 0, base, rows, LANDING[name])
        kind, j, copy, start, size, first = self.at[name]
        if kind == "give":
            self.given(name, j, copy, start, size, first)
            if j + 1 < STAGES:
                return self.give(name, j + 1, start, size, first + size)
            self.only(self.lined(name), lambda: self.outer(name, start, size))
            self.store[name] = self.own(name, start, size)
            self.only(self.lined(name), self.store[name].start)
            self.spread(name, j, start, size)
        else:
            self.spread_done(name, j, copy)
            if j > 0:
                self.spread(name, j - 1, start, size)
            else:
                self.at[name] = None

    def outer(self, name, start, size):
        others = outer_partners(self.docs_count)
        if not others:
            return
        r = self.r
        here = rows_at(start, size)
        share = pl.ds(UNITS[name][0] // 16, size)
        for b in range(outer_bits(self.docs_count)):
            partner = place_of(("docs", GROUP << b))[1]
            copy = self.other(
                r.grad.at[here], r.outer.at[b, share], (r.outer_s, r.outer_r), self.index[name], b, partner
            )
            copy.start()
            copy.wait()
            r.grad[here, :] = (r.grad[here, :].astype(F32) + r.outer[b, share, :].astype(F32)).astype(LOW)

    def step_gains(self):
        r = self.r
        j = self.at.get("gains", 0)
        if j > 0:
            self.gain_copy(j - 1).wait()
            more = r.gain_landed[j - 1]
            if j == 1:
                more = more * self.share
            r.gain_steps[j] = r.gain_steps[j - 1] + more
        if j < STAGES:
            self.gain_copy(j).start()
        else:
            others = outer_partners(self.docs_count)
            if others:
                mine = lax.div(lax.axis_index("docs"), GROUP)
                r.gain_outer[mine] = r.gain_steps[j]
                copies = [
                    self.other(r.gain_steps.at[j], r.gain_outer.at[mine], (r.gain_os, r.gain_or), 0, k, partner)
                    for k, partner in enumerate(others)
                ]
                for copy in copies:
                    copy.start()
                for copy in copies:
                    copy.wait()
                r.gain_steps[j] = sum(r.gain_outer[k] for k in range(len(others) + 1))
        self.at["gains"] = j + 1

    def gain_copy(self, j):
        r = self.r
        partner = self.places[SINGLE[j]][1]
        return self.other(r.gain_steps.at[j], r.gain_landed.at[j], (r.gain_s, r.gain_r), 0, j, partner)


def add_rows(total, start, rows, landed, first, share=None):
    tile = min(rows, 128)

    def turn(t, carry):
        here = rows_at(start + t * tile, tile)
        more = landed[rows_at(first + t * tile, tile), :].astype(F32)
        if share is not None:
            more = more * share
        total[here, :] = (total[here, :].astype(F32) + more).astype(total.dtype)
        return carry

    lax.fori_loop(0, rows // tile, turn, 0)


def dot(left, right, left_dim, right_dim):
    return lax.dot_general(
        left, right, (((left_dim,), (right_dim,)), ((), ())), preferred_element_type=F32
    )


def nn(left, right):
    return dot(left, right, 1, 0)


def nt(left, right):
    return dot(left, right, 1, 1)


def tn(left, right):
    return dot(left, right, 0, 0)


def tiles(rows, tile, body):
    def turn(t, carry):
        body(pl.ds(pl.multiple_of(t * tile, tile), tile), t)
        return carry

    lax.fori_loop(0, rows // tile, turn, 0)


def rows_at(start, size):
    return pl.ds(pl.multiple_of(start, 16), size)


def norm_rows(values, gain_row):
    centered = values - jnp.mean(values, axis=-1, keepdims=True)
    inverse = lax.rsqrt(jnp.mean(centered * centered, axis=-1, keepdims=True) + 1e-05)
    unit = centered * inverse
    return (unit * gain_row).astype(LOW), unit, inverse


def norm_back(grad, unit, inverse, gain_row):
    scaled = grad * gain_row
    adjusted = (
        scaled
        - jnp.mean(scaled, axis=-1, keepdims=True)
        - unit * jnp.mean(scaled * unit, axis=-1, keepdims=True)
    )
    return adjusted * inverse


def same_head():
    left = lax.div(lax.broadcasted_iota(jnp.int32, (256, 256), 0), HD)
    right = lax.div(lax.broadcasted_iota(jnp.int32, (256, 256), 1), HD)
    return left == right


def four_heads(values):
    return jnp.where(same_head(), jnp.concatenate([values] * 4, axis=0), 0.0)


def own_blocks(values):
    return jnp.sum(jnp.where(same_head(), values, 0.0).reshape(4, HD, 256), axis=0)


def swap(values):
    return own_blocks(four_heads(values).T)


def head_stack(values):
    low_half = lax.broadcasted_iota(jnp.int32, values.shape, 1) < HD
    return jnp.concatenate(
        [jnp.where(low_half, values, 0.0), jnp.where(low_half, 0.0, values)], axis=0
    )


def head_pick(values):
    first_head = lax.broadcasted_iota(jnp.int32, (128, 128), 1) < HD
    return jnp.where(first_head, values[:128], values[128:])


BLOCKS = SEG // 128
BLOCK_ROWS = [sum(128 * (k + 1) for k in range(i)) for i in range(BLOCKS + 1)]
PAIRS = D // 128

WEIGHTS = (
    "self_qkv", "cross_qkv", "writer_qkv", "writer_out", "self_out", "cross_out", "ffn_in", "ffn_out",
)
INPUTS = (
    "x", "memory", "lengths", "seg_index", "self_qkv", "self_out", "cross_qkv", "cross_out",
    "ffn_in", "ffn_out", "writer_qkv", "writer_out", "gains", "out_cot", "mem_cot",
)
OUTPUTS = ("enc_out", "new_memory", "input_grad", "memory_grad", "grads", "gains_grad")
def scratch_of(docs, rows, slots, weights, docs_count):
    keys = SEG + slots
    units, outers = len(UNITS), max(1, docs_count // GROUP)
    dma = pltpu.SemaphoreType.DMA
    low = lambda *shape: pltpu.VMEM(shape, LOW)
    full = lambda *shape: pltpu.VMEM(shape, F32)
    fetched = {"w_" + name: pltpu.VMEM(weights[name].shape, LOW) for name in WEIGHTS}
    return dict(
        **fetched,
        mem=low(slots, D),
        mem_back=low(slots, D),
        gain_rows=full(5, D),
        x_all=low(SEG, D),
        cot_all=low(SEG, D),
        enc=low(SEG, D),
        slot_grad=low(slots, D),
        new_slots=low(slots, D),
        unit0=full(SEG, D),
        unit1=full(SEG, D),
        unit2=full(SEG, D),
        unit4=full(SEG, D),
        unit3=full(slots, D),
        inv0=full(SEG, 1),
        inv1=full(SEG, 1),
        inv2=full(SEG, 1),
        inv4=full(SEG, 1),
        inv3=full(slots, 1),
        h0=low(SEG, D),
        h1=low(SEG, D),
        h2=low(SEG, D),
        src=low(keys, D),
        q=low(SEG, D),
        k=low(SEG, D),
        v=low(SEG, D),
        prob=low(PAIRS, BLOCK_ROWS[-1], 256),
        mix=low(SEG, D),
        inv_total=full(SEG, D),
        acc=full(SEG, D),
        res=full(SEG, D),
        cq=low(SEG, D),
        cross_k=low(2, 256, 256),
        cross_v=low(2, 256, 256),
        cross_p=low(2, 256, SEG),
        co=low(SEG, D),
        z=low(4, SEG, D),
        slope=low(4, SEG, D),
        wkey=low(keys, D),
        wvalue=low(keys, D),
        dkey=low(keys, D),
        dvalue=low(keys, D),
        wprob=low(2, keys, 256),
        wslope=low(2, keys, 256),
        wquery=low(2, 256, 256),
        dmix=low(2, 256, 256),
        wo=low(slots, D),
        dwq=low(slots, D),
        dck=low(slots, D),
        dcv=low(slots, D),
        low=low(SEG, D),
        dsend=low(SEG, D),
        delta=full(16, SEG),
        dk_sum=full(SEG, 128),
        dv_sum=full(SEG, 128),
        gain_sum=full(5, 8, D),
        gain_steps=full(STAGES + 1, 8, D),
        gain_landed=full(STAGES, 8, D),
        gain_outer=full(outers, 8, D),
        grad=low(GRAD_ROWS, D),
        landed=low(LANDED_ROWS, D),
        outer=low(*((outer_bits(docs_count), GRAD_ROWS // 16, D) if outers > 1 else (1, 16, D))),
        unit_s=dma((units,)),
        unit_r=dma((units, 2 * STAGES)),
        own_sem=dma((units,)),
        outer_s=dma((units if outers > 1 else 1, outers)),
        outer_r=dma((units if outers > 1 else 1, outers)),
        gain_s=dma((1, STAGES)),
        gain_r=dma((1, STAGES)),
        gain_os=dma((1, outers)),
        gain_or=dma((1, outers)),
        load_sem=dma((len(WEIGHTS) + 5,)),
        xs=dma((3,)),
        xr=dma((3,)),
        cs=dma((3,)),
        cr=dma((3,)),
        es=dma((3,)),
        er=dma((3,)),
        us=dma((3,)),
        ur=dma((3,)),
        gs=dma((3,)),
        gr=dma((3,)),
        ms=dma((3,)),
        mr=dma((3,)),
        out_sem=dma((5,)),
    )


def layer_kernel(docs, rows, slots, docs_count, names, *refs):
    r = types.SimpleNamespace(**dict(zip(names, refs)))
    s = lax.axis_index("seq")
    bit0, bit1 = lax.rem(s, 2), lax.div(s, 2)
    near = s + 1 - 2 * bit0
    far = s + 2 - 4 * bit1
    across = near + 2 - 4 * bit1
    peers = (near, far, across)

    def doc_of(index):
        return jnp.minimum(index, docs - 1)

    mine = doc_of(s)

    def remote(source, target, send_sem, recv_sem, to):
        return pltpu.make_async_remote_copy(
            src_ref=source, dst_ref=target, send_sem=send_sem, recv_sem=recv_sem,
            device_id={"seq": to}, device_id_type=MESH,
        )

    def gain(k):
        return r.gain_rows[k : k + 1, :]

    def add_gain(k, values):
        r.gain_sum[k] += jnp.sum(values.reshape(-1, 8, D), axis=0)

    barrier = pltpu.get_barrier_semaphore()
    greeted = [{"seq": across}] + partners_of(docs_count)
    for partner in greeted:
        pl.semaphore_signal(barrier, inc=1, device_id=partner, device_id_type=MESH)
    own_rows = rows_at(s * rows, rows)
    doc_rows, doc_slots = rows_at(mine * rows, rows), rows_at(mine * slots, slots)
    fetched = dict(
        mem=(r.memory.at[doc_slots], r.mem),
        gains=(r.gains, r.gain_rows),
        x=(r.x.at[doc_rows], r.x_all.at[own_rows]),
        mem_cot=(r.mem_cot.at[doc_slots], r.mem_back),
        **{name: (getattr(r, name), getattr(r, "w_" + name)) for name in WEIGHTS},
        cot=(r.out_cot.at[doc_rows], r.cot_all.at[own_rows]),
    )
    loads = {}
    for k, (name, (source, target)) in enumerate(fetched.items()):
        loads[name] = pltpu.make_async_copy(source, target, r.load_sem.at[k])
        loads[name].start()
    r.gain_sum[...] = jnp.zeros_like(r.gain_sum)
    loads["mem"].wait()
    loads["gains"].wait()
    slot_range = pl.ds(SEG, slots)
    hm, r.unit3[...], r.inv3[...] = norm_rows(r.mem[...].astype(F32), gain(3))
    r.src[slot_range, :] = hm
    pl.semaphore_wait(barrier, len(greeted))

    def gather_copy(source, target, send_sem, recv_sem, k):
        return remote(
            source.at[rows_at(doc_of(peers[k]) * rows, rows)],
            target.at[rows_at(s * rows, rows)], send_sem.at[k], recv_sem.at[k], peers[k],
        )

    for k in range(3):
        gather_copy(r.x, r.x_all, r.xs, r.xr, k).start()

    def spread_copy(source, target, size, own, send_sem, recv_sem, k):
        piece = source.at[rows_at(peers[k] * size, size)] if own else source
        return remote(
            piece, target.at[rows_at(mine * size, size)], send_sem.at[k], recv_sem.at[k], peers[k]
        )

    def keep_copy(k, source, target, size, own, *sems):
        piece = source.at[rows_at(s * size, size)] if own else source
        return pltpu.make_async_copy(piece, target.at[rows_at(mine * size, size)], r.out_sem.at[k])

    summer = Summer(r, docs_count, 1.0 - bit1.astype(F32))
    ticks = iter(SCHEDULE)

    def tick():
        for name in next(ticks):
            summer.step(name)

    def spread(*where):
        spread_copy(*where, 1).start()

        @pl.when(bit1 == 0)
        def _():
            spread_copy(*where, 0).start()
            spread_copy(*where, 2).start()

    def spread_wait(*where):
        spread_copy(*where, 1).wait()

        @pl.when(bit1 == 0)
        def _():
            spread_copy(*where, 0).wait()
            spread_copy(*where, 2).wait_send()

        @pl.when(bit1 == 1)
        def _():
            spread_copy(*where, 2).wait_recv()

    def place_heads(target, values):
        for g in range(2):
            piece = values[:, g * 256 : (g + 1) * 256].astype(LOW).astype(F32)
            target[g] = four_heads(piece).astype(LOW)

    loads["cross_qkv"].wait()
    place_heads(r.cross_k, nn(hm, r.w_cross_qkv[1]))
    place_heads(r.cross_v, nn(hm, r.w_cross_qkv[2]))
    loads["writer_qkv"].wait()
    r.wkey[slot_range, :] = nn(hm, r.w_writer_qkv[1]).astype(LOW)
    r.wvalue[slot_range, :] = nn(hm, r.w_writer_qkv[2]).astype(LOW)
    place_heads(r.wquery, nn(hm, r.w_writer_qkv[0]) * SCALE)
    loads["writer_out"].wait()
    loads["mem_cot"].wait()
    mem_cot = r.mem_back[...]
    place_heads(r.dmix, nt(mem_cot, r.w_writer_out[...]))

    def enter(start):
        here = rows_at(start, SEG // 2)
        normed, unit, inverse = norm_rows(r.x_all[here, :].astype(F32), gain(0))
        r.unit0[here, :] = unit
        r.inv0[here, :] = inverse
        r.h0[here, :] = normed
        r.q[here, :] = (nn(normed, r.w_self_qkv[0]) * SCALE).astype(LOW)
        r.k[here, :] = nn(normed, r.w_self_qkv[1]).astype(LOW)
        r.v[here, :] = nn(normed, r.w_self_qkv[2]).astype(LOW)

    loads["x"].wait()
    loads["self_qkv"].wait()
    gather_copy(r.x, r.x_all, r.xs, r.xr, 0).wait_recv()
    enter(bit1 * (SEG // 2))
    for k in (1, 2):
        gather_copy(r.x, r.x_all, r.xs, r.xr, k).wait_recv()
    for k in range(3):
        gather_copy(r.out_cot, r.cot_all, r.cs, r.cr, k).start()
    enter((1 - bit1) * (SEG // 2))
    for k in range(3):
        gather_copy(r.x, r.x_all, r.xs, r.xr, k).wait_send()
    live = jnp.minimum(r.lengths[mine] - r.seg_index[mine] * SEG, SEG)

    ones = jnp.ones((SEG, 128), LOW)
    for p in range(PAIRS):
        columns = slice(p * 128, (p + 1) * 128)
        for i in range(BLOCKS):
            depth = 128 * (i + 1)
            here = slice(i * 128, (i + 1) * 128)
            stacked = head_stack(r.q[here, columns].astype(F32)).astype(LOW)
            scores = nt(r.k[:depth, columns], stacked)
            key_pos = lax.broadcasted_iota(jnp.int32, scores.shape, 0)
            query_pos = i * 128 + lax.rem(lax.broadcasted_iota(jnp.int32, scores.shape, 1), 128)
            scores = jnp.where((key_pos <= query_pos) & (key_pos < live), scores, SHUT)
            powers = jnp.exp(scores - jnp.max(scores, axis=0, keepdims=True)).astype(LOW)
            r.prob[p, BLOCK_ROWS[i] : BLOCK_ROWS[i + 1], :] = powers
            mixed = tn(powers, jnp.concatenate([r.v[:depth, columns], ones[:depth]], axis=1))
            inverse = 1.0 / head_pick(mixed[:, 128:])
            r.inv_total[here, columns] = inverse
            r.mix[here, columns] = (head_pick(mixed[:, :128]) * inverse).astype(LOW)

    loads["self_out"].wait()
    total = r.x_all[...].astype(F32) + nn(r.mix[...], r.w_self_out[...])
    r.res[...] = total
    r.h1[...], r.unit1[...], r.inv1[...] = norm_rows(total, gain(1))
    r.cq[...] = (nn(r.h1[...], r.w_cross_qkv[0]) * SCALE).astype(LOW)

    for g in range(2):
        columns = slice(g * 256, (g + 1) * 256)
        scores = nt(r.cross_k[g], r.cq[:, columns]).reshape(4, slots, SEG)
        powers = jnp.exp(scores - jnp.max(scores, axis=1, keepdims=True))
        inverse = 1.0 / jnp.sum(powers, axis=1, keepdims=True)
        r.cross_p[g] = (powers * inverse).reshape(256, SEG).astype(LOW)
        r.co[:, columns] = tn(r.cross_p[g], r.cross_v[g]).astype(LOW)

    loads["cross_out"].wait()
    total = r.res[...] + nn(r.co[...], r.w_cross_out[...])
    r.res[...] = total
    r.h2[...], r.unit2[...], r.inv2[...] = norm_rows(total, gain(2))

    rate, cube = 0.7978845608028654, 0.044715
    loads["ffn_in"].wait()
    loads["ffn_out"].wait()

    for c in range(4):
        columns = slice(c * D, (c + 1) * D)
        u = nn(r.h2[...], r.w_ffn_in[:, columns])
        square = u * u
        bend = jnp.tanh(rate * u * (1.0 + cube * square))
        half = 0.5 * (1.0 + bend)
        r.z[c] = (u * half).astype(LOW)
        slope = half + (0.5 * rate) * u * (1.0 - bend * bend) * (1.0 + 3.0 * cube * square)
        r.slope[c] = slope.astype(LOW)
        r.res[...] += nn(r.z[c], r.w_ffn_out[columns, :])

    total = r.res[...]
    r.enc[...] = total.astype(LOW)
    r.src[:SEG, :], r.unit4[...], r.inv4[...] = norm_rows(total, gain(4))
    enc_way = (r.enc, r.enc_out, rows, True, r.es, r.er)
    spread(*enc_way)
    keep_copy(0, *enc_way).start()

    written = r.src[:SEG, :]
    r.wkey[:SEG, :] = nn(written, r.w_writer_qkv[1]).astype(LOW)
    r.wvalue[:SEG, :] = nn(written, r.w_writer_qkv[2]).astype(LOW)
    for g in range(2):
        columns = slice(g * 256, (g + 1) * 256)
        keys, values = r.wkey[:, columns], r.wvalue[:, columns]
        scores = nt(keys, r.wquery[g])
        key_pos = lax.broadcasted_iota(jnp.int32, scores.shape, 0)
        scores = jnp.where((key_pos >= SEG) | (key_pos < live), scores, SHUT)
        powers = jnp.exp(scores - jnp.max(scores, axis=0, keepdims=True))
        probs = powers * (1.0 / jnp.sum(powers, axis=0, keepdims=True))
        dprobs = nt(values, r.dmix[g])
        delta = jnp.sum(probs * dprobs, axis=0, keepdims=True)
        r.wslope[g] = (probs * (dprobs - delta)).astype(LOW)
        r.wprob[g] = probs.astype(LOW)
        r.dkey[:, columns] = nn(r.wslope[g], r.wquery[g]).astype(LOW)
        r.dvalue[:, columns] = nn(r.wprob[g], r.dmix[g]).astype(LOW)

    def put(block, values):
        r.grad[block * D : (block + 1) * D, :] = values.astype(LOW)

    put(BLOCK["writer_kv"], tn(r.src[...], r.dkey[...]))
    put(BLOCK["writer_kv"] + 1, tn(r.src[...], r.dvalue[...]))
    tick()

    grad = nt(r.dkey[:SEG, :], r.w_writer_qkv[1]) + nt(r.dvalue[:SEG, :], r.w_writer_qkv[2])
    loads["cot"].wait()
    for k in range(3):
        gather_copy(r.out_cot, r.cot_all, r.cs, r.cr, k).wait()
    add_gain(4, grad * r.unit4[...])
    total = r.cot_all[...].astype(F32) + norm_back(grad, r.unit4[...], r.inv4[...], gain(4))
    r.res[...] = total
    r.low[...] = total.astype(LOW)
    tick()

    for g in range(2):
        columns = slice(g * 256, (g + 1) * 256)
        mixed = own_blocks(tn(r.wvalue[:, columns], r.wprob[g])).astype(LOW).astype(F32)
        r.wo[:, columns] = swap(mixed).astype(LOW)
        dquery = own_blocks(tn(r.wslope[g], r.wkey[:, columns])).astype(LOW).astype(F32)
        r.dwq[:, columns] = (dquery * SCALE).astype(LOW)
    put(BLOCK["writer_q"], tn(hm, r.dwq[...]))
    put(BLOCK["writer_out"], tn(r.wo[...], mem_cot))
    tick()
    r.new_slots[...] = (
        r.mem[...].astype(F32) + nn(r.wo[...], r.w_writer_out[...])
    ).astype(LOW)
    new_way = (r.new_slots, r.new_memory, slots, False, r.us, r.ur)
    spread(*new_way)
    keep_copy(1, *new_way).start()

    for c in range(4):
        columns = slice(c * D, (c + 1) * D)
        put(BLOCK["ffn"] + 2 * c, tn(r.z[c], r.low[...]))
        tick()
        r.z[c] = (nt(r.low[...], r.w_ffn_out[columns, :]) * r.slope[c].astype(F32)).astype(LOW)
        put(BLOCK["ffn"] + 2 * c + 1, tn(r.h2[...], r.z[c]))
        back = nt(r.z[c], r.w_ffn_in[:, columns])
        r.acc[...] = back if c == 0 else r.acc[...] + back
        tick()

    grad, unit = r.acc[...], r.unit2[...]
    add_gain(2, grad * unit)
    total = r.res[...] + norm_back(grad, unit, r.inv2[...], gain(2))
    r.res[...] = total
    r.low[...] = total.astype(LOW)
    tick()

    r.dsend[...] = nt(r.low[...], r.w_cross_out[...]).astype(LOW)
    put(BLOCK["cross_out"], tn(r.co[...], r.low[...]))
    tick()
    for g in range(2):
        columns = slice(g * 256, (g + 1) * 256)
        dmix, queries = r.dsend[:, columns], r.cq[:, columns]
        dprobs = nt(r.cross_v[g], dmix)
        probs = r.cross_p[g].astype(F32)
        delta = jnp.sum((probs * dprobs).reshape(4, slots, SEG), axis=1, keepdims=True)
        slopes = (probs * (dprobs.reshape(4, slots, SEG) - delta).reshape(256, SEG)).astype(LOW)
        r.dck[:, columns] = own_blocks(nn(slopes, queries)).astype(LOW)
        r.dcv[:, columns] = own_blocks(nn(r.cross_p[g], dmix)).astype(LOW)
        r.cq[:, columns] = (tn(slopes, r.cross_k[g]).astype(LOW).astype(F32) * SCALE).astype(LOW)
    tick()
    r.acc[...] = nt(r.cq[...], r.w_cross_qkv[0])

    grad, unit = r.acc[...], r.unit1[...]
    add_gain(1, grad * unit)
    total = r.res[...] + norm_back(grad, unit, r.inv1[...], gain(1))
    r.res[...] = total
    r.low[...] = total.astype(LOW)
    tick()
    put(BLOCK["cross_qkv"], tn(r.h1[...], r.cq[...]))
    put(BLOCK["cross_qkv"] + 1, tn(hm, r.dck[...]))
    put(BLOCK["cross_qkv"] + 2, tn(hm, r.dcv[...]))
    tick()

    dmix = nt(r.low[...], r.w_self_out[...]).astype(LOW).astype(F32) * r.inv_total[...]
    r.dsend[...] = dmix.astype(LOW)
    product = dmix * r.mix[...].astype(F32)
    upper = product.astype(LOW)
    lower = (product - upper.astype(F32)).astype(LOW)
    head_rows = lax.div(lax.broadcasted_iota(jnp.int32, (16, D), 1), HD)
    head_rows = (head_rows == lax.broadcasted_iota(jnp.int32, (16, D), 0)).astype(F32).astype(LOW)
    r.delta[...] = nt(head_rows, upper) + nt(head_rows, lower)
    put(BLOCK["self_out"], tn(r.mix[...], r.low[...]))
    tick()

    for p in range(PAIRS):
        columns = slice(p * 128, (p + 1) * 128)
        r.dk_sum[...] = jnp.zeros_like(r.dk_sum)
        r.dv_sum[...] = jnp.zeros_like(r.dv_sum)
        for i in range(BLOCKS):
            depth = 128 * (i + 1)
            here = slice(i * 128, (i + 1) * 128)
            stacked = head_stack(r.dsend[here, columns].astype(F32)).astype(LOW)
            queries = head_stack(r.q[here, columns].astype(F32)).astype(LOW)
            probs = r.prob[p, BLOCK_ROWS[i] : BLOCK_ROWS[i + 1], :]
            dprobs = nt(r.v[:depth, columns], stacked)
            delta = jnp.concatenate([r.delta[2 * p + h : 2 * p + h + 1, here] for h in range(2)], axis=1)
            slopes = (probs.astype(F32) * (dprobs - delta)).astype(LOW)
            r.dk_sum[:depth, :] += nn(slopes, queries)
            r.dv_sum[:depth, :] += nn(probs, stacked)
            dquery = head_pick(tn(slopes, r.k[:depth, columns]))
            r.q[here, columns] = (dquery.astype(LOW).astype(F32) * SCALE).astype(LOW)
            if i == 2:
                tick()
        r.k[:, columns] = r.dk_sum[...].astype(LOW)
        r.v[:, columns] = r.dv_sum[...].astype(LOW)
        tick()
    for k, grad in enumerate((r.q, r.k, r.v)):
        put(BLOCK["self_qkv"] + k, tn(r.h0[...], grad[...]))
    tick()
    r.acc[...] = (
        nt(r.q[...], r.w_self_qkv[0]) + nt(r.k[...], r.w_self_qkv[1]) + nt(r.v[...], r.w_self_qkv[2])
    )
    spread_wait(*enc_way)
    keep_copy(0, *enc_way).wait()

    grad, unit = r.acc[...], r.unit0[...]
    add_gain(0, grad * unit)
    total = r.res[...] + norm_back(grad, unit, r.inv0[...], gain(0))
    r.enc[...] = total.astype(LOW)
    grad_way = (r.enc, r.input_grad, rows, True, r.gs, r.gr)
    spread(*grad_way)
    keep_copy(2, *grad_way).start()
    tick()

    dhm = (
        nt(r.dwq[...], r.w_writer_qkv[0])
        + nt(r.dkey[slot_range, :], r.w_writer_qkv[1])
        + nt(r.dvalue[slot_range, :], r.w_writer_qkv[2])
        + nt(r.dck[...], r.w_cross_qkv[1])
        + nt(r.dcv[...], r.w_cross_qkv[2])
    )
    unit = r.unit3[...]
    add_gain(3, dhm * unit)
    r.slot_grad[...] = (
        mem_cot.astype(F32) + norm_back(dhm, unit, r.inv3[...], gain(3))
    ).astype(LOW)
    slot_way = (r.slot_grad, r.memory_grad, slots, False, r.ms, r.mr)
    spread(*slot_way)
    keep_copy(3, *slot_way).start()
    r.gain_steps[0] = jnp.concatenate(
        [jnp.sum(r.gain_sum[k], axis=0, keepdims=True) for k in range(5)] + [jnp.zeros((3, D), F32)], axis=0
    )
    tick()
    tick()
    last = pltpu.make_async_copy(r.gain_steps.at[STAGES], r.gains_grad, r.out_sem.at[4])
    last.start()
    last.wait()
    for k, way in enumerate((enc_way, new_way, grad_way, slot_way)):
        if k > 0:
            spread_wait(*way)
            keep_copy(k, *way).wait()


def finish_kernel(enc, new, in_grad, mem_grad, grads, gains, *refs):
    outs, (low, wide, row_low, row_wide, slot_low, slot_wide, enc_low, new_low, gain_wide, load_sem, store_sem,
           pass_sem) = refs[:13], refs[13:]
    (o_enc, o_new, o_in, o_mem, self_qkv, self_out, cross_qkv, cross_out, ffn_in, ffn_out, writer_qkv,
     writer_out, o_gains) = outs
    slots = wide.shape[0]

    def place(block):
        parts = ((("writer_kv", 2, 1), writer_qkv), (("writer_q", 1, 0), writer_qkv), (("cross_qkv", 3, 0), cross_qkv),
                 (("self_qkv", 3, 0), self_qkv))
        for (name, many, first), ref in parts:
            if 0 <= block - BLOCK[name] < many:
                return ref.at[block - BLOCK[name] + first]
        for name, ref in (("writer_out", writer_out), ("cross_out", cross_out), ("self_out", self_out)):
            if block == BLOCK[name]:
                return ref
        c, second = divmod(block - BLOCK["ffn"], 2)
        return (ffn_in.at[:, pl.ds(c * D, D)] if second else ffn_out.at[pl.ds(c * D, D), :])

    count = GRAD_ROWS // D
    loads = [
        pltpu.make_async_copy(grads.at[pl.ds(k * D, D)], low.at[pl.ds(k * D, D)], load_sem.at[k])
        for k in range(count)
    ]
    rest = [
        pltpu.make_async_copy(source, target, pass_sem.at[k])
        for k, (source, target) in enumerate(
            ((in_grad, row_low), (mem_grad, slot_low), (enc, enc_low), (new, new_low), (gains, gain_wide))
        )
    ]
    for copy in loads + rest:
        copy.start()
    stores = []
    for k in range(count):
        loads[k].wait()
        if k >= slots:
            stores[k - slots].wait()

        def turn(here, t):
            wide[k % slots, here, :] = low[rows_at(k * D + t * 128, 128), :].astype(F32)

        tiles(D, 128, turn)
        stores.append(pltpu.make_async_copy(wide.at[k % slots], place(k), store_sem.at[k % slots]))
        stores[k].start()
    ways = (
        (row_low, row_wide, o_in), (slot_low, slot_wide, o_mem), (enc_low, enc_low, o_enc), (new_low, new_low, o_new),
        (gain_wide, gain_wide, o_gains),
    )
    for k, (read, held, out) in enumerate(ways):
        rest[k].wait()
        if read is not held:
            held[...] = read[...].astype(F32)
        stores.append(pltpu.make_async_copy(held, out, store_sem.at[slots + k]))
        stores[-1].start()
    for copy in stores[count - slots :]:
        copy.wait()


def on_device(*arguments):
    seg_input, memory = arguments[0], arguments[1]
    docs, rows, _ = seg_input.shape
    slots = memory.shape[1]
    docs_count = lax.axis_size("docs")
    scratch = scratch_of(docs, rows, slots, dict(zip(INPUTS, arguments)), docs_count)
    smem, anywhere = pl.BlockSpec(memory_space=pltpu.SMEM), pl.BlockSpec(memory_space=pl.ANY)
    arguments = list(arguments)
    for k in (0, 1, 13, 14):
        arguments[k] = arguments[k].reshape(-1, D)
    names = INPUTS + OUTPUTS + tuple(scratch)
    low = lambda *shape: jax.ShapeDtypeStruct(shape, LOW)
    full = lambda *shape: jax.ShapeDtypeStruct(shape, F32)
    parts = pl.pallas_call(
        functools.partial(layer_kernel, docs, rows, slots, docs_count, names),
        out_shape=(
            low(docs * rows, D), low(docs * slots, D), low(docs * rows, D), low(docs * slots, D),
            low(GRAD_ROWS, D), full(8, D),
        ),
        in_specs=[
            smem if name in ("lengths", "seg_index") else anywhere for name in INPUTS
        ],
        out_specs=(anywhere,) * 6,
        scratch_shapes=list(scratch.values()),
        compiler_params=pltpu.CompilerParams(
            collective_id=1, has_side_effects=True, vmem_limit_bytes=VMEM_BYTES
        ),
    )(*arguments)
    shapes = dict(zip(INPUTS, (full(*argument.shape) for argument in arguments)))
    results = pl.pallas_call(
        finish_kernel,
        out_shape=(
            low(docs * rows, D), low(docs * slots, D), full(docs * rows, D), full(docs * slots, D),
            *(shapes[name] for name in INPUTS[4:12]), full(8, D),
        ),
        in_specs=[pl.BlockSpec(memory_space=pltpu.HBM)] * 6,
        out_specs=(pl.BlockSpec(memory_space=pltpu.HBM),) * 13,
        scratch_shapes=[
            pltpu.VMEM((GRAD_ROWS, D), LOW),
            pltpu.VMEM((6, D, D), F32),
            pltpu.VMEM((docs * rows, D), LOW),
            pltpu.VMEM((docs * rows, D), F32),
            pltpu.VMEM((docs * slots, D), LOW),
            pltpu.VMEM((docs * slots, D), F32),
            pltpu.VMEM((docs * rows, D), LOW),
            pltpu.VMEM((docs * slots, D), LOW),
            pltpu.VMEM((8, D), F32),
            pltpu.SemaphoreType.DMA((GRAD_ROWS // D,)),
            pltpu.SemaphoreType.DMA((6 + 5,)),
            pltpu.SemaphoreType.DMA((5,)),
        ],
        compiler_params=pltpu.CompilerParams(vmem_limit_bytes=VMEM_BYTES),
    )(*parts)
    results = list(results)
    for k in (0, 2):
        results[k] = results[k].reshape(docs, rows, D)
    for k in (1, 3):
        results[k] = results[k].reshape(docs, slots, D)
    results[12] = results[12][:5]
    return tuple(results)


def solution(mesh):
    row, slot, whole = P("docs", "seq", None), P("docs", None, None), P()
    return jax.shard_map(
        on_device,
        mesh=mesh,
        in_specs=(row, slot, P("docs"), P("docs")) + (whole,) * 9 + (row, slot),
        out_specs=(row, slot, row, slot) + (whole,) * 9,
        check_vma=False,
    )
```

```python
import functools
import types

import jax
import jax.numpy as jnp
from jax import lax
from jax.experimental import pallas as pl
from jax.experimental.pallas import tpu as pltpu
from jax.sharding import PartitionSpec as P

MESH = pl.DeviceIdType.MESH
F32, LOW = jnp.float32, jnp.bfloat16
VMEM_BYTES = 63 << 20
D = 512
HD = 64
SEG = 512
SHUT = -1e30
SCALE = HD ** (-0.5)

CORE, X, Y, Z0, Z1 = ("seq", 1), ("seq", 2), ("docs", 1), ("docs", 2), ("docs", 4)
SINGLE = (CORE, X, Y, Z0, Z1)
PUSH, MIDDLE = "push", "middle"
ORDERS = dict(
    X=(CORE, X, Y, PUSH, MIDDLE), Y=(CORE, Y, X, PUSH, MIDDLE), A=(CORE, Z0, X, Y, Z1), B=(CORE, Z0, Y, X, Z1),
)
UNITS = {
    "Wa": (0, 512, "Y"),
    "Wb": (512, 1024, "X"),
    "Wc": (1536, 512, "B"),
    "F0a": (2048, 512, "A"),
    "F0b": (2560, 512, "Y"),
    "F1a": (3072, 1024, "B"),
    "F2a": (4096, 1024, "X"),
    "F3a": (5120, 512, "Y"),
    "F3b": (5632, 512, "Y"),
    "Xa": (6144, 512, "B"),
    "Xb": (6656, 512, "X"),
    "Xc": (7168, 512, "Y"),
    "Xd": (7680, 512, "X"),
    "Sa": (8192, 512, "B"),
    "Qa": (8704, 512, "Y"),
    "Qb": (9216, 512, "Y"),
    "Qc": (9728, 512, "B"),
}
SCHEDULE = (
    ("Wb", "Wa", "Wc",),
    (),
    ("F0a", "F0b", "Wb", "Wa", "Wc",),
    ("F0a", "F0b",),
    ("F1a",),
    (),
    ("F2a", "F1a", "Wa", "Wc",),
    (),
    ("F3a", "F3b", "F0b", "Wb", "F2a", "F0a",),
    ("Wa", "F3a", "Wc", "F3b",),
    (),
    (),
    ("F0b",),
    ("Xa", "Xb", "Xc", "Xd", "F1a", "Wb",),
    ("Sa", "Xa", "Xc", "Xd", "Wa", "F3a", "Xb", "F0b", "Sa", "F2a",),
    (),
    (),
    (),
    ("F3b", "Wb", "F0a", "Wa",),
    ("Wc", "F0b",),
    (),
    (),
    (),
    ("Qc", "Qb", "Qa", "F1a", "Xd", "Xa", "F3a", "Wb", "Wa", "Xc", "Sa", "Qc", "Qb", "F0b", "Qa",),
    ("F2a", "F3a", "Wc", "Wb", "Wa", "F0a", "Xb", "F3b",),
    ("F1a", "Xd",),
    (
        "gains", "Qc", "Xc", "Xa", "F3a", "Sa", "F0b", "F2a", "Wc", "Qb", "F3a", "Wb", "F3b", "F2a", "F0a",
        "Wa", "Qa", "F1a", "Xd", "Xb", "F3a", "gains", "F3b", "Xa", "Xc", "Sa", "Qc", "F2a", "F0b", "F0a",
        "Wc", "F1a", "Wb", "Xb", "Xd", "Qb", "F3b", "Qa", "Xa", "Wa", "Xc", "F2a", "gains", "F3a", "Sa",
        "Xb", "Qc", "Wa", "Qb", "Xd", "F3b", "F1a", "F0b", "Qa", "Xc", "F0a", "Xa", "F0b", "Xb", "Sa", "Wc",
        "Qc", "Xd", "Qb", "gains", "Qa", "Wb", "Xc", "F2a", "Xb", "Wb", "F3b", "Qb", "F3a", "Qa", "F0a",
        "Wc", "Xa", "F3a", "Sa", "Qc", "F1a", "Wc", "Xc", "Qb", "gains", "Xd", "Qa", "Xb", "F0a", "F2a",
        "F3b", "F0a", "Qc", "Xa", "F2a", "F3b", "Qb", "Sa", "F1a", "Xd", "Xc", "F1a", "Xd", "Qa", "Xc",
        "gains", "Xa", "Qc", "Xa", "Xb", "Qb", "Sa", "Xb", "Qb", "Sa", "Qa", "Qc", "Qa", "Qc",
    ),
)
GROUP = 8


def bit_of(axis, stride):
    return lax.rem(lax.div(lax.axis_index(axis), stride), 2)


def in_middle():
    return bit_of("docs", 2) != bit_of("docs", 4)


def place_of(stage):
    if stage == MIDDLE:
        low_bit, bit = bit_of("docs", 2), bit_of("docs", 4)
        return bit, {"docs": lax.axis_index("docs") + 2 * (1 - 2 * low_bit) + 4 * (1 - 2 * bit)}
    axis, stride = Z0 if stage == PUSH else stage
    bit = bit_of(axis, stride)
    return bit, {axis: lax.axis_index(axis) + stride * (1 - 2 * bit)}


def outer_partners(docs_count):
    index = lax.axis_index("docs")
    return [{"docs": lax.rem(index + GROUP * k, docs_count)} for k in range(1, docs_count // GROUP)]


def outer_bits(docs_count):
    return (docs_count // GROUP).bit_length() - 1


def partners_of(docs_count):
    return [place_of(stage)[1] for stage in SINGLE + (MIDDLE,)] + outer_partners(docs_count)


BLOCK = dict(
    writer_qkv=0, writer_out=3, ffn=4, cross_out=12, cross_qkv=13, self_out=16, self_qkv=17,
)
GRAD_ROWS = 20 * 512
STAGES = 5
LANDING, LANDED_ROWS = {}, 0
for _name, (_base, _rows, _order) in UNITS.items():
    LANDING[_name] = LANDED_ROWS
    LANDED_ROWS += _rows + (_rows // 16 if PUSH in ORDERS[_order] else 0)


class Summer:
    def __init__(self, r, docs_count, share):
        self.r, self.share, self.docs_count = r, share, docs_count
        self.index = {name: k for k, name in enumerate(UNITS)}
        self.at, self.store = {}, {}
        self.middle = in_middle()

    def remote(self, source, target, name, j, partner):
        k = self.index[name]
        return pltpu.make_async_remote_copy(
            src_ref=source, dst_ref=target, send_sem=self.r.unit_s.at[k], recv_sem=self.r.unit_r.at[k, j],
            device_id=partner, device_id_type=MESH,
        )

    def other(self, source, target, sems, k, j, partner):
        return pltpu.make_async_remote_copy(
            src_ref=source, dst_ref=target, send_sem=sems[0].at[k, j], recv_sem=sems[1].at[k, j],
            device_id=partner, device_id_type=MESH,
        )

    def only(self, inside, body):
        if inside:
            pl.when(self.middle)(body)
        else:
            body()

    def lined(self, name):
        return PUSH in ORDERS[UNITS[name][2]]

    def give(self, name, j, start, size, first):
        r = self.r
        stage = ORDERS[UNITS[name][2]][j]
        bit, partner = place_of(stage)
        if stage == PUSH:
            half, sent, kept = size, start, start
        else:
            half = size // 2
            sent, kept = start + (1 - bit) * half, start + bit * half
        copy = self.remote(
            r.grad.at[rows_at(sent, half)], r.landed.at[pl.ds(first, half)], name, j, partner
        )
        if stage == PUSH:
            pl.when(jnp.logical_not(self.middle))(copy.start)
        else:
            self.only(stage == MIDDLE, copy.start)
        self.at[name] = ("give", j, copy, kept, half, first)

    def given(self, name, j, copy, start, size, first):
        stage = ORDERS[UNITS[name][2]][j]

        def add():
            add_rows(self.r.grad, start, size, self.r.landed, first, self.share if j == 0 else None)

        if stage == PUSH:

            @pl.when(self.middle)
            def _():
                copy.wait_recv()
                add()

            pl.when(jnp.logical_not(self.middle))(copy.wait_send)
        else:

            def both():
                copy.wait()
                add()

            self.only(stage == MIDDLE, both)

    def spread(self, name, j, start, size):
        r = self.r
        stage = ORDERS[UNITS[name][2]][j]
        bit, partner = place_of(stage)
        here = rows_at(start, size)
        source = r.grad if j == STAGES - 1 else r.grads
        copy = self.remote(source.at[here], r.grads.at[here], name, 2 * STAGES - 1 - j, partner)
        self.only(stage in (PUSH, MIDDLE), copy.start)
        if stage == PUSH:
            self.at[name] = ("spread", j, copy, start, size, None)
        else:
            self.at[name] = ("spread", j, copy, start - bit * size, 2 * size, None)

    def spread_done(self, name, j, copy):
        stage = ORDERS[UNITS[name][2]][j]
        if stage == PUSH:
            pl.when(self.middle)(copy.wait_send)
            pl.when(jnp.logical_not(self.middle))(copy.wait_recv)
        else:
            self.only(stage == MIDDLE, copy.wait)
        if j == STAGES - 1:
            self.only(self.lined(name), self.store[name].wait)

    def own(self, name, start, size):
        here = rows_at(start, size)
        return pltpu.make_async_copy(
            self.r.grad.at[here], self.r.grads.at[here], self.r.own_sem.at[self.index[name]]
        )

    def step(self, name):
        if name == "gains":
            return self.step_gains()
        base, rows, order = UNITS[name]
        if name not in self.at:
            return self.give(name, 0, base, rows, LANDING[name])
        kind, j, copy, start, size, first = self.at[name]
        if kind == "give":
            self.given(name, j, copy, start, size, first)
            if j + 1 < STAGES:
                return self.give(name, j + 1, start, size, first + size)
            self.only(self.lined(name), lambda: self.outer(name, start, size))
            self.store[name] = self.own(name, start, size)
            self.only(self.lined(name), self.store[name].start)
            self.spread(name, j, start, size)
        else:
            self.spread_done(name, j, copy)
            if j > 0:
                self.spread(name, j - 1, start, size)
            else:
                self.at[name] = None

    def outer(self, name, start, size):
        others = outer_partners(self.docs_count)
        if not others:
            return
        r = self.r
        here = rows_at(start, size)
        share = pl.ds(UNITS[name][0] // 16, size)
        for b in range(outer_bits(self.docs_count)):
            partner = place_of(("docs", GROUP << b))[1]
            copy = self.other(
                r.grad.at[here], r.outer.at[b, share], (r.outer_s, r.outer_r), self.index[name], b, partner
            )
            copy.start()
            copy.wait()
            r.grad[here, :] = (r.grad[here, :].astype(F32) + r.outer[b, share, :].astype(F32)).astype(LOW)

    def step_gains(self):
        r = self.r
        j = self.at.get("gains", 0)
        if j > 0:
            self.gain_copy(j - 1).wait()
            more = r.gain_landed[j - 1]
            if j == 1:
                more = more * self.share
            r.gain_steps[j] = r.gain_steps[j - 1] + more
        if j < STAGES:
            self.gain_copy(j).start()
        else:
            others = outer_partners(self.docs_count)
            if others:
                mine = lax.div(lax.axis_index("docs"), GROUP)
                r.gain_outer[mine] = r.gain_steps[j]
                copies = [
                    self.other(r.gain_steps.at[j], r.gain_outer.at[mine], (r.gain_os, r.gain_or), 0, k, partner)
                    for k, partner in enumerate(others)
                ]
                for copy in copies:
                    copy.start()
                for copy in copies:
                    copy.wait()
                r.gain_steps[j] = sum(r.gain_outer[k] for k in range(len(others) + 1))
        self.at["gains"] = j + 1

    def gain_copy(self, j):
        r = self.r
        partner = place_of(SINGLE[j])[1]
        return self.other(r.gain_steps.at[j], r.gain_landed.at[j], (r.gain_s, r.gain_r), 0, j, partner)


def add_rows(total, start, rows, landed, first, share=None):
    tile = min(rows, 128)

    def turn(t, carry):
        here = rows_at(start + t * tile, tile)
        more = landed[rows_at(first + t * tile, tile), :].astype(F32)
        if share is not None:
            more = more * share
        total[here, :] = (total[here, :].astype(F32) + more).astype(total.dtype)
        return carry

    lax.fori_loop(0, rows // tile, turn, 0)


def dot(left, right, left_dim, right_dim):
    return lax.dot_general(
        left, right, (((left_dim,), (right_dim,)), ((), ())), preferred_element_type=F32
    )


def nn(left, right):
    return dot(left, right, 1, 0)


def nt(left, right):
    return dot(left, right, 1, 1)


def tn(left, right):
    return dot(left, right, 0, 0)


def tiles(rows, tile, body):
    def turn(t, carry):
        body(pl.ds(pl.multiple_of(t * tile, tile), tile), t)
        return carry

    lax.fori_loop(0, rows // tile, turn, 0)


def rows_at(start, size):
    return pl.ds(pl.multiple_of(start, 16), size)


def norm_rows(values, gain_row):
    centered = values - jnp.mean(values, axis=-1, keepdims=True)
    inverse = lax.rsqrt(jnp.mean(centered * centered, axis=-1, keepdims=True) + 1e-05)
    unit = centered * inverse
    return (unit * gain_row).astype(LOW), unit, inverse


def norm_back(grad, unit, inverse, gain_row):
    scaled = grad * gain_row
    adjusted = (
        scaled
        - jnp.mean(scaled, axis=-1, keepdims=True)
        - unit * jnp.mean(scaled * unit, axis=-1, keepdims=True)
    )
    return adjusted * inverse


def same_head():
    left = lax.div(lax.broadcasted_iota(jnp.int32, (256, 256), 0), HD)
    right = lax.div(lax.broadcasted_iota(jnp.int32, (256, 256), 1), HD)
    return left == right


def four_heads(values):
    return jnp.where(same_head(), jnp.concatenate([values] * 4, axis=0), 0.0)


def own_blocks(values):
    return jnp.sum(jnp.where(same_head(), values, 0.0).reshape(4, HD, 256), axis=0)


def swap(values):
    return own_blocks(four_heads(values).T)


def head_stack(values):
    low_half = lax.broadcasted_iota(jnp.int32, values.shape, 1) < HD
    return jnp.concatenate(
        [jnp.where(low_half, values, 0.0), jnp.where(low_half, 0.0, values)], axis=0
    )


def head_pick(values):
    first_head = lax.broadcasted_iota(jnp.int32, (128, 128), 1) < HD
    return jnp.where(first_head, values[:128], values[128:])


BLOCKS = SEG // 128
BLOCK_ROWS = [sum(128 * (k + 1) for k in range(i)) for i in range(BLOCKS + 1)]
PAIRS = D // 128

WEIGHTS = (
    "self_qkv", "cross_qkv", "writer_qkv", "writer_out", "self_out", "cross_out", "ffn_in", "ffn_out",
)
INPUTS = (
    "x", "memory", "lengths", "seg_index", "self_qkv", "self_out", "cross_qkv", "cross_out",
    "ffn_in", "ffn_out", "writer_qkv", "writer_out", "gains", "out_cot", "mem_cot",
)
OUTPUTS = ("enc_out", "new_memory", "input_grad", "memory_grad", "grads", "gains_grad")
def scratch_of(docs, rows, slots, weights, docs_count):
    keys = SEG + slots
    units, outers = len(UNITS), max(1, docs_count // GROUP)
    dma = pltpu.SemaphoreType.DMA
    low = lambda *shape: pltpu.VMEM(shape, LOW)
    full = lambda *shape: pltpu.VMEM(shape, F32)
    fetched = {"w_" + name: pltpu.VMEM(weights[name].shape, LOW) for name in WEIGHTS}
    return dict(
        **fetched,
        mem=low(slots, D),
        mem_back=low(slots, D),
        gain_rows=full(5, D),
        x_all=low(SEG, D),
        cot_all=low(SEG, D),
        enc=low(SEG, D),
        slot_grad=low(slots, D),
        new_slots=low(slots, D),
        unit0=full(SEG, D),
        unit1=full(SEG, D),
        unit2=full(SEG, D),
        unit4=full(SEG, D),
        unit3=full(slots, D),
        inv0=full(SEG, 1),
        inv1=full(SEG, 1),
        inv2=full(SEG, 1),
        inv4=full(SEG, 1),
        inv3=full(slots, 1),
        h0=low(SEG, D),
        h1=low(SEG, D),
        h2=low(SEG, D),
        src=low(keys, D),
        q=low(SEG, D),
        k=low(SEG, D),
        v=low(SEG, D),
        prob=low(PAIRS, BLOCK_ROWS[-1], 256),
        mix=low(SEG, D),
        inv_total=full(SEG, D),
        acc=full(SEG, D),
        res=full(SEG, D),
        cq=low(SEG, D),
        cross_k=low(2, 256, 256),
        cross_v=low(2, 256, 256),
        cross_p=low(2, 256, SEG),
        co=low(SEG, D),
        z=low(4, SEG, D),
        slope=low(4, SEG, D),
        wkey=low(keys, D),
        wvalue=low(keys, D),
        wquery=low(2, 256, 256),
        dmix=low(2, 256, 256),
        wo=low(slots, D),
        dwq=low(slots, D),
        dck=low(slots, D),
        dcv=low(slots, D),
        low=low(SEG, D),
        dsend=low(SEG, D),
        delta=full(16, SEG),
        dk_sum=full(SEG, 128),
        dv_sum=full(SEG, 128),
        gain_sum=full(5, 8, D),
        gain_steps=full(STAGES + 1, 8, D),
        gain_landed=full(STAGES, 8, D),
        gain_outer=full(outers, 8, D),
        grad=low(GRAD_ROWS, D),
        landed=low(LANDED_ROWS, D),
        outer=low(*((outer_bits(docs_count), GRAD_ROWS // 16, D) if outers > 1 else (1, 16, D))),
        unit_s=dma((units,)),
        unit_r=dma((units, 2 * STAGES)),
        own_sem=dma((units,)),
        outer_s=dma((units if outers > 1 else 1, outers)),
        outer_r=dma((units if outers > 1 else 1, outers)),
        gain_s=dma((1, STAGES)),
        gain_r=dma((1, STAGES)),
        gain_os=dma((1, outers)),
        gain_or=dma((1, outers)),
        load_sem=dma((len(WEIGHTS) + 5,)),
        xs=dma((3,)),
        xr=dma((3,)),
        cs=dma((3,)),
        cr=dma((3,)),
        es=dma((3,)),
        er=dma((3,)),
        us=dma((3,)),
        ur=dma((3,)),
        gs=dma((3,)),
        gr=dma((3,)),
        ms=dma((3,)),
        mr=dma((3,)),
        out_sem=dma((5,)),
    )


def layer_kernel(docs, rows, slots, docs_count, names, *refs):
    r = types.SimpleNamespace(**dict(zip(names, refs)))
    s = lax.axis_index("seq")
    bit0, bit1 = lax.rem(s, 2), lax.div(s, 2)
    near = s + 1 - 2 * bit0
    far = s + 2 - 4 * bit1
    across = near + 2 - 4 * bit1
    peers = (near, far, across)

    def doc_of(index):
        return jnp.minimum(index, docs - 1)

    mine = doc_of(s)

    def remote(source, target, send_sem, recv_sem, to):
        return pltpu.make_async_remote_copy(
            src_ref=source, dst_ref=target, send_sem=send_sem, recv_sem=recv_sem,
            device_id={"seq": to}, device_id_type=MESH,
        )

    def gain(k):
        return r.gain_rows[k : k + 1, :]

    def add_gain(k, values):
        r.gain_sum[k] += jnp.sum(values.reshape(-1, 8, D), axis=0)

    barrier = pltpu.get_barrier_semaphore()
    greeted = [{"seq": across}] + partners_of(docs_count)
    for partner in greeted:
        pl.semaphore_signal(barrier, inc=1, device_id=partner, device_id_type=MESH)
    own_rows = rows_at(s * rows, rows)
    doc_rows, doc_slots = rows_at(mine * rows, rows), rows_at(mine * slots, slots)
    fetched = dict(
        mem=(r.memory.at[doc_slots], r.mem),
        gains=(r.gains, r.gain_rows),
        x=(r.x.at[doc_rows], r.x_all.at[own_rows]),
        mem_cot=(r.mem_cot.at[doc_slots], r.mem_back),
        **{name: (getattr(r, name), getattr(r, "w_" + name)) for name in WEIGHTS},
        cot=(r.out_cot.at[doc_rows], r.cot_all.at[own_rows]),
    )
    loads = {}
    for k, (name, (source, target)) in enumerate(fetched.items()):
        loads[name] = pltpu.make_async_copy(source, target, r.load_sem.at[k])
        loads[name].start()
    r.gain_sum[...] = jnp.zeros_like(r.gain_sum)
    loads["mem"].wait()
    loads["gains"].wait()
    slot_range = pl.ds(SEG, slots)
    hm, r.unit3[...], r.inv3[...] = norm_rows(r.mem[...].astype(F32), gain(3))
    r.src[slot_range, :] = hm
    pl.semaphore_wait(barrier, len(greeted))

    def gather_copy(source, target, send_sem, recv_sem, k):
        return remote(
            source.at[rows_at(doc_of(peers[k]) * rows, rows)],
            target.at[rows_at(s * rows, rows)], send_sem.at[k], recv_sem.at[k], peers[k],
        )

    for k in range(3):
        gather_copy(r.x, r.x_all, r.xs, r.xr, k).start()

    def spread_copy(source, target, size, own, send_sem, recv_sem, k):
        piece = source.at[rows_at(peers[k] * size, size)] if own else source
        return remote(
            piece, target.at[rows_at(mine * size, size)], send_sem.at[k], recv_sem.at[k], peers[k]
        )

    def keep_copy(k, source, target, size, own, *sems):
        piece = source.at[rows_at(s * size, size)] if own else source
        return pltpu.make_async_copy(piece, target.at[rows_at(mine * size, size)], r.out_sem.at[k])

    summer = Summer(r, docs_count, 1.0 - bit1.astype(F32))
    ticks = iter(SCHEDULE)

    def tick():
        for name in next(ticks):
            summer.step(name)

    def spread(*where):
        spread_copy(*where, 1).start()

        @pl.when(bit1 == 0)
        def _():
            spread_copy(*where, 0).start()
            spread_copy(*where, 2).start()

    def spread_wait(*where):
        spread_copy(*where, 1).wait()

        @pl.when(bit1 == 0)
        def _():
            spread_copy(*where, 0).wait()
            spread_copy(*where, 2).wait_send()

        @pl.when(bit1 == 1)
        def _():
            spread_copy(*where, 2).wait_recv()

    def place_heads(target, values):
        for g in range(2):
            piece = values[:, g * 256 : (g + 1) * 256].astype(LOW).astype(F32)
            target[g] = four_heads(piece).astype(LOW)

    loads["cross_qkv"].wait()
    place_heads(r.cross_k, nn(hm, r.w_cross_qkv[1]))
    place_heads(r.cross_v, nn(hm, r.w_cross_qkv[2]))
    loads["writer_qkv"].wait()
    r.wkey[slot_range, :] = nn(hm, r.w_writer_qkv[1]).astype(LOW)
    r.wvalue[slot_range, :] = nn(hm, r.w_writer_qkv[2]).astype(LOW)
    place_heads(r.wquery, nn(hm, r.w_writer_qkv[0]) * SCALE)
    loads["writer_out"].wait()
    loads["mem_cot"].wait()
    mem_cot = r.mem_back[...]
    place_heads(r.dmix, nt(mem_cot, r.w_writer_out[...]))

    def enter(start):
        here = rows_at(start, SEG // 2)
        normed, unit, inverse = norm_rows(r.x_all[here, :].astype(F32), gain(0))
        r.unit0[here, :] = unit
        r.inv0[here, :] = inverse
        r.h0[here, :] = normed
        r.q[here, :] = (nn(normed, r.w_self_qkv[0]) * SCALE).astype(LOW)
        r.k[here, :] = nn(normed, r.w_self_qkv[1]).astype(LOW)
        r.v[here, :] = nn(normed, r.w_self_qkv[2]).astype(LOW)

    loads["x"].wait()
    loads["self_qkv"].wait()
    gather_copy(r.x, r.x_all, r.xs, r.xr, 0).wait_recv()
    enter(bit1 * (SEG // 2))
    for k in (1, 2):
        gather_copy(r.x, r.x_all, r.xs, r.xr, k).wait_recv()
    for k in range(3):
        gather_copy(r.out_cot, r.cot_all, r.cs, r.cr, k).start()
    enter((1 - bit1) * (SEG // 2))
    for k in range(3):
        gather_copy(r.x, r.x_all, r.xs, r.xr, k).wait_send()
    live = jnp.minimum(r.lengths[mine] - r.seg_index[mine] * SEG, SEG)

    ones = jnp.ones((SEG, 128), LOW)
    for p in range(PAIRS):
        columns = slice(p * 128, (p + 1) * 128)
        for i in range(BLOCKS):
            depth = 128 * (i + 1)
            here = slice(i * 128, (i + 1) * 128)
            stacked = head_stack(r.q[here, columns].astype(F32)).astype(LOW)
            scores = nt(r.k[:depth, columns], stacked)
            key_pos = lax.broadcasted_iota(jnp.int32, scores.shape, 0)
            query_pos = i * 128 + lax.rem(lax.broadcasted_iota(jnp.int32, scores.shape, 1), 128)
            scores = jnp.where((key_pos <= query_pos) & (key_pos < live), scores, SHUT)
            powers = jnp.exp(scores - jnp.max(scores, axis=0, keepdims=True)).astype(LOW)
            r.prob[p, BLOCK_ROWS[i] : BLOCK_ROWS[i + 1], :] = powers
            mixed = tn(powers, jnp.concatenate([r.v[:depth, columns], ones[:depth]], axis=1))
            inverse = 1.0 / head_pick(mixed[:, 128:])
            r.inv_total[here, columns] = inverse
            r.mix[here, columns] = (head_pick(mixed[:, :128]) * inverse).astype(LOW)

    loads["self_out"].wait()
    total = r.x_all[...].astype(F32) + nn(r.mix[...], r.w_self_out[...])
    r.res[...] = total
    r.h1[...], r.unit1[...], r.inv1[...] = norm_rows(total, gain(1))
    r.cq[...] = (nn(r.h1[...], r.w_cross_qkv[0]) * SCALE).astype(LOW)

    for g in range(2):
        columns = slice(g * 256, (g + 1) * 256)
        scores = nt(r.cross_k[g], r.cq[:, columns]).reshape(4, slots, SEG)
        powers = jnp.exp(scores - jnp.max(scores, axis=1, keepdims=True))
        inverse = 1.0 / jnp.sum(powers, axis=1, keepdims=True)
        r.cross_p[g] = (powers * inverse).reshape(256, SEG).astype(LOW)
        r.co[:, columns] = tn(r.cross_p[g], r.cross_v[g]).astype(LOW)

    loads["cross_out"].wait()
    total = r.res[...] + nn(r.co[...], r.w_cross_out[...])
    r.res[...] = total
    r.h2[...], r.unit2[...], r.inv2[...] = norm_rows(total, gain(2))

    rate, cube = 0.7978845608028654, 0.044715
    loads["ffn_in"].wait()
    loads["ffn_out"].wait()

    for c in range(4):
        columns = slice(c * D, (c + 1) * D)
        u = nn(r.h2[...], r.w_ffn_in[:, columns])
        square = u * u
        bend = jnp.tanh(rate * u * (1.0 + cube * square))
        half = 0.5 * (1.0 + bend)
        r.z[c] = (u * half).astype(LOW)
        slope = half + (0.5 * rate) * u * (1.0 - bend * bend) * (1.0 + 3.0 * cube * square)
        r.slope[c] = slope.astype(LOW)
        r.res[...] += nn(r.z[c], r.w_ffn_out[columns, :])

    total = r.res[...]
    r.enc[...] = total.astype(LOW)
    r.src[:SEG, :], r.unit4[...], r.inv4[...] = norm_rows(total, gain(4))
    enc_way = (r.enc, r.enc_out, rows, True, r.es, r.er)
    spread(*enc_way)
    keep_copy(0, *enc_way).start()

    written = r.src[:SEG, :]
    r.wkey[:SEG, :] = nn(written, r.w_writer_qkv[1]).astype(LOW)
    r.wvalue[:SEG, :] = nn(written, r.w_writer_qkv[2]).astype(LOW)
    for g in range(2):
        columns = slice(g * 256, (g + 1) * 256)
        keys = r.wkey[:, columns]
        scores = nt(keys, r.wquery[g])
        key_pos = lax.broadcasted_iota(jnp.int32, scores.shape, 0)
        scores = jnp.where((key_pos >= SEG) | (key_pos < live), scores, SHUT)
        powers = jnp.exp(scores - jnp.max(scores, axis=0, keepdims=True))
        probs = powers * (1.0 / jnp.sum(powers, axis=0, keepdims=True))
        probs_low = probs.astype(LOW)
        mixed = own_blocks(tn(r.wvalue[:, columns], probs_low)).astype(LOW).astype(F32)
        r.wo[:, columns] = swap(mixed).astype(LOW)
        dprobs = nt(r.wvalue[:, columns], r.dmix[g])
        delta = jnp.sum(probs * dprobs, axis=0, keepdims=True)
        slopes = (probs * (dprobs - delta)).astype(LOW)
        dquery = own_blocks(tn(slopes, keys)).astype(LOW).astype(F32)
        r.dwq[:, columns] = (dquery * SCALE).astype(LOW)
        r.wkey[:, columns] = nn(slopes, r.wquery[g]).astype(LOW)
        r.wvalue[:, columns] = nn(probs_low, r.dmix[g]).astype(LOW)

    r.new_slots[...] = (
        r.mem[...].astype(F32) + nn(r.wo[...], r.w_writer_out[...])
    ).astype(LOW)
    new_way = (r.new_slots, r.new_memory, slots, False, r.us, r.ur)
    spread(*new_way)
    keep_copy(1, *new_way).start()

    def put(block, values):
        r.grad[block * D : (block + 1) * D, :] = values.astype(LOW)

    grad = nt(r.wkey[:SEG, :], r.w_writer_qkv[1]) + nt(r.wvalue[:SEG, :], r.w_writer_qkv[2])
    loads["cot"].wait()
    for k in range(3):
        gather_copy(r.out_cot, r.cot_all, r.cs, r.cr, k).wait()
    add_gain(4, grad * r.unit4[...])
    total = r.cot_all[...].astype(F32) + norm_back(grad, r.unit4[...], r.inv4[...], gain(4))
    r.res[...] = total
    r.low[...] = total.astype(LOW)
    put(BLOCK["writer_qkv"], tn(hm, r.dwq[...]))
    put(BLOCK["writer_qkv"] + 1, tn(r.src[...], r.wkey[...]))
    put(BLOCK["writer_qkv"] + 2, tn(r.src[...], r.wvalue[...]))
    put(BLOCK["writer_out"], tn(r.wo[...], mem_cot))
    tick()

    for c in range(4):
        columns = slice(c * D, (c + 1) * D)
        put(BLOCK["ffn"] + 2 * c, tn(r.z[c], r.low[...]))
        tick()
        r.z[c] = (nt(r.low[...], r.w_ffn_out[columns, :]) * r.slope[c].astype(F32)).astype(LOW)
        put(BLOCK["ffn"] + 2 * c + 1, tn(r.h2[...], r.z[c]))
        back = nt(r.z[c], r.w_ffn_in[:, columns])
        r.acc[...] = back if c == 0 else r.acc[...] + back
        tick()

    grad, unit = r.acc[...], r.unit2[...]
    add_gain(2, grad * unit)
    total = r.res[...] + norm_back(grad, unit, r.inv2[...], gain(2))
    r.res[...] = total
    r.low[...] = total.astype(LOW)
    tick()

    r.dsend[...] = nt(r.low[...], r.w_cross_out[...]).astype(LOW)
    put(BLOCK["cross_out"], tn(r.co[...], r.low[...]))
    tick()
    for g in range(2):
        columns = slice(g * 256, (g + 1) * 256)
        dmix, queries = r.dsend[:, columns], r.cq[:, columns]
        dprobs = nt(r.cross_v[g], dmix)
        probs = r.cross_p[g].astype(F32)
        delta = jnp.sum((probs * dprobs).reshape(4, slots, SEG), axis=1, keepdims=True)
        slopes = (probs * (dprobs.reshape(4, slots, SEG) - delta).reshape(256, SEG)).astype(LOW)
        r.dck[:, columns] = own_blocks(nn(slopes, queries)).astype(LOW)
        r.dcv[:, columns] = own_blocks(nn(r.cross_p[g], dmix)).astype(LOW)
        r.cq[:, columns] = (tn(slopes, r.cross_k[g]).astype(LOW).astype(F32) * SCALE).astype(LOW)
    tick()
    r.acc[...] = nt(r.cq[...], r.w_cross_qkv[0])

    grad, unit = r.acc[...], r.unit1[...]
    add_gain(1, grad * unit)
    total = r.res[...] + norm_back(grad, unit, r.inv1[...], gain(1))
    r.res[...] = total
    r.low[...] = total.astype(LOW)
    tick()
    put(BLOCK["cross_qkv"], tn(r.h1[...], r.cq[...]))
    put(BLOCK["cross_qkv"] + 1, tn(hm, r.dck[...]))
    put(BLOCK["cross_qkv"] + 2, tn(hm, r.dcv[...]))
    tick()

    dmix = nt(r.low[...], r.w_self_out[...]).astype(LOW).astype(F32) * r.inv_total[...]
    r.dsend[...] = dmix.astype(LOW)
    product = dmix * r.mix[...].astype(F32)
    upper = product.astype(LOW)
    lower = (product - upper.astype(F32)).astype(LOW)
    head_rows = lax.div(lax.broadcasted_iota(jnp.int32, (16, D), 1), HD)
    head_rows = (head_rows == lax.broadcasted_iota(jnp.int32, (16, D), 0)).astype(F32).astype(LOW)
    r.delta[...] = nt(head_rows, upper) + nt(head_rows, lower)
    put(BLOCK["self_out"], tn(r.mix[...], r.low[...]))
    tick()

    for p in range(PAIRS):
        columns = slice(p * 128, (p + 1) * 128)
        r.dk_sum[...] = jnp.zeros_like(r.dk_sum)
        r.dv_sum[...] = jnp.zeros_like(r.dv_sum)
        for i in range(BLOCKS):
            depth = 128 * (i + 1)
            here = slice(i * 128, (i + 1) * 128)
            stacked = head_stack(r.dsend[here, columns].astype(F32)).astype(LOW)
            queries = head_stack(r.q[here, columns].astype(F32)).astype(LOW)
            probs = r.prob[p, BLOCK_ROWS[i] : BLOCK_ROWS[i + 1], :]
            dprobs = nt(r.v[:depth, columns], stacked)
            delta = jnp.concatenate([r.delta[2 * p + h : 2 * p + h + 1, here] for h in range(2)], axis=1)
            slopes = (probs.astype(F32) * (dprobs - delta)).astype(LOW)
            r.dk_sum[:depth, :] += nn(slopes, queries)
            r.dv_sum[:depth, :] += nn(probs, stacked)
            dquery = head_pick(tn(slopes, r.k[:depth, columns]))
            r.q[here, columns] = (dquery.astype(LOW).astype(F32) * SCALE).astype(LOW)
            if i == 2:
                tick()
        r.k[:, columns] = r.dk_sum[...].astype(LOW)
        r.v[:, columns] = r.dv_sum[...].astype(LOW)
        tick()
    for k, grad in enumerate((r.q, r.k, r.v)):
        put(BLOCK["self_qkv"] + k, tn(r.h0[...], grad[...]))
    tick()
    r.acc[...] = (
        nt(r.q[...], r.w_self_qkv[0]) + nt(r.k[...], r.w_self_qkv[1]) + nt(r.v[...], r.w_self_qkv[2])
    )
    spread_wait(*enc_way)
    keep_copy(0, *enc_way).wait()

    grad, unit = r.acc[...], r.unit0[...]
    add_gain(0, grad * unit)
    total = r.res[...] + norm_back(grad, unit, r.inv0[...], gain(0))
    r.enc[...] = total.astype(LOW)
    grad_way = (r.enc, r.input_grad, rows, True, r.gs, r.gr)
    spread(*grad_way)
    keep_copy(2, *grad_way).start()
    tick()

    dhm = (
        nt(r.dwq[...], r.w_writer_qkv[0])
        + nt(r.wkey[slot_range, :], r.w_writer_qkv[1])
        + nt(r.wvalue[slot_range, :], r.w_writer_qkv[2])
        + nt(r.dck[...], r.w_cross_qkv[1])
        + nt(r.dcv[...], r.w_cross_qkv[2])
    )
    unit = r.unit3[...]
    add_gain(3, dhm * unit)
    r.slot_grad[...] = (
        mem_cot.astype(F32) + norm_back(dhm, unit, r.inv3[...], gain(3))
    ).astype(LOW)
    slot_way = (r.slot_grad, r.memory_grad, slots, False, r.ms, r.mr)
    spread(*slot_way)
    keep_copy(3, *slot_way).start()
    r.gain_steps[0] = jnp.concatenate(
        [jnp.sum(r.gain_sum[k], axis=0, keepdims=True) for k in range(5)] + [jnp.zeros((3, D), F32)], axis=0
    )
    tick()
    tick()
    last = pltpu.make_async_copy(r.gain_steps.at[STAGES], r.gains_grad, r.out_sem.at[4])
    last.start()
    last.wait()
    for k, way in enumerate((enc_way, new_way, grad_way, slot_way)):
        if k > 0:
            spread_wait(*way)
            keep_copy(k, *way).wait()


def finish_kernel(enc, new, in_grad, mem_grad, grads, gains, *refs):
    outs, (low, wide, row_low, row_wide, slot_low, slot_wide, enc_low, new_low, gain_wide, load_sem, store_sem,
           pass_sem) = refs[:13], refs[13:]
    (o_enc, o_new, o_in, o_mem, self_qkv, self_out, cross_qkv, cross_out, ffn_in, ffn_out, writer_qkv,
     writer_out, o_gains) = outs
    slots = wide.shape[0]

    def place(block):
        for name, ref in (("writer_qkv", writer_qkv), ("cross_qkv", cross_qkv), ("self_qkv", self_qkv)):
            if 0 <= block - BLOCK[name] < 3:
                return ref.at[block - BLOCK[name]]
        for name, ref in (("writer_out", writer_out), ("cross_out", cross_out), ("self_out", self_out)):
            if block == BLOCK[name]:
                return ref
        c, second = divmod(block - BLOCK["ffn"], 2)
        return (ffn_in.at[:, pl.ds(c * D, D)] if second else ffn_out.at[pl.ds(c * D, D), :])

    count = GRAD_ROWS // D
    loads = [
        pltpu.make_async_copy(grads.at[pl.ds(k * D, D)], low.at[pl.ds(k * D, D)], load_sem.at[k])
        for k in range(count)
    ]
    rest = [
        pltpu.make_async_copy(source, target, pass_sem.at[k])
        for k, (source, target) in enumerate(
            ((in_grad, row_low), (mem_grad, slot_low), (enc, enc_low), (new, new_low), (gains, gain_wide))
        )
    ]
    for copy in loads + rest:
        copy.start()
    stores = []
    for k in range(count):
        loads[k].wait()
        if k >= slots:
            stores[k - slots].wait()

        def turn(here, t):
            wide[k % slots, here, :] = low[rows_at(k * D + t * 128, 128), :].astype(F32)

        tiles(D, 128, turn)
        stores.append(pltpu.make_async_copy(wide.at[k % slots], place(k), store_sem.at[k % slots]))
        stores[k].start()
    ways = (
        (row_low, row_wide, o_in), (slot_low, slot_wide, o_mem), (enc_low, enc_low, o_enc), (new_low, new_low, o_new),
        (gain_wide, gain_wide, o_gains),
    )
    for k, (read, held, out) in enumerate(ways):
        rest[k].wait()
        if read is not held:
            held[...] = read[...].astype(F32)
        stores.append(pltpu.make_async_copy(held, out, store_sem.at[slots + k]))
        stores[-1].start()
    for copy in stores[count - slots :]:
        copy.wait()


def on_device(*arguments):
    seg_input, memory = arguments[0], arguments[1]
    docs, rows, _ = seg_input.shape
    slots = memory.shape[1]
    docs_count = lax.axis_size("docs")
    scratch = scratch_of(docs, rows, slots, dict(zip(INPUTS, arguments)), docs_count)
    smem, anywhere = pl.BlockSpec(memory_space=pltpu.SMEM), pl.BlockSpec(memory_space=pl.ANY)
    arguments = list(arguments)
    for k in (0, 1, 13, 14):
        arguments[k] = arguments[k].reshape(-1, D)
    names = INPUTS + OUTPUTS + tuple(scratch)
    low = lambda *shape: jax.ShapeDtypeStruct(shape, LOW)
    full = lambda *shape: jax.ShapeDtypeStruct(shape, F32)
    parts = pl.pallas_call(
        functools.partial(layer_kernel, docs, rows, slots, docs_count, names),
        out_shape=(
            low(docs * rows, D), low(docs * slots, D), low(docs * rows, D), low(docs * slots, D),
            low(GRAD_ROWS, D), full(8, D),
        ),
        in_specs=[
            smem if name in ("lengths", "seg_index") else anywhere for name in INPUTS
        ],
        out_specs=(anywhere,) * 6,
        scratch_shapes=list(scratch.values()),
        compiler_params=pltpu.CompilerParams(
            collective_id=1, has_side_effects=True, vmem_limit_bytes=VMEM_BYTES
        ),
    )(*arguments)
    shapes = dict(zip(INPUTS, (full(*argument.shape) for argument in arguments)))
    results = pl.pallas_call(
        finish_kernel,
        out_shape=(
            low(docs * rows, D), low(docs * slots, D), full(docs * rows, D), full(docs * slots, D),
            *(shapes[name] for name in INPUTS[4:12]), full(8, D),
        ),
        in_specs=[pl.BlockSpec(memory_space=pltpu.HBM)] * 6,
        out_specs=(pl.BlockSpec(memory_space=pltpu.HBM),) * 13,
        scratch_shapes=[
            pltpu.VMEM((GRAD_ROWS, D), LOW),
            pltpu.VMEM((6, D, D), F32),
            pltpu.VMEM((docs * rows, D), LOW),
            pltpu.VMEM((docs * rows, D), F32),
            pltpu.VMEM((docs * slots, D), LOW),
            pltpu.VMEM((docs * slots, D), F32),
            pltpu.VMEM((docs * rows, D), LOW),
            pltpu.VMEM((docs * slots, D), LOW),
            pltpu.VMEM((8, D), F32),
            pltpu.SemaphoreType.DMA((GRAD_ROWS // D,)),
            pltpu.SemaphoreType.DMA((6 + 5,)),
            pltpu.SemaphoreType.DMA((5,)),
        ],
        compiler_params=pltpu.CompilerParams(vmem_limit_bytes=VMEM_BYTES),
    )(*parts)
    results = list(results)
    for k in (0, 2):
        results[k] = results[k].reshape(docs, rows, D)
    for k in (1, 3):
        results[k] = results[k].reshape(docs, slots, D)
    results[12] = results[12][:5]
    return tuple(results)


def solution(mesh):
    row, slot, whole = P("docs", "seq", None), P("docs", None, None), P()
    return jax.shard_map(
        on_device,
        mesh=mesh,
        in_specs=(row, slot, P("docs"), P("docs")) + (whole,) * 9 + (row, slot),
        out_specs=(row, slot, row, slot) + (whole,) * 9,
        check_vma=False,
    )
```

```python
import functools
import types

import jax
import jax.numpy as jnp
from jax import lax
from jax.experimental import pallas as pl
from jax.experimental.pallas import tpu as pltpu
from jax.sharding import PartitionSpec as P

MESH = pl.DeviceIdType.MESH
F32, LOW = jnp.float32, jnp.bfloat16
VMEM_BYTES = 63 << 20
D = 512
HD = 64
SEG = 512
SHUT = -1e30
SCALE = HD ** (-0.5)

CORE, X, Y, Z0, Z1 = ("seq", 1), ("seq", 2), ("docs", 1), ("docs", 2), ("docs", 4)
SINGLE = (CORE, X, Y, Z0, Z1)
PUSH, MIDDLE = "push", "middle"
ORDERS = dict(
    X=(CORE, X, Y, PUSH, MIDDLE), Y=(CORE, Y, X, PUSH, MIDDLE), A=(CORE, Z0, X, Y, Z1), B=(CORE, Z0, Y, X, Z1),
)
UNITS = {
    "Wa": (0, 512, "Y"),
    "Wb": (512, 1024, "X"),
    "Wc": (1536, 512, "B"),
    "F0a": (2048, 512, "A"),
    "F0b": (2560, 512, "Y"),
    "F1a": (3072, 1024, "B"),
    "F2a": (4096, 1024, "X"),
    "F3a": (5120, 512, "Y"),
    "F3b": (5632, 512, "Y"),
    "Xa": (6144, 512, "B"),
    "Xb": (6656, 512, "X"),
    "Xc": (7168, 512, "Y"),
    "Xd": (7680, 512, "X"),
    "Sa": (8192, 512, "B"),
    "Qa": (8704, 512, "Y"),
    "Qb": (9216, 512, "Y"),
    "Qc": (9728, 512, "B"),
}
SCHEDULE = (
    ("Wb", "Wa", "Wc",),
    (),
    ("F0a", "F0b", "Wb", "Wa", "Wc",),
    ("F0a", "F0b",),
    ("F1a",),
    (),
    ("F2a", "F1a", "Wa", "Wc",),
    (),
    ("F3a", "F3b", "F0b", "Wb", "F2a", "F0a",),
    ("Wa", "F3a", "Wc", "F3b",),
    (),
    (),
    ("F0b",),
    ("Xa", "Xb", "Xc", "Xd", "F1a", "Wb",),
    ("Sa", "Xa", "Xc", "Xd", "Wa", "F3a", "Xb", "F0b", "Sa", "F2a",),
    (),
    (),
    (),
    ("F3b", "Wb", "F0a", "Wa",),
    ("Wc", "F0b",),
    (),
    (),
    (),
    ("Qc", "Qb", "Qa", "F1a", "Xd", "Xa", "F3a", "Wb", "Wa", "Xc", "Sa", "Qc", "Qb", "F0b", "Qa",),
    ("F2a", "F3a", "Wc", "Wb", "Wa", "F0a", "Xb", "F3b",),
    ("F1a", "Xd",),
    (
        "gains", "Qc", "Xc", "Xa", "F3a", "Sa", "F0b", "F2a", "Wc", "Qb", "F3a", "Wb", "F3b", "F2a", "F0a",
        "Wa", "Qa", "F1a", "Xd", "Xb", "F3a", "gains", "F3b", "Xa", "Xc", "Sa", "Qc", "F2a", "F0b", "F0a",
        "Wc", "F1a", "Wb", "Xb", "Xd", "Qb", "F3b", "Qa", "Xa", "Wa", "Xc", "F2a", "gains", "F3a", "Sa",
        "Xb", "Qc", "Wa", "Qb", "Xd", "F3b", "F1a", "F0b", "Qa", "Xc", "F0a", "Xa", "F0b", "Xb", "Sa", "Wc",
        "Qc", "Xd", "Qb", "gains", "Qa", "Wb", "Xc", "F2a", "Xb", "Wb", "F3b", "Qb", "F3a", "Qa", "F0a",
        "Wc", "Xa", "F3a", "Sa", "Qc", "F1a", "Wc", "Xc", "Qb", "gains", "Xd", "Qa", "Xb", "F0a", "F2a",
        "F3b", "F0a", "Qc", "Xa", "F2a", "F3b", "Qb", "Sa", "F1a", "Xd", "Xc", "F1a", "Xd", "Qa", "Xc",
        "gains", "Xa", "Qc", "Xa", "Xb", "Qb", "Sa", "Xb", "Qb", "Sa", "Qa", "Qc", "Qa", "Qc",
    ),
)
GROUP = 8


def bit_of(axis, stride):
    return lax.rem(lax.div(lax.axis_index(axis), stride), 2)


def in_middle():
    return bit_of("docs", 2) != bit_of("docs", 4)


def place_of(stage):
    if stage == MIDDLE:
        low_bit, bit = bit_of("docs", 2), bit_of("docs", 4)
        return bit, {"docs": lax.axis_index("docs") + 2 * (1 - 2 * low_bit) + 4 * (1 - 2 * bit)}
    axis, stride = Z0 if stage == PUSH else stage
    bit = bit_of(axis, stride)
    return bit, {axis: lax.axis_index(axis) + stride * (1 - 2 * bit)}


def outer_partners(docs_count):
    index = lax.axis_index("docs")
    return [{"docs": lax.rem(index + GROUP * k, docs_count)} for k in range(1, docs_count // GROUP)]


def outer_bits(docs_count):
    return (docs_count // GROUP).bit_length() - 1


def partners_of(docs_count):
    return [place_of(stage)[1] for stage in SINGLE + (MIDDLE,)] + outer_partners(docs_count)


BLOCK = dict(
    writer_qkv=0, writer_out=3, ffn=4, cross_out=12, cross_qkv=13, self_out=16, self_qkv=17,
)
GRAD_ROWS = 20 * 512
STAGES = 5
LANDING, LANDED_ROWS = {}, 0
for _name, (_base, _rows, _order) in UNITS.items():
    LANDING[_name] = LANDED_ROWS
    LANDED_ROWS += _rows + (_rows // 16 if PUSH in ORDERS[_order] else 0)


class Summer:
    def __init__(self, r, docs_count, share):
        self.r, self.share, self.docs_count = r, share, docs_count
        self.index = {name: k for k, name in enumerate(UNITS)}
        self.at, self.store = {}, {}
        self.middle = in_middle()

    def remote(self, source, target, name, j, partner):
        k = self.index[name]
        return pltpu.make_async_remote_copy(
            src_ref=source, dst_ref=target, send_sem=self.r.unit_s.at[k], recv_sem=self.r.unit_r.at[k, j],
            device_id=partner, device_id_type=MESH,
        )

    def other(self, source, target, sems, k, j, partner):
        return pltpu.make_async_remote_copy(
            src_ref=source, dst_ref=target, send_sem=sems[0].at[k, j], recv_sem=sems[1].at[k, j],
            device_id=partner, device_id_type=MESH,
        )

    def only(self, inside, body):
        if inside:
            pl.when(self.middle)(body)
        else:
            body()

    def lined(self, name):
        return PUSH in ORDERS[UNITS[name][2]]

    def give(self, name, j, start, size, first):
        r = self.r
        stage = ORDERS[UNITS[name][2]][j]
        bit, partner = place_of(stage)
        if stage == PUSH:
            half, sent, kept = size, start, start
        else:
            half = size // 2
            sent, kept = start + (1 - bit) * half, start + bit * half
        copy = self.remote(
            r.grad.at[rows_at(sent, half)], r.landed.at[pl.ds(first, half)], name, j, partner
        )
        if stage == PUSH:
            pl.when(jnp.logical_not(self.middle))(copy.start)
        else:
            self.only(stage == MIDDLE, copy.start)
        self.at[name] = ("give", j, copy, kept, half, first)

    def given(self, name, j, copy, start, size, first):
        stage = ORDERS[UNITS[name][2]][j]

        def add():
            add_rows(self.r.grad, start, size, self.r.landed, first, self.share if j == 0 else None)

        if stage == PUSH:

            @pl.when(self.middle)
            def _():
                copy.wait_recv()
                add()

            pl.when(jnp.logical_not(self.middle))(copy.wait_send)
        else:

            def both():
                copy.wait()
                add()

            self.only(stage == MIDDLE, both)

    def spread(self, name, j, start, size):
        r = self.r
        stage = ORDERS[UNITS[name][2]][j]
        bit, partner = place_of(stage)
        here = rows_at(start, size)
        source = r.grad if j == STAGES - 1 else r.grads
        copy = self.remote(source.at[here], r.grads.at[here], name, 2 * STAGES - 1 - j, partner)
        self.only(stage in (PUSH, MIDDLE), copy.start)
        if stage == PUSH:
            self.at[name] = ("spread", j, copy, start, size, None)
        else:
            self.at[name] = ("spread", j, copy, start - bit * size, 2 * size, None)

    def spread_done(self, name, j, copy):
        stage = ORDERS[UNITS[name][2]][j]
        if stage == PUSH:
            pl.when(self.middle)(copy.wait_send)
            pl.when(jnp.logical_not(self.middle))(copy.wait_recv)
        else:
            self.only(stage == MIDDLE, copy.wait)
        if j == STAGES - 1:
            self.only(self.lined(name), self.store[name].wait)

    def own(self, name, start, size):
        here = rows_at(start, size)
        return pltpu.make_async_copy(
            self.r.grad.at[here], self.r.grads.at[here], self.r.own_sem.at[self.index[name]]
        )

    def step(self, name):
        if name == "gains":
            return self.step_gains()
        base, rows, order = UNITS[name]
        if name not in self.at:
            return self.give(name, 0, base, rows, LANDING[name])
        kind, j, copy, start, size, first = self.at[name]
        if kind == "give":
            self.given(name, j, copy, start, size, first)
            if j + 1 < STAGES:
                return self.give(name, j + 1, start, size, first + size)
            self.only(self.lined(name), lambda: self.outer(name, start, size))
            self.store[name] = self.own(name, start, size)
            self.only(self.lined(name), self.store[name].start)
            self.spread(name, j, start, size)
        else:
            self.spread_done(name, j, copy)
            if j > 0:
                self.spread(name, j - 1, start, size)
            else:
                self.at[name] = None

    def outer(self, name, start, size):
        others = outer_partners(self.docs_count)
        if not others:
            return
        r = self.r
        here = rows_at(start, size)
        share = pl.ds(UNITS[name][0] // 16, size)
        for b in range(outer_bits(self.docs_count)):
            partner = place_of(("docs", GROUP << b))[1]
            copy = self.other(
                r.grad.at[here], r.outer.at[b, share], (r.outer_s, r.outer_r), self.index[name], b, partner
            )
            copy.start()
            copy.wait()
            r.grad[here, :] = (r.grad[here, :].astype(F32) + r.outer[b, share, :].astype(F32)).astype(LOW)

    def step_gains(self):
        r = self.r
        j = self.at.get("gains", 0)
        if j > 0:
            self.gain_copy(j - 1).wait()
            more = r.gain_landed[j - 1]
            if j == 1:
                more = more * self.share
            r.gain_steps[j] = r.gain_steps[j - 1] + more
        if j < STAGES:
            self.gain_copy(j).start()
        else:
            others = outer_partners(self.docs_count)
            if others:
                mine = lax.div(lax.axis_index("docs"), GROUP)
                r.gain_outer[mine] = r.gain_steps[j]
                copies = [
                    self.other(r.gain_steps.at[j], r.gain_outer.at[mine], (r.gain_os, r.gain_or), 0, k, partner)
                    for k, partner in enumerate(others)
                ]
                for copy in copies:
                    copy.start()
                for copy in copies:
                    copy.wait()
                r.gain_steps[j] = sum(r.gain_outer[k] for k in range(len(others) + 1))
        self.at["gains"] = j + 1

    def gain_copy(self, j):
        r = self.r
        partner = place_of(SINGLE[j])[1]
        return self.other(r.gain_steps.at[j], r.gain_landed.at[j], (r.gain_s, r.gain_r), 0, j, partner)


def add_rows(total, start, rows, landed, first, share=None):
    tile = min(rows, 128)

    def turn(t, carry):
        here = rows_at(start + t * tile, tile)
        more = landed[rows_at(first + t * tile, tile), :].astype(F32)
        if share is not None:
            more = more * share
        total[here, :] = (total[here, :].astype(F32) + more).astype(total.dtype)
        return carry

    lax.fori_loop(0, rows // tile, turn, 0)


def dot(left, right, left_dim, right_dim):
    return lax.dot_general(
        left, right, (((left_dim,), (right_dim,)), ((), ())), preferred_element_type=F32
    )


def nn(left, right):
    return dot(left, right, 1, 0)


def nt(left, right):
    return dot(left, right, 1, 1)


def tn(left, right):
    return dot(left, right, 0, 0)


def tiles(rows, tile, body):
    def turn(t, carry):
        body(pl.ds(pl.multiple_of(t * tile, tile), tile), t)
        return carry

    lax.fori_loop(0, rows // tile, turn, 0)


def rows_at(start, size):
    return pl.ds(pl.multiple_of(start, 16), size)


def norm_rows(values, gain_row):
    centered = values - jnp.mean(values, axis=-1, keepdims=True)
    inverse = lax.rsqrt(jnp.mean(centered * centered, axis=-1, keepdims=True) + 1e-05)
    unit = centered * inverse
    return (unit * gain_row).astype(LOW), unit, inverse


def norm_back(grad, unit, inverse, gain_row):
    scaled = grad * gain_row
    adjusted = (
        scaled
        - jnp.mean(scaled, axis=-1, keepdims=True)
        - unit * jnp.mean(scaled * unit, axis=-1, keepdims=True)
    )
    return adjusted * inverse


def same_head():
    left = lax.div(lax.broadcasted_iota(jnp.int32, (256, 256), 0), HD)
    right = lax.div(lax.broadcasted_iota(jnp.int32, (256, 256), 1), HD)
    return left == right


def four_heads(values):
    return jnp.where(same_head(), jnp.concatenate([values] * 4, axis=0), 0.0)


def own_blocks(values):
    return jnp.sum(jnp.where(same_head(), values, 0.0).reshape(4, HD, 256), axis=0)


def swap(values):
    return own_blocks(four_heads(values).T)


def head_stack(values):
    low_half = lax.broadcasted_iota(jnp.int32, values.shape, 1) < HD
    return jnp.concatenate(
        [jnp.where(low_half, values, 0.0), jnp.where(low_half, 0.0, values)], axis=0
    )


def head_pick(values):
    first_head = lax.broadcasted_iota(jnp.int32, (128, 128), 1) < HD
    return jnp.where(first_head, values[:128], values[128:])


BLOCKS = SEG // 128
BLOCK_ROWS = [sum(128 * (k + 1) for k in range(i)) for i in range(BLOCKS + 1)]
PAIRS = D // 128

WEIGHTS = (
    "self_qkv", "cross_qkv", "writer_qkv", "writer_out", "self_out", "cross_out", "ffn_in", "ffn_out",
)
INPUTS = (
    "x", "memory", "lengths", "seg_index", "self_qkv", "self_out", "cross_qkv", "cross_out",
    "ffn_in", "ffn_out", "writer_qkv", "writer_out", "gains", "out_cot", "mem_cot",
)
OUTPUTS = ("enc_out", "new_memory", "input_grad", "memory_grad", "grads", "gains_grad")
def scratch_of(docs, rows, slots, weights, docs_count):
    keys = SEG + slots
    units, outers = len(UNITS), max(1, docs_count // GROUP)
    dma = pltpu.SemaphoreType.DMA
    low = lambda *shape: pltpu.VMEM(shape, LOW)
    full = lambda *shape: pltpu.VMEM(shape, F32)
    fetched = {"w_" + name: pltpu.VMEM(weights[name].shape, LOW) for name in WEIGHTS}
    return dict(
        **fetched,
        mem=low(slots, D),
        mem_back=low(slots, D),
        gain_rows=full(5, D),
        x_all=low(SEG, D),
        cot_all=low(SEG, D),
        enc=low(SEG, D),
        slot_grad=low(slots, D),
        new_slots=low(slots, D),
        unit0=full(SEG, D),
        unit1=full(SEG, D),
        unit2=full(SEG, D),
        unit4=full(SEG, D),
        unit3=full(slots, D),
        inv0=full(SEG, 1),
        inv1=full(SEG, 1),
        inv2=full(SEG, 1),
        inv4=full(SEG, 1),
        inv3=full(slots, 1),
        h0=low(SEG, D),
        h1=low(SEG, D),
        h2=low(SEG, D),
        src=low(keys, D),
        q=low(SEG, D),
        k=low(SEG, D),
        v=low(SEG, D),
        prob=low(PAIRS, BLOCK_ROWS[-1], 256),
        mix=low(SEG, D),
        inv_total=full(SEG, D),
        acc=full(SEG, D),
        res=full(SEG, D),
        cq=low(SEG, D),
        cross_k=low(2, 256, 256),
        cross_v=low(2, 256, 256),
        cross_p=low(2, 256, SEG),
        co=low(SEG, D),
        z=low(4, SEG, D),
        slope=low(4, SEG, D),
        wkey=low(keys, D),
        wvalue=low(keys, D),
        wquery=low(2, 256, 256),
        dmix=low(2, 256, 256),
        wo=low(slots, D),
        dwq=low(slots, D),
        dck=low(slots, D),
        dcv=low(slots, D),
        low=low(SEG, D),
        dsend=low(SEG, D),
        delta=full(16, SEG),
        dk_sum=full(SEG, 128),
        dv_sum=full(SEG, 128),
        gain_sum=full(5, 8, D),
        gain_steps=full(STAGES + 1, 8, D),
        gain_landed=full(STAGES, 8, D),
        gain_outer=full(outers, 8, D),
        grad=low(GRAD_ROWS, D),
        landed=low(LANDED_ROWS, D),
        outer=low(*((outer_bits(docs_count), GRAD_ROWS // 16, D) if outers > 1 else (1, 16, D))),
        unit_s=dma((units,)),
        unit_r=dma((units, 2 * STAGES)),
        own_sem=dma((units,)),
        outer_s=dma((units if outers > 1 else 1, outers)),
        outer_r=dma((units if outers > 1 else 1, outers)),
        gain_s=dma((1, STAGES)),
        gain_r=dma((1, STAGES)),
        gain_os=dma((1, outers)),
        gain_or=dma((1, outers)),
        load_sem=dma((len(WEIGHTS) + 5,)),
        xs=dma((3,)),
        xr=dma((3,)),
        cs=dma((3,)),
        cr=dma((3,)),
        es=dma((3,)),
        er=dma((3,)),
        us=dma((3,)),
        ur=dma((3,)),
        gs=dma((3,)),
        gr=dma((3,)),
        ms=dma((3,)),
        mr=dma((3,)),
        out_sem=dma((5,)),
    )


def layer_kernel(docs, rows, slots, docs_count, names, *refs):
    r = types.SimpleNamespace(**dict(zip(names, refs)))
    s = lax.axis_index("seq")
    bit0, bit1 = lax.rem(s, 2), lax.div(s, 2)
    near = s + 1 - 2 * bit0
    far = s + 2 - 4 * bit1
    across = near + 2 - 4 * bit1
    peers = (near, far, across)

    def doc_of(index):
        return jnp.minimum(index, docs - 1)

    mine = doc_of(s)

    def remote(source, target, send_sem, recv_sem, to):
        return pltpu.make_async_remote_copy(
            src_ref=source, dst_ref=target, send_sem=send_sem, recv_sem=recv_sem,
            device_id={"seq": to}, device_id_type=MESH,
        )

    def gain(k):
        return r.gain_rows[k : k + 1, :]

    def add_gain(k, values):
        r.gain_sum[k] += jnp.sum(values.reshape(-1, 8, D), axis=0)

    barrier = pltpu.get_barrier_semaphore()
    greeted = [{"seq": across}] + partners_of(docs_count)
    for partner in greeted:
        pl.semaphore_signal(barrier, inc=1, device_id=partner, device_id_type=MESH)
    own_rows = rows_at(s * rows, rows)
    doc_rows, doc_slots = rows_at(mine * rows, rows), rows_at(mine * slots, slots)
    fetched = dict(
        mem=(r.memory.at[doc_slots], r.mem),
        gains=(r.gains, r.gain_rows),
        x=(r.x.at[doc_rows], r.x_all.at[own_rows]),
        mem_cot=(r.mem_cot.at[doc_slots], r.mem_back),
        **{name: (getattr(r, name), getattr(r, "w_" + name)) for name in WEIGHTS},
        cot=(r.out_cot.at[doc_rows], r.cot_all.at[own_rows]),
    )
    loads = {}
    for k, (name, (source, target)) in enumerate(fetched.items()):
        loads[name] = pltpu.make_async_copy(source, target, r.load_sem.at[k])
        loads[name].start()
    r.gain_sum[...] = jnp.zeros_like(r.gain_sum)
    loads["mem"].wait()
    loads["gains"].wait()
    slot_range = pl.ds(SEG, slots)
    hm, r.unit3[...], r.inv3[...] = norm_rows(r.mem[...].astype(F32), gain(3))
    r.src[slot_range, :] = hm
    pl.semaphore_wait(barrier, len(greeted))

    def gather_copy(source, target, send_sem, recv_sem, k):
        return remote(
            source.at[rows_at(doc_of(peers[k]) * rows, rows)],
            target.at[rows_at(s * rows, rows)], send_sem.at[k], recv_sem.at[k], peers[k],
        )

    for k in range(3):
        gather_copy(r.x, r.x_all, r.xs, r.xr, k).start()

    def spread_copy(source, target, size, own, send_sem, recv_sem, k):
        piece = source.at[rows_at(peers[k] * size, size)] if own else source
        return remote(
            piece, target.at[rows_at(mine * size, size)], send_sem.at[k], recv_sem.at[k], peers[k]
        )

    def keep_copy(k, source, target, size, own, *sems):
        piece = source.at[rows_at(s * size, size)] if own else source
        return pltpu.make_async_copy(piece, target.at[rows_at(mine * size, size)], r.out_sem.at[k])

    summer = Summer(r, docs_count, 1.0 - bit1.astype(F32))
    ticks = iter(SCHEDULE)

    def tick():
        for name in next(ticks):
            summer.step(name)

    def spread(*where):
        spread_copy(*where, 1).start()

        @pl.when(bit1 == 0)
        def _():
            spread_copy(*where, 0).start()
            spread_copy(*where, 2).start()

    def spread_wait(*where):
        spread_copy(*where, 1).wait()

        @pl.when(bit1 == 0)
        def _():
            spread_copy(*where, 0).wait()
            spread_copy(*where, 2).wait_send()

        @pl.when(bit1 == 1)
        def _():
            spread_copy(*where, 2).wait_recv()

    def place_heads(target, values):
        for g in range(2):
            piece = values[:, g * 256 : (g + 1) * 256].astype(LOW).astype(F32)
            target[g] = four_heads(piece).astype(LOW)

    loads["cross_qkv"].wait()
    place_heads(r.cross_k, nn(hm, r.w_cross_qkv[1]))
    place_heads(r.cross_v, nn(hm, r.w_cross_qkv[2]))
    loads["writer_qkv"].wait()
    r.wkey[slot_range, :] = nn(hm, r.w_writer_qkv[1]).astype(LOW)
    r.wvalue[slot_range, :] = nn(hm, r.w_writer_qkv[2]).astype(LOW)
    place_heads(r.wquery, nn(hm, r.w_writer_qkv[0]) * SCALE)
    loads["writer_out"].wait()
    loads["mem_cot"].wait()
    mem_cot = r.mem_back[...]
    place_heads(r.dmix, nt(mem_cot, r.w_writer_out[...]))

    def enter(start):
        here = rows_at(start, SEG // 2)
        normed, unit, inverse = norm_rows(r.x_all[here, :].astype(F32), gain(0))
        r.unit0[here, :] = unit
        r.inv0[here, :] = inverse
        r.h0[here, :] = normed
        r.q[here, :] = (nn(normed, r.w_self_qkv[0]) * SCALE).astype(LOW)
        r.k[here, :] = nn(normed, r.w_self_qkv[1]).astype(LOW)
        r.v[here, :] = nn(normed, r.w_self_qkv[2]).astype(LOW)

    loads["x"].wait()
    loads["self_qkv"].wait()
    gather_copy(r.x, r.x_all, r.xs, r.xr, 0).wait_recv()
    enter(bit1 * (SEG // 2))
    for k in (1, 2):
        gather_copy(r.x, r.x_all, r.xs, r.xr, k).wait_recv()
    for k in range(3):
        gather_copy(r.out_cot, r.cot_all, r.cs, r.cr, k).start()
    enter((1 - bit1) * (SEG // 2))
    for k in range(3):
        gather_copy(r.x, r.x_all, r.xs, r.xr, k).wait_send()
    live = jnp.minimum(r.lengths[mine] - r.seg_index[mine] * SEG, SEG)

    ones = jnp.ones((SEG, 128), LOW)
    for p in range(PAIRS):
        columns = slice(p * 128, (p + 1) * 128)
        for i in range(BLOCKS):
            depth = 128 * (i + 1)
            here = slice(i * 128, (i + 1) * 128)
            stacked = head_stack(r.q[here, columns].astype(F32)).astype(LOW)
            scores = nt(r.k[:depth, columns], stacked)
            key_pos = lax.broadcasted_iota(jnp.int32, scores.shape, 0)
            query_pos = i * 128 + lax.rem(lax.broadcasted_iota(jnp.int32, scores.shape, 1), 128)
            scores = jnp.where((key_pos <= query_pos) & (key_pos < live), scores, SHUT)
            powers = jnp.exp(scores - jnp.max(scores, axis=0, keepdims=True)).astype(LOW)
            r.prob[p, BLOCK_ROWS[i] : BLOCK_ROWS[i + 1], :] = powers
            mixed = tn(powers, jnp.concatenate([r.v[:depth, columns], ones[:depth]], axis=1))
            inverse = 1.0 / head_pick(mixed[:, 128:])
            r.inv_total[here, columns] = inverse
            r.mix[here, columns] = (head_pick(mixed[:, :128]) * inverse).astype(LOW)

    loads["self_out"].wait()
    total = r.x_all[...].astype(F32) + nn(r.mix[...], r.w_self_out[...])
    r.res[...] = total
    r.h1[...], r.unit1[...], r.inv1[...] = norm_rows(total, gain(1))
    r.cq[...] = (nn(r.h1[...], r.w_cross_qkv[0]) * SCALE).astype(LOW)

    for g in range(2):
        columns = slice(g * 256, (g + 1) * 256)
        scores = nt(r.cross_k[g], r.cq[:, columns]).reshape(4, slots, SEG)
        powers = jnp.exp(scores - jnp.max(scores, axis=1, keepdims=True))
        inverse = 1.0 / jnp.sum(powers, axis=1, keepdims=True)
        r.cross_p[g] = (powers * inverse).reshape(256, SEG).astype(LOW)
        r.co[:, columns] = tn(r.cross_p[g], r.cross_v[g]).astype(LOW)

    loads["cross_out"].wait()
    total = r.res[...] + nn(r.co[...], r.w_cross_out[...])
    r.res[...] = total
    r.h2[...], r.unit2[...], r.inv2[...] = norm_rows(total, gain(2))

    rate, cube = 0.7978845608028654, 0.044715
    loads["ffn_in"].wait()
    loads["ffn_out"].wait()

    for c in range(4):
        columns = slice(c * D, (c + 1) * D)
        u = nn(r.h2[...], r.w_ffn_in[:, columns])
        square = u * u
        bend = jnp.tanh(rate * u * (1.0 + cube * square))
        half = 0.5 * (1.0 + bend)
        r.z[c] = (u * half).astype(LOW)
        slope = half + (0.5 * rate) * u * (1.0 - bend * bend) * (1.0 + 3.0 * cube * square)
        r.slope[c] = slope.astype(LOW)
        r.res[...] += nn(r.z[c], r.w_ffn_out[columns, :])

    total = r.res[...]
    r.enc[...] = total.astype(LOW)
    r.src[:SEG, :], r.unit4[...], r.inv4[...] = norm_rows(total, gain(4))
    enc_way = (r.enc, r.enc_out, rows, True, r.es, r.er)
    spread(*enc_way)
    keep_copy(0, *enc_way).start()

    written = r.src[:SEG, :]
    r.wkey[:SEG, :] = nn(written, r.w_writer_qkv[1]).astype(LOW)
    r.wvalue[:SEG, :] = nn(written, r.w_writer_qkv[2]).astype(LOW)
    for g in range(2):
        columns = slice(g * 256, (g + 1) * 256)
        keys = r.wkey[:, columns]
        scores = nt(keys, r.wquery[g])
        key_pos = lax.broadcasted_iota(jnp.int32, scores.shape, 0)
        scores = jnp.where((key_pos >= SEG) | (key_pos < live), scores, SHUT)
        powers = jnp.exp(scores - jnp.max(scores, axis=0, keepdims=True))
        probs = powers * (1.0 / jnp.sum(powers, axis=0, keepdims=True))
        probs_low = probs.astype(LOW)
        mixed = own_blocks(tn(r.wvalue[:, columns], probs_low)).astype(LOW).astype(F32)
        r.wo[:, columns] = swap(mixed).astype(LOW)
        dprobs = nt(r.wvalue[:, columns], r.dmix[g])
        delta = jnp.sum(probs * dprobs, axis=0, keepdims=True)
        slopes = (probs * (dprobs - delta)).astype(LOW)
        dquery = own_blocks(tn(slopes, keys)).astype(LOW).astype(F32)
        r.dwq[:, columns] = (dquery * SCALE).astype(LOW)
        r.wkey[:, columns] = nn(slopes, r.wquery[g]).astype(LOW)
        r.wvalue[:, columns] = nn(probs_low, r.dmix[g]).astype(LOW)

    r.new_slots[...] = (
        r.mem[...].astype(F32) + nn(r.wo[...], r.w_writer_out[...])
    ).astype(LOW)
    new_way = (r.new_slots, r.new_memory, slots, False, r.us, r.ur)
    spread(*new_way)
    keep_copy(1, *new_way).start()

    def put(block, values):
        r.grad[block * D : (block + 1) * D, :] = values.astype(LOW)

    grad = nt(r.wkey[:SEG, :], r.w_writer_qkv[1]) + nt(r.wvalue[:SEG, :], r.w_writer_qkv[2])
    loads["cot"].wait()
    for k in range(3):
        gather_copy(r.out_cot, r.cot_all, r.cs, r.cr, k).wait()
    add_gain(4, grad * r.unit4[...])
    total = r.cot_all[...].astype(F32) + norm_back(grad, r.unit4[...], r.inv4[...], gain(4))
    r.res[...] = total
    r.low[...] = total.astype(LOW)
    put(BLOCK["writer_qkv"], tn(hm, r.dwq[...]))
    put(BLOCK["writer_qkv"] + 1, tn(r.src[...], r.wkey[...]))
    put(BLOCK["writer_qkv"] + 2, tn(r.src[...], r.wvalue[...]))
    put(BLOCK["writer_out"], tn(r.wo[...], mem_cot))
    tick()

    for c in range(4):
        columns = slice(c * D, (c + 1) * D)
        put(BLOCK["ffn"] + 2 * c, tn(r.z[c], r.low[...]))
        tick()
        r.z[c] = (nt(r.low[...], r.w_ffn_out[columns, :]) * r.slope[c].astype(F32)).astype(LOW)
        put(BLOCK["ffn"] + 2 * c + 1, tn(r.h2[...], r.z[c]))
        back = nt(r.z[c], r.w_ffn_in[:, columns])
        r.acc[...] = back if c == 0 else r.acc[...] + back
        tick()

    grad, unit = r.acc[...], r.unit2[...]
    add_gain(2, grad * unit)
    total = r.res[...] + norm_back(grad, unit, r.inv2[...], gain(2))
    r.res[...] = total
    r.low[...] = total.astype(LOW)
    tick()

    r.dsend[...] = nt(r.low[...], r.w_cross_out[...]).astype(LOW)
    put(BLOCK["cross_out"], tn(r.co[...], r.low[...]))
    tick()
    for g in range(2):
        columns = slice(g * 256, (g + 1) * 256)
        dmix, queries = r.dsend[:, columns], r.cq[:, columns]
        dprobs = nt(r.cross_v[g], dmix)
        probs = r.cross_p[g].astype(F32)
        delta = jnp.sum((probs * dprobs).reshape(4, slots, SEG), axis=1, keepdims=True)
        slopes = (probs * (dprobs.reshape(4, slots, SEG) - delta).reshape(256, SEG)).astype(LOW)
        r.dck[:, columns] = own_blocks(nn(slopes, queries)).astype(LOW)
        r.dcv[:, columns] = own_blocks(nn(r.cross_p[g], dmix)).astype(LOW)
        r.cq[:, columns] = (tn(slopes, r.cross_k[g]).astype(LOW).astype(F32) * SCALE).astype(LOW)
    tick()
    r.acc[...] = nt(r.cq[...], r.w_cross_qkv[0])

    grad, unit = r.acc[...], r.unit1[...]
    add_gain(1, grad * unit)
    total = r.res[...] + norm_back(grad, unit, r.inv1[...], gain(1))
    r.res[...] = total
    r.low[...] = total.astype(LOW)
    tick()
    put(BLOCK["cross_qkv"], tn(r.h1[...], r.cq[...]))
    put(BLOCK["cross_qkv"] + 1, tn(hm, r.dck[...]))
    put(BLOCK["cross_qkv"] + 2, tn(hm, r.dcv[...]))
    tick()

    dmix = nt(r.low[...], r.w_self_out[...]).astype(LOW).astype(F32) * r.inv_total[...]
    r.dsend[...] = dmix.astype(LOW)
    product = dmix * r.mix[...].astype(F32)
    upper = product.astype(LOW)
    lower = (product - upper.astype(F32)).astype(LOW)
    head_rows = lax.div(lax.broadcasted_iota(jnp.int32, (16, D), 1), HD)
    head_rows = (head_rows == lax.broadcasted_iota(jnp.int32, (16, D), 0)).astype(F32).astype(LOW)
    r.delta[...] = nt(head_rows, upper) + nt(head_rows, lower)
    put(BLOCK["self_out"], tn(r.mix[...], r.low[...]))
    tick()

    for p in range(PAIRS):
        columns = slice(p * 128, (p + 1) * 128)
        r.dk_sum[...] = jnp.zeros_like(r.dk_sum)
        r.dv_sum[...] = jnp.zeros_like(r.dv_sum)
        for i in range(BLOCKS):
            depth = 128 * (i + 1)
            here = slice(i * 128, (i + 1) * 128)
            stacked = head_stack(r.dsend[here, columns].astype(F32)).astype(LOW)
            queries = head_stack(r.q[here, columns].astype(F32)).astype(LOW)
            probs = r.prob[p, BLOCK_ROWS[i] : BLOCK_ROWS[i + 1], :]
            dprobs = nt(r.v[:depth, columns], stacked)
            delta = jnp.concatenate([r.delta[2 * p + h : 2 * p + h + 1, here] for h in range(2)], axis=1)
            slopes = (probs.astype(F32) * (dprobs - delta)).astype(LOW)
            r.dk_sum[:depth, :] += nn(slopes, queries)
            r.dv_sum[:depth, :] += nn(probs, stacked)
            dquery = head_pick(tn(slopes, r.k[:depth, columns]))
            r.q[here, columns] = (dquery.astype(LOW).astype(F32) * SCALE).astype(LOW)
            if i == 2:
                tick()
        r.k[:, columns] = r.dk_sum[...].astype(LOW)
        r.v[:, columns] = r.dv_sum[...].astype(LOW)
        tick()
    for k, grad in enumerate((r.q, r.k, r.v)):
        put(BLOCK["self_qkv"] + k, tn(r.h0[...], grad[...]))
    tick()
    r.acc[...] = (
        nt(r.q[...], r.w_self_qkv[0]) + nt(r.k[...], r.w_self_qkv[1]) + nt(r.v[...], r.w_self_qkv[2])
    )
    spread_wait(*enc_way)
    keep_copy(0, *enc_way).wait()

    grad, unit = r.acc[...], r.unit0[...]
    add_gain(0, grad * unit)
    total = r.res[...] + norm_back(grad, unit, r.inv0[...], gain(0))
    r.enc[...] = total.astype(LOW)
    grad_way = (r.enc, r.input_grad, rows, True, r.gs, r.gr)
    spread(*grad_way)
    keep_copy(2, *grad_way).start()
    tick()

    dhm = (
        nt(r.dwq[...], r.w_writer_qkv[0])
        + nt(r.wkey[slot_range, :], r.w_writer_qkv[1])
        + nt(r.wvalue[slot_range, :], r.w_writer_qkv[2])
        + nt(r.dck[...], r.w_cross_qkv[1])
        + nt(r.dcv[...], r.w_cross_qkv[2])
    )
    unit = r.unit3[...]
    add_gain(3, dhm * unit)
    r.slot_grad[...] = (
        mem_cot.astype(F32) + norm_back(dhm, unit, r.inv3[...], gain(3))
    ).astype(LOW)
    slot_way = (r.slot_grad, r.memory_grad, slots, False, r.ms, r.mr)
    spread(*slot_way)
    keep_copy(3, *slot_way).start()
    r.gain_steps[0] = jnp.concatenate(
        [jnp.sum(r.gain_sum[k], axis=0, keepdims=True) for k in range(5)] + [jnp.zeros((3, D), F32)], axis=0
    )
    tick()
    tick()
    last = pltpu.make_async_copy(r.gain_steps.at[STAGES], r.gains_grad, r.out_sem.at[4])
    last.start()
    last.wait()
    for k, way in enumerate((enc_way, new_way, grad_way, slot_way)):
        if k > 0:
            spread_wait(*way)
            keep_copy(k, *way).wait()


def finish_kernel(enc, new, in_grad, mem_grad, grads, gains, *refs):
    outs, (low, wide, row_low, row_wide, slot_low, slot_wide, enc_low, new_low, gain_wide, load_sem, store_sem,
           pass_sem) = refs[:13], refs[13:]
    (o_enc, o_new, o_in, o_mem, self_qkv, self_out, cross_qkv, cross_out, ffn_in, ffn_out, writer_qkv,
     writer_out, o_gains) = outs
    slots = wide.shape[0]

    def place(block):
        for name, ref in (("writer_qkv", writer_qkv), ("cross_qkv", cross_qkv), ("self_qkv", self_qkv)):
            if 0 <= block - BLOCK[name] < 3:
                return ref.at[block - BLOCK[name]]
        for name, ref in (("writer_out", writer_out), ("cross_out", cross_out), ("self_out", self_out)):
            if block == BLOCK[name]:
                return ref
        c, second = divmod(block - BLOCK["ffn"], 2)
        return (ffn_in.at[:, pl.ds(c * D, D)] if second else ffn_out.at[pl.ds(c * D, D), :])

    count = GRAD_ROWS // D
    loads = [
        pltpu.make_async_copy(grads.at[pl.ds(k * D, D)], low.at[pl.ds(k * D, D)], load_sem.at[k])
        for k in range(count)
    ]
    rest = [
        pltpu.make_async_copy(source, target, pass_sem.at[k])
        for k, (source, target) in enumerate(
            ((in_grad, row_low), (mem_grad, slot_low), (enc, enc_low), (new, new_low), (gains, gain_wide))
        )
    ]
    for copy in rest + loads:
        copy.start()
    side = []
    ways = (
        (row_low, row_wide, o_in), (slot_low, slot_wide, o_mem), (enc_low, enc_low, o_enc), (new_low, new_low, o_new),
        (gain_wide, gain_wide, o_gains),
    )
    for k, (read, held, out) in enumerate(ways):
        rest[k].wait()
        if read is not held:
            held[...] = read[...].astype(F32)
        side.append(pltpu.make_async_copy(held, out, store_sem.at[slots + k]))
        side[-1].start()
    stores = []
    for k in range(count):
        loads[k].wait()
        if k >= slots:
            stores[k - slots].wait()

        def turn(here, t):
            wide[k % slots, here, :] = low[rows_at(k * D + t * 128, 128), :].astype(F32)

        tiles(D, 128, turn)
        stores.append(pltpu.make_async_copy(wide.at[k % slots], place(k), store_sem.at[k % slots]))
        stores[k].start()
    for copy in side + stores[count - slots :]:
        copy.wait()


def on_device(*arguments):
    seg_input, memory = arguments[0], arguments[1]
    docs, rows, _ = seg_input.shape
    slots = memory.shape[1]
    docs_count = lax.axis_size("docs")
    scratch = scratch_of(docs, rows, slots, dict(zip(INPUTS, arguments)), docs_count)
    smem, anywhere = pl.BlockSpec(memory_space=pltpu.SMEM), pl.BlockSpec(memory_space=pl.ANY)
    arguments = list(arguments)
    for k in (0, 1, 13, 14):
        arguments[k] = arguments[k].reshape(-1, D)
    names = INPUTS + OUTPUTS + tuple(scratch)
    low = lambda *shape: jax.ShapeDtypeStruct(shape, LOW)
    full = lambda *shape: jax.ShapeDtypeStruct(shape, F32)
    parts = pl.pallas_call(
        functools.partial(layer_kernel, docs, rows, slots, docs_count, names),
        out_shape=(
            low(docs * rows, D), low(docs * slots, D), low(docs * rows, D), low(docs * slots, D),
            low(GRAD_ROWS, D), full(8, D),
        ),
        in_specs=[
            smem if name in ("lengths", "seg_index") else anywhere for name in INPUTS
        ],
        out_specs=(anywhere,) * 6,
        scratch_shapes=list(scratch.values()),
        compiler_params=pltpu.CompilerParams(
            collective_id=1, has_side_effects=True, vmem_limit_bytes=VMEM_BYTES
        ),
    )(*arguments)
    shapes = dict(zip(INPUTS, (full(*argument.shape) for argument in arguments)))
    results = pl.pallas_call(
        finish_kernel,
        out_shape=(
            low(docs * rows, D), low(docs * slots, D), full(docs * rows, D), full(docs * slots, D),
            *(shapes[name] for name in INPUTS[4:12]), full(8, D),
        ),
        in_specs=[pl.BlockSpec(memory_space=pltpu.HBM)] * 6,
        out_specs=(pl.BlockSpec(memory_space=pltpu.HBM),) * 13,
        scratch_shapes=[
            pltpu.VMEM((GRAD_ROWS, D), LOW),
            pltpu.VMEM((6, D, D), F32),
            pltpu.VMEM((docs * rows, D), LOW),
            pltpu.VMEM((docs * rows, D), F32),
            pltpu.VMEM((docs * slots, D), LOW),
            pltpu.VMEM((docs * slots, D), F32),
            pltpu.VMEM((docs * rows, D), LOW),
            pltpu.VMEM((docs * slots, D), LOW),
            pltpu.VMEM((8, D), F32),
            pltpu.SemaphoreType.DMA((GRAD_ROWS // D,)),
            pltpu.SemaphoreType.DMA((6 + 5,)),
            pltpu.SemaphoreType.DMA((5,)),
        ],
        compiler_params=pltpu.CompilerParams(vmem_limit_bytes=VMEM_BYTES),
    )(*parts)
    results = list(results)
    for k in (0, 2):
        results[k] = results[k].reshape(docs, rows, D)
    for k in (1, 3):
        results[k] = results[k].reshape(docs, slots, D)
    results[12] = results[12][:5]
    return tuple(results)


def solution(mesh):
    row, slot, whole = P("docs", "seq", None), P("docs", None, None), P()
    return jax.shard_map(
        on_device,
        mesh=mesh,
        in_specs=(row, slot, P("docs"), P("docs")) + (whole,) * 9 + (row, slot),
        out_specs=(row, slot, row, slot) + (whole,) * 9,
        check_vma=False,
    )
```
